128 devices in a mesh: ctx: 16 (over z_hi, x, core), wsh: 8 (over z_lo, y).
Axes of the slice: x: 4, y: 4, z: 4 (z_hi: 2, z_lo: 2; z = z_hi * 2 + z_lo), core: 2. Of those that a mesh axis runs over, the one named last changes fastest.
Arguments:
- tokens: bfloat16 [8, 2048, 1024], P('wsh', 'ctx'), may hold values from -6 to 6
- teacher: bfloat16 [8, 2048, 1024], P('wsh', 'ctx'), may hold values from -6 to 6
- doc_starts: int32 [8, 8], P('wsh'), may hold values from 0 to 2047, as said below
- valid_mask: int32 [8, 2048], P('wsh', 'ctx'), may hold values from 0 to 1
- qkv_weight: bfloat16 [1, 1024, 4096], P(None, ('ctx', 'wsh')), may hold values from -0.1875 to 0.1875
- out_weight: bfloat16 [1, 2048, 1024], P(None, ('ctx', 'wsh')), may hold values from -1 to 1
- gate_up_weight: bfloat16 [1, 1024, 6144], P(None, ('ctx', 'wsh')), may hold values from -0.1875 to 0.1875
- down_weight: bfloat16 [1, 3072, 1024], P(None, ('ctx', 'wsh')), may hold values from -0.109375 to 0.109375
- attn_gain: bfloat16 [1, 1024], P(None, ('ctx', 'wsh')), may hold values from 0.099609375 to 1.8984375
- ffn_gain: bfloat16 [1, 1024], P(None, ('ctx', 'wsh')), may hold values from 0.099609375 to 1.8984375
- qk_gain: bfloat16 [1, 256], P(None, ('ctx', 'wsh')), may hold values from 0.099609375 to 1.8984375
Outputs:
- mean_loss: float32 [], replicated
- block_out: bfloat16 [8, 2048, 1024], P('wsh', 'ctx')
- tokens_grad: float32 [8, 2048, 1024], P('wsh', 'ctx')
- qkv_grad: float32 [1, 1024, 4096], P(None, ('ctx', 'wsh'))
- out_grad: float32 [1, 2048, 1024], P(None, ('ctx', 'wsh'))
- gate_up_grad: float32 [1, 1024, 6144], P(None, ('ctx', 'wsh'))
- down_grad: float32 [1, 3072, 1024], P(None, ('ctx', 'wsh'))
- attn_gain_grad: float32 [1, 1024], P(None, ('ctx', 'wsh'))
- ffn_gain_grad: float32 [1, 1024], P(None, ('ctx', 'wsh'))
- qk_gain_grad: float32 [1, 256], P(None, ('ctx', 'wsh'))
The draws below stay inside these ranges and needn't reach their ends.
Inputs may be any that keep to these rules, and one draw needn't show every extreme that they name: `doc_starts`: each stream's 8 document starts increase strictly, the first is 0 and the last is 2047, and every start lies in the first 128 or the last 128 positions of the stream; one document runs from the first 128 positions into the last 128.
All inputs are finite; a program needn't handle non-finite values.
Results may differ from the reference program's by a relative error of at most 0.017.
Values may be sent and summed in bfloat16 or wider, within the bound.
No kernel may reach another device: no remote copies, remote signals or barrier semaphores. Data moves between devices by JAX's collectives and lax.ppermute only.
A program may use at most 192 MiB of HBM per device.

```python
import math
import jax
import jax.numpy as jnp
from jax import lax

D = 1024
HEADS = 16
KV_HEADS = 8
HD = 128
FF = 3072
LAYERS = 1
NDOC = 8
TOK_DEV = 128
QD = 2048
KVD = 1024
STREAMS = 8
SEQ = 2048
TOKENS = 16384


def draw_doc_starts(key, part):
    key = jax.random.fold_in(key, 11)

    def one_stream(stream_index):
        stream_key = jax.random.fold_in(key, stream_index)
        head_key, tail_key, split_key = jax.random.split(stream_key, 3)
        head_starts = jnp.sort(jax.random.permutation(head_key, TOK_DEV - 1)[:NDOC]) + 1
        tail_starts = jnp.sort(jax.random.permutation(tail_key, TOK_DEV - 2)[:NDOC]) + SEQ - TOK_DEV + 1
        split_at = jax.random.randint(split_key, (), 1, NDOC)
        slots = jnp.arange(NDOC)
        from_head = head_starts[jnp.clip(slots - 1, 0, NDOC - 1)]
        from_tail = tail_starts[jnp.clip(slots - split_at, 0, NDOC - 1)]
        chosen = jnp.where(slots < split_at, from_head, from_tail)
        chosen = jnp.where(slots == NDOC - 1, SEQ - 1, chosen)
        return jnp.where(slots == 0, 0, chosen).astype(jnp.int32)
    return jax.vmap(one_stream)(jnp.arange(STREAMS))


def draw_valid_mask(key, part):
    key = jax.random.fold_in(key, 23)
    positions = jnp.arange(SEQ, dtype=jnp.int32)
    draws = jax.random.randint(key, (STREAMS, SEQ), 0, 4 * SEQ)
    return (draws < SEQ + 2 * positions[None, :]).astype(jnp.int32)


def level_of(key, dims, cuts, low, top_value):
    level, own = 1.0, jax.random.fold_in(key, 6)
    for position, shards_of in cuts:
        heights = jnp.exp(jax.random.uniform(jax.random.fold_in(own, position), (shards_of,), jnp.float32, low / len(cuts), top_value / len(cuts)))
        level = level * jnp.repeat(heights, dims[position] // shards_of).reshape([-1 if axis == position else 1 for axis in range(len(dims))])
    return level


def bell_draw(key, extent, deviation, limit, cuts=(), kind=jnp.bfloat16):
    entries = jax.random.normal(key, extent, jnp.float32) * deviation
    if len(cuts) > 0:
        entries = level_of(key, extent, cuts, -0.22, 0.18) * entries
    return jnp.clip(entries, min=-limit, max=limit).astype(kind)


def setup_inputs(seed: int = 0) -> dict:
    key_list = jax.random.split(jax.random.key(seed), 12)
    return {
        "tokens": bell_draw(key_list[0], (STREAMS, SEQ, D), 1.0, 6.0, ((0, 8), (1, 16))),
        "teacher": bell_draw(key_list[1], (STREAMS, SEQ, D), 1.0, 6.0, ((0, 8), (1, 16))),
        "doc_starts": draw_doc_starts(jax.random.fold_in(key_list[11], 71), 0),
        "valid_mask": draw_valid_mask(jax.random.fold_in(key_list[11], 71), 0),
        "qkv_weight": bell_draw(key_list[4], (LAYERS, D, QD + 2 * KVD), D ** -0.5, 0.1875, ((1, 128),)),
        "out_weight": bell_draw(key_list[5], (LAYERS, QD, D), (QD // 64) ** -0.5, 1.0, ((1, 128),)),
        "gate_up_weight": bell_draw(key_list[6], (LAYERS, D, 2 * FF), D ** -0.5, 0.1875, ((1, 128),)),
        "down_weight": bell_draw(key_list[7], (LAYERS, FF, D), FF ** -0.5, 0.109375, ((1, 128),)),
        "attn_gain": jnp.clip(1.0 + 0.18 * jax.random.normal(key_list[8], (LAYERS, D), jnp.float32), 0.099609375, 1.8984375).astype(jnp.bfloat16),
        "ffn_gain": jnp.clip(1.0 + 0.18 * jax.random.normal(key_list[9], (LAYERS, D), jnp.float32), 0.099609375, 1.8984375).astype(jnp.bfloat16),
        "qk_gain": jnp.clip(1.0 + 0.18 * jax.random.normal(key_list[10], (LAYERS, 2 * HD), jnp.float32), 0.099609375, 1.8984375).astype(jnp.bfloat16),
    }


@jax.custom_vjp
def low(v):
    return lax.optimization_barrier(v.astype(jnp.bfloat16)).astype(jnp.float32)

@jax.custom_vjp
def low_back(v):
    return v

def low_keep(v):
    return (low(v), None)

def low_pass(kept, grad):
    return (grad,)

def back_keep(v):
    return (v, None)

def back_low(kept, grad):
    return (low(grad),)
low.defvjp(low_keep, low_pass)
low_back.defvjp(back_keep, back_low)
EPS = 1e-06
THETA = 1000000.0
HIGH = lax.Precision.HIGHEST

def matmul_hi(left, right):
    return jnp.dot(left, right, precision=HIGH, preferred_element_type=jnp.float32)

def rms_scale(values_in, gain_vec):
    return values_in * lax.rsqrt(lax.optimization_barrier(jnp.mean(values_in * values_in, axis=-1, keepdims=True)) + EPS) * gain_vec

def rope_tables(positions):
    half_dim = HD // 2
    frequency = jnp.exp(-(jnp.arange(half_dim, dtype=jnp.float32) * 2.0 / HD) * math.log(THETA))
    angles = positions.astype(jnp.float32)[:, None] * frequency[None, :]
    cosine_table = jnp.concatenate([jnp.cos(angles), jnp.cos(angles)], axis=-1)
    sine_table = jnp.concatenate([jnp.sin(angles), jnp.sin(angles)], axis=-1)
    return (cosine_table, sine_table)

def rotate(vectors):
    half_dim = vectors.shape[-1] // 2
    return jnp.concatenate([-vectors[..., half_dim:], vectors[..., :half_dim]], axis=-1)

def rotary(vectors, cosine_table, sine_table):
    return vectors * cosine_table[:, None, :] + rotate(vectors) * sine_table[:, None, :]

def doc_numbers(starts, positions):
    return lax.optimization_barrier(jnp.sum((starts[None, :] <= positions[:, None]).astype(jnp.int32), axis=1)) - 1

def attend(queries, keys_in, values_in, documents):
    block = math.gcd(SEQ, 512)
    groups = HEADS // KV_HEADS
    positions = jnp.arange(SEQ, dtype=jnp.int32)
    query_blocks = queries.reshape(SEQ // block, block, KV_HEADS, groups, HD)
    pos_blocks = positions.reshape(SEQ // block, block)
    doc_blocks = documents.reshape(SEQ // block, block)
    score_scale = 1.0 / math.sqrt(HD)

    @jax.checkpoint
    def one_block(block_items):
        query_part, query_pos, query_doc = block_items
        products = low_back(jnp.einsum('tkgd,skd->kgts', query_part, keys_in, precision=HIGH))
        scores = products * score_scale
        allowed = (positions[None, :] <= query_pos[:, None]) & (documents[None, :] == query_doc[:, None])
        scores = jnp.where(allowed[None, None], scores, -1e+30)
        row_max = lax.optimization_barrier(jnp.max(scores, axis=-1, keepdims=True))
        log_total = row_max + jnp.log(lax.optimization_barrier(jnp.sum(jnp.exp(scores - row_max), axis=-1, keepdims=True)))
        probability = low(jnp.exp(scores - log_total))
        return jnp.einsum('kgts,skd->tkgd', probability, values_in, precision=HIGH)
    outputs = lax.map(one_block, (query_blocks, pos_blocks, doc_blocks))
    return outputs.reshape(SEQ, HEADS * HD)

def layer_forward(hidden, weights, cosine_table, sine_table, documents):
    w_qkv, w_out, w_gate_up, w_down, gain_attn, gain_ffn, gain_qk = weights
    query_width = HEADS * HD
    kv_width = KV_HEADS * HD
    h_attn = low(rms_scale(hidden, gain_attn))
    qkv_all = low_back(matmul_hi(h_attn, w_qkv))
    query_raw = qkv_all[:, :query_width].reshape(SEQ, HEADS, HD)
    key_raw = qkv_all[:, query_width:query_width + kv_width].reshape(SEQ, KV_HEADS, HD)
    value_low = low(qkv_all[:, query_width + kv_width:].reshape(SEQ, KV_HEADS, HD))
    queries = low(rotary(rms_scale(query_raw, gain_qk[:HD]), cosine_table, sine_table))
    key_low = low(rotary(rms_scale(key_raw, gain_qk[HD:]), cosine_table, sine_table))
    attended = low(low_back(attend(queries, key_low, value_low, documents)))
    mid_state = hidden + low_back(matmul_hi(attended, w_out))
    h_ffn = low(rms_scale(mid_state, gain_ffn))
    gate_up = low_back(matmul_hi(h_ffn, w_gate_up))
    activated = low(jax.nn.silu(gate_up[:, :FF]) * gate_up[:, FF:])
    return mid_state + low_back(matmul_hi(activated, w_down))

def reference(tokens, teacher, doc_starts, valid_mask, qkv_weight, out_weight, gate_up_weight, down_weight, attn_gain, ffn_gain, qk_gain):
    params = tuple((weight.astype(jnp.float32) for weight in (qkv_weight, out_weight, gate_up_weight, down_weight, attn_gain, ffn_gain, qk_gain)))
    token_count = jnp.sum(valid_mask.astype(jnp.float32))
    loss_scale = float(TOKENS) * D / 2.0
    positions = jnp.arange(SEQ, dtype=jnp.int32)
    cosine_table, sine_table = rope_tables(positions)

    def stream(totals, stream_item):
        hidden_in, teach, starts, loss_mask = stream_item
        documents = doc_numbers(starts, positions)

        def run_loss(hidden, layer_params):
            state = hidden
            for layer_index in range(LAYERS):
                state = layer_forward(state, tuple((weight[layer_index] for weight in layer_params)), cosine_table, sine_table, documents)
            difference = state - teach
            squares = jnp.sum(loss_mask[:, None] * difference * difference)
            return (loss_scale * squares / (D * token_count), (state, squares))
        scaled_value, pullback, aux_out = jax.vjp(run_loss, hidden_in, params, has_aux=True)
        state, squares = aux_out
        hidden_grad, param_grads = pullback(jnp.ones_like(scaled_value))
        totals = (totals[0] + squares, jax.tree.map(jnp.add, totals[1], param_grads))
        return (totals, (state.astype(jnp.bfloat16), hidden_grad))
    zero_grads = jax.tree.map(jnp.zeros_like, params)
    (total_sq, grads), (block_out, tokens_grad) = lax.scan(stream, (jnp.zeros((), jnp.float32), zero_grads), (tokens.astype(jnp.float32), teacher.astype(jnp.float32), doc_starts, valid_mask.astype(jnp.float32)))
    mean_loss = total_sq / (D * token_count)
    return (mean_loss, block_out, tokens_grad, grads[0], grads[1], grads[2], grads[3], grads[4], grads[5], grads[6])
```

```python
import math

import jax
import jax.numpy as jnp
from jax import lax
from jax.experimental import pallas as pl
from jax.experimental.pallas import tpu as pltpu
from jax.sharding import Mesh
from jax.sharding import PartitionSpec as P

D = 1024
HEADS = 16
KV_HEADS = 8
HD = 128
FF = 3072
T = 128
G = 512
HALF = 1024
EPS = 1e-06
THETA = 1000000.0
SCALE = 1.0 / math.sqrt(HD)
SCALE2 = SCALE / math.log(2.0)
TOKENS = 16384.0

ALL = ("zh", "x", "c", "zl", "y")
ROWS = ("zh", "zl", "y")
CHIPS = ("zh", "x", "zl", "y")
BF = jnp.bfloat16
F32 = jnp.float32


def nt(a, b):
    return lax.dot_general(a, b, (((1,), (1,)), ((), ())), preferred_element_type=F32)


def nn(a, b):
    return lax.dot_general(a, b, (((1,), (0,)), ((), ())), preferred_element_type=F32)


def tn(a, b):
    return lax.dot_general(a, b, (((0,), (0,)), ((), ())), preferred_element_type=F32)


def sds(shape, dtype):
    return jax.ShapeDtypeStruct(shape, dtype)


def call(body, outs, args, scratch=(), smem=0, flops=0, limit=40):
    specs = [pl.BlockSpec(memory_space=pltpu.SMEM)] * smem
    specs += [pl.BlockSpec(memory_space=pltpu.VMEM)] * (len(args) - smem)
    size = sum(math.prod(a.shape) * a.dtype.itemsize for a in list(args) + list(outs))
    return pl.pallas_call(
        body,
        out_shape=list(outs),
        in_specs=specs,
        out_specs=[pl.BlockSpec(memory_space=pltpu.VMEM)] * len(outs),
        scratch_shapes=list(scratch),
        compiler_params=pltpu.CompilerParams(vmem_limit_bytes=limit * 1024 * 1024),
        cost_estimate=pl.CostEstimate(flops=flops, bytes_accessed=size, transcendentals=0),
    )(*args)


def shift_from(x_id, k):
    return lax.rem(x_id - k + 4, 4)


def rows_at(index, size):
    return pl.ds(pl.multiple_of(index * size, size), size)


def qkv_kernel(ids, t0, t1, t2, t3, gain, qk_gain, own, sib, cos, sin, h_ref, q_ref, kv_ref, qraw, kraw):
    x_id, c_id = ids[1], ids[2]
    for k, t_ref in enumerate((t0, t1, t2, t3)):
        t = t_ref[...].astype(F32)
        r = lax.rsqrt(jnp.mean(t * t, axis=-1, keepdims=True) + EPS)
        h_ref[rows_at(shift_from(x_id, k), T), :] = (t * r * gain[...]).astype(BF)
    first = c_id == 0

    def rope(v, gains, rows):
        r = lax.rsqrt(jnp.mean(v * v, axis=-1, keepdims=True) + EPS)
        n = v * r * gains
        return (n * cos[rows, :] + pltpu.roll(n, 64, 1) * sin[rows, :]).astype(BF)

    for j in range(4):
        rows = slice(j * T, (j + 1) * T)
        h = h_ref[rows, :]
        a = nn(h, own[:, :G])
        b = nn(h, sib[:, :G])
        q = jnp.where(first, a, b)
        kv = jnp.where(first, b, a)
        qraw[rows, :] = q
        kraw[rows, :] = kv[:, :256]
        kv_ref[rows, 256:] = kv[:, 256:].astype(BF)
        for n in range(4):
            q_ref[rows, n * HD : (n + 1) * HD] = rope(q[:, n * HD : (n + 1) * HD], qk_gain[:, :HD], rows)
        for n in range(2):
            kv_ref[rows, n * HD : (n + 1) * HD] = rope(kv[:, n * HD : (n + 1) * HD], qk_gain[:, HD:], rows)


def head_pair(ref, hh, j):
    rows = slice(j * T, (j + 1) * T)
    base = hh * 256
    return jnp.concatenate([ref[rows, base : base + HD], ref[rows, base + HD : base + 256]], axis=0)


def row_pair(row):
    return jnp.concatenate([row, row], axis=1)


def key_positions(base, start, count):
    index = lax.broadcasted_iota(jnp.int32, (count, 1), 0) + start
    return base + index + (index >> 7) * T


def query_positions(zh, c, j):
    row = lax.broadcasted_iota(jnp.int32, (1, T), 1) + (zh * HALF + j * 256 + c * T)
    return row_pair(row)


def fill_values(vt, slot, kv_ref):
    for hh in range(2):
        vt[slot, hh, :HD, :] = kv_ref[:, 256 + hh * HD : 256 + (hh + 1) * HD].T
        vt[slot, hh, HD:, :] = jnp.ones((16, G), BF)


def tiles(count):
    return [(t, min(256, count - t)) for t in range(0, count, 256)]


def attend(q_ref, kv_ref, vt, slot, hh, j, count, base, qpos, lo_row, causal):
    qj = head_pair(q_ref, hh, j)
    total = None
    for start, n in tiles(count):
        keys = kv_ref[start : start + n, hh * HD : (hh + 1) * HD]
        s = nt(keys, qj)
        kpos = key_positions(base, start, n)
        mask = kpos >= lo_row
        if causal:
            mask = mask & (kpos <= qpos)
        p = jnp.where(mask, jnp.exp2(s * SCALE2), 0.0).astype(BF)
        part = nn(vt[slot, hh, :, start : start + n], p)
        total = part if total is None else total + part
    return total


def near_kernel(ids, q_ref, own, sib, lo, acc, lsum, vt):
    zh, c = ids[0], ids[2]
    fill_values(vt, 0, own)
    fill_values(vt, 1, sib)
    for hh in range(2):
        for j in range(4):
            cols = slice(j * T, (j + 1) * T)
            lo_row = row_pair(lo[:, cols])
            qpos = query_positions(zh, c, j)
            total = None
            for slot, ref in enumerate((own, sib)):
                whose = c if slot == 0 else 1 - c
                part = attend(
                    q_ref, ref, vt, slot, hh, j, (j + 1) * T, zh * HALF + whose * T, qpos, lo_row, True
                )
                total = part if total is None else total + part
            for g in range(2):
                n = 2 * hh + g
                acc[n * HD : (n + 1) * HD, cols] = total[:HD, g * T : (g + 1) * T]
                lsum[n : n + 1, cols] = total[HD : HD + 1, g * T : (g + 1) * T]
    lsum[4:8, :] = jnp.ones((4, G), F32)


def far_kernel(ids, q_ref, own, sib, lo, acc, lsum, w_own, w_sib, att, att_t, lse, p0, p1, p2, p3, vt, sums, wide, w_nat):
    zh, x_id, c = ids[0], ids[1], ids[2]
    wide[...] = acc[...]
    sums[...] = lsum[...]

    @pl.when(zh == 1)
    def _():
        fill_values(vt, 0, own)
        fill_values(vt, 1, sib)
        for hh in range(2):
            for j in range(4):
                cols = slice(j * T, (j + 1) * T)
                lo_row = row_pair(lo[:, cols])
                total = None
                for slot, ref in enumerate((own, sib)):
                    whose = c if slot == 0 else 1 - c
                    part = attend(q_ref, ref, vt, slot, hh, j, G, whose * T, None, lo_row, False)
                    total = part if total is None else total + part
                for g in range(2):
                    n = 2 * hh + g
                    wide[n * HD : (n + 1) * HD, cols] += total[:HD, g * T : (g + 1) * T]
                    sums[n : n + 1, cols] += total[HD : HD + 1, g * T : (g + 1) * T]

    lse[...] = jnp.log2(sums[...])
    for n in range(4):
        inverse = 1.0 / sums[n : n + 1, :]
        scaled = wide[n * HD : (n + 1) * HD, :] * inverse
        att_t[n * HD : (n + 1) * HD, :] = scaled
        for j in range(4):
            att[j * T : (j + 1) * T, n * HD : (n + 1) * HD] = scaled[:, j * T : (j + 1) * T].T.astype(BF)
    for hh in range(2):
        w_nat[rows_at(2 * hh + c, HD), :] = w_own[hh]
        w_nat[rows_at(2 * hh + 1 - c, HD), :] = w_sib[hh]
    for k, out in enumerate((p0, p1, p2, p3)):
        rows = att[rows_at(shift_from(x_id, k), T), :]
        out[...] = nn(rows, w_nat[...]).astype(out.dtype)


def attend_back(q_ref, kv_ref, kt, slot, datt, hh, j, count, base, qpos, lo_row, lse_row, delta_row, dkv, causal):
    qj = head_pair(q_ref, hh, j)
    dj = head_pair(datt, hh, j)
    dq = None
    for start, n in tiles(count):
        rows = slice(start, start + n)
        kc = slice(hh * HD, (hh + 1) * HD)
        vc = slice(256 + hh * HD, 256 + (hh + 1) * HD)
        s = nt(kv_ref[rows, kc], qj)
        dp = nt(kv_ref[rows, vc], dj)
        kpos = key_positions(base, start, n)
        mask = kpos >= lo_row
        if causal:
            mask = mask & (kpos <= qpos)
        p = jnp.where(mask, jnp.exp2(s * SCALE2 - lse_row), 0.0)
        ds = (p * (dp - delta_row) * SCALE).astype(BF)
        dkv[rows, vc] += nn(p.astype(BF), dj)
        dkv[rows, kc] += nn(ds, qj)
        part = nn(kt[slot, hh, :, start : start + n], ds)
        dq = part if dq is None else dq + part
    return dq


def fill_keys(kt, slot, kv_ref):
    for hh in range(2):
        kt[slot, hh] = kv_ref[:, hh * HD : (hh + 1) * HD].T


def far_back_kernel(ids, b0, b1, b2, b3, w_own, w_sib, q_ref, own, sib, lo, lse, att_t,
                    dmb, datt, delta, dq, dkv_own, dkv_sib, kt, w_nat, sum_own, sum_sib):
    zh, x_id, c = ids[0], ids[1], ids[2]
    for hh in range(2):
        w_nat[rows_at(2 * hh + c, HD), :] = w_own[hh]
        w_nat[rows_at(2 * hh + 1 - c, HD), :] = w_sib[hh]
    for k, ref in enumerate((b0, b1, b2, b3)):
        dmb[rows_at(shift_from(x_id, k), T), :] = ref[...]
    datt[...] = nt(dmb[...], w_nat[...]).astype(BF)
    for n in range(4):
        cols = slice(n * HD, (n + 1) * HD)
        back = nt(w_nat[cols, :], dmb[...]).astype(BF).astype(F32)
        delta[n : n + 1, :] = jnp.sum(back * att_t[cols, :], axis=0, keepdims=True)
    delta[4:8, :] = jnp.zeros((4, G), F32)
    dq[...] = jnp.zeros_like(dq)
    sum_own[...] = jnp.zeros_like(sum_own)
    sum_sib[...] = jnp.zeros_like(sum_sib)

    @pl.when(zh == 1)
    def _():
        fill_keys(kt, 0, own)
        fill_keys(kt, 1, sib)
        for hh in range(2):
            for j in range(4):
                cols = slice(j * T, (j + 1) * T)
                lo_row = row_pair(lo[:, cols])
                lse_row = jnp.concatenate([lse[2 * hh : 2 * hh + 1, cols], lse[2 * hh + 1 : 2 * hh + 2, cols]], axis=1)
                delta_row = jnp.concatenate([delta[2 * hh : 2 * hh + 1, cols], delta[2 * hh + 1 : 2 * hh + 2, cols]], axis=1)
                total = None
                for slot, (ref, dref) in enumerate(((own, sum_own), (sib, sum_sib))):
                    whose = c if slot == 0 else 1 - c
                    part = attend_back(q_ref, ref, kt, slot, datt, hh, j, G, whose * T, None,
                                       lo_row, lse_row, delta_row, dref, False)
                    total = part if total is None else total + part
                for g in range(2):
                    n = 2 * hh + g
                    dq[cols, n * HD : (n + 1) * HD] = total[:, g * T : (g + 1) * T].T

    dkv_own[...] = sum_own[...].astype(BF)
    dkv_sib[...] = sum_sib[...].astype(BF)


def near_back_kernel(ids, q_ref, own, sib, lo, lse, datt, delta, dq_in, dq, dkv_own, dkv_sib, kt, sum_sib):
    zh, c = ids[0], ids[2]
    dkv_own[...] = jnp.zeros_like(dkv_own)
    sum_sib[...] = jnp.zeros_like(sum_sib)
    fill_keys(kt, 0, own)
    fill_keys(kt, 1, sib)
    for hh in range(2):
        for j in range(4):
            cols = slice(j * T, (j + 1) * T)
            lo_row = row_pair(lo[:, cols])
            qpos = query_positions(zh, c, j)
            lse_row = jnp.concatenate([lse[2 * hh : 2 * hh + 1, cols], lse[2 * hh + 1 : 2 * hh + 2, cols]], axis=1)
            delta_row = jnp.concatenate([delta[2 * hh : 2 * hh + 1, cols], delta[2 * hh + 1 : 2 * hh + 2, cols]], axis=1)
            total = None
            for slot, (ref, dref) in enumerate(((own, dkv_own), (sib, sum_sib))):
                whose = c if slot == 0 else 1 - c
                part = attend_back(q_ref, ref, kt, slot, datt, hh, j, (j + 1) * T, zh * HALF + whose * T, qpos,
                                   lo_row, lse_row, delta_row, dref, True)
                total = part if total is None else total + part
            for g in range(2):
                n = 2 * hh + g
                hc = slice(n * HD, (n + 1) * HD)
                dq[cols, hc] = dq_in[cols, hc] + total[:, g * T : (g + 1) * T].T
    dkv_sib[...] = sum_sib[...].astype(BF)


def qkv_back_kernel(ids, dq, dkv_own, from_sib, from_far, qraw, kraw, qk_gain, cos, sin, own, sib,
                    dqkv, gains, p0, p1, p2, p3, wq, wkv):
    x_id, c_id = ids[1], ids[2]
    first = c_id == 0

    def back(w, raw, gain, rows):
        w = w * cos[rows, :] - pltpu.roll(w, 64, 1) * sin[rows, :]
        r = lax.rsqrt(jnp.mean(raw * raw, axis=-1, keepdims=True) + EPS)
        a = w * gain
        out = r * a - raw * (r * r * r * jnp.mean(a * raw, axis=-1, keepdims=True))
        return out, jnp.sum(w * raw * r, axis=0, keepdims=True)

    sum_q = jnp.zeros((1, HD), F32)
    sum_k = jnp.zeros((1, HD), F32)
    for j in range(4):
        rows = slice(j * T, (j + 1) * T)
        dkv = dkv_own[rows, :] + from_sib[rows, :].astype(F32) + from_far[rows, :].astype(F32)
        for n in range(4):
            hc = slice(n * HD, (n + 1) * HD)
            out, part = back(dq[rows, hc], qraw[rows, hc], qk_gain[:, :HD], rows)
            sum_q += part
            dqkv[rows, hc] = out.astype(BF)
        for n in range(2):
            hc = slice(n * HD, (n + 1) * HD)
            out, part = back(dkv[:, hc], kraw[rows, hc], qk_gain[:, HD:], rows)
            sum_k += part
            dqkv[rows, G + n * HD : G + (n + 1) * HD] = out.astype(BF)
        dqkv[rows, G + 256 :] = dkv[:, 256:].astype(BF)
    gains[:, :HD] = sum_q
    gains[:, HD:] = sum_k
    wq[...] = jnp.where(first, own[:, :G], sib[:, :G])
    wkv[...] = jnp.where(first, sib[:, :G], own[:, :G])
    for k, out in enumerate((p0, p1, p2, p3)):
        rows = dqkv[rows_at(shift_from(x_id, k), T), :]
        out[...] = (nt(rows[:, :G], wq[...]) + nt(rows[:, G:], wkv[...])).astype(out.dtype)


def split_rows(c_id, value, keep, send, index):
    half = value.shape[0] // 2
    first = c_id == 0
    keep[index] = jnp.where(first, value[:half], value[half:])
    send[index] = jnp.where(first, value[half:], value[:half]).astype(BF)


def qkv_grad_kernel(ids, h, dqkv, keep, send):
    for b in range(8):
        split_rows(ids[2], tn(h[:, b * 128 : (b + 1) * 128], dqkv[...]), keep, send, b)


def out_grad_kernel(ids, att, dmb, keep, send):
    for b in range(2):
        split_rows(ids[2], tn(att[:, b * 256 : (b + 1) * 256], dmb[...]), keep, send, b)


def stack4(a, b, c, d):
    return jnp.concatenate([a[...], b[...], c[...], d[...]], axis=0)


def ffn_kernel(ids, h0, h1, h2, h3, own, sib, d_own, d_sib, gate, up, act, p0, p1, p2, p3, h, down):
    c_id = ids[2]
    first = c_id == 0
    h[...] = stack4(h0, h1, h2, h3)
    for zz in range(2):
        down[pl.ds(pl.multiple_of(zz * 384 + c_id * 192, 192), 192), :] = d_own[zz]
        down[pl.ds(pl.multiple_of(zz * 384 + (1 - c_id) * 192, 192), 192), :] = d_sib[zz]
    for t in range(3):
        cols = slice(t * 256, (t + 1) * 256)
        a = nn(h[...], own[:, cols])
        b = nn(h[...], sib[:, cols])
        g = jnp.where(first, a, b)
        u = jnp.where(first, b, a)
        gate[:, cols] = g
        up[:, cols] = u
        act[:, cols] = (g * jax.nn.sigmoid(g) * u).astype(BF)
    for k, out in enumerate((p0, p1, p2, p3)):
        out[...] = nn(act[k * T : (k + 1) * T, :], down[...]).astype(out.dtype)


def ffn_back_kernel(ids, g0, g1, g2, g3, gate, up, own, sib, d_own, d_sib, dg, du, p0, p1, p2, p3, gb, down):
    c_id = ids[2]
    first = c_id == 0
    gb[...] = stack4(g0, g1, g2, g3)
    for zz in range(2):
        down[pl.ds(pl.multiple_of(zz * 384 + c_id * 192, 192), 192), :] = d_own[zz]
        down[pl.ds(pl.multiple_of(zz * 384 + (1 - c_id) * 192, 192), 192), :] = d_sib[zz]
    for t in range(3):
        cols = slice(t * 256, (t + 1) * 256)
        dact = nt(gb[...], down[cols, :])
        g = gate[:, cols]
        u = up[:, cols]
        s = jax.nn.sigmoid(g)
        dg[:, cols] = (dact * u * s * (1.0 + g * (1.0 - s))).astype(BF)
        du[:, cols] = (dact * g * s).astype(BF)
    for k, out in enumerate((p0, p1, p2, p3)):
        rows = slice(k * T, (k + 1) * T)
        a = jnp.where(first, dg[rows, :], du[rows, :])
        b = jnp.where(first, du[rows, :], dg[rows, :])
        out[...] = (nt(a, own[...]) + nt(b, sib[...])).astype(out.dtype)


def ffn_grad_kernel(ids, h0, h1, h2, h3, g0, g1, g2, g3, act, dg, du, d_keep, d_send, u_keep, u_send, h, gb):
    c_id = ids[2]
    h[...] = stack4(h0, h1, h2, h3)
    gb[...] = stack4(g0, g1, g2, g3)
    for b in range(2):
        split_rows(c_id, tn(act[:, b * 384 : (b + 1) * 384], gb[...]), d_keep, d_send, b)
    for b in range(8):
        hb = h[:, b * 128 : (b + 1) * 128]
        value = jnp.concatenate([tn(hb, dg[...]), tn(hb, du[...])], axis=1)
        split_rows(c_id, value, u_keep, u_send, b)


def total_of(own, r1, r2, r3):
    return own[...] + r1[...].astype(F32) + r2[...].astype(F32) + r3[...].astype(F32)


def mid_kernel(tok, own, r1, r2, r3, gain, mid, h):
    v = tok[...].astype(F32) + total_of(own, r1, r2, r3)
    mid[...] = v
    r = lax.rsqrt(jnp.mean(v * v, axis=-1, keepdims=True) + EPS)
    h[...] = (v * r * gain[...]).astype(BF)


def loss_kernel(factor, mid, own, r1, r2, r3, teacher, mask, block, grad, grad_low, squares):
    v = mid[...] + total_of(own, r1, r2, r3)
    block[...] = v.astype(BF)
    diff = v - teacher[...].astype(F32)
    kept = mask[...] * diff
    out = factor[0] * kept
    grad[...] = out
    grad_low[...] = out.astype(BF)
    squares[...] = jnp.sum((kept * diff).reshape(16, 8, D), axis=0)


def norm_back(v, gain, w):
    r = lax.rsqrt(jnp.mean(v * v, axis=-1, keepdims=True) + EPS)
    a = w * gain
    return r * a - v * (r * r * r * jnp.mean(a * v, axis=-1, keepdims=True))


def dmid_kernel(grad, own, r1, r2, r3, mid, gain, dmid, dmb):
    out = grad[...] + norm_back(mid[...], gain[...], total_of(own, r1, r2, r3))
    dmid[...] = out
    dmb[...] = out.astype(BF)


def last_kernel(dmid, own, r1, r2, r3, tok, gain, out):
    out[...] = dmid[...] + norm_back(tok[...].astype(F32), gain[...], total_of(own, r1, r2, r3))


def around(v, k):
    return lax.ppermute(v, "x", [(i, (i + k) % 4) for i in range(4)])


def spread(v):
    return (v,) + tuple(around(v, k) for k in (1, 2, 3))


def collect(parts):
    return (parts[0],) + tuple(around(parts[k], -k) for k in (1, 2, 3))


def swap(v):
    return lax.ppermute(v, "c", [(0, 1), (1, 0)])


def tokens_shape(dtype):
    return sds((T, D), dtype)


def partials():
    return [tokens_shape(F32)] + [tokens_shape(BF)] * 3


def local(tokens, teacher, doc_starts, valid_mask, qkv_weight, out_weight, gate_up_weight, down_weight,
          attn_gain, ffn_gain, qk_gain):
    zh, x_id, c_id = lax.axis_index("zh"), lax.axis_index("x"), lax.axis_index("c")
    ids = jnp.stack([zh, x_id, c_id]).astype(jnp.int32)
    tok = tokens[0]
    mask = valid_mask[0].astype(F32)

    w = qkv_weight[0]
    wq = w[:, : HEADS * HD].reshape(8, 2, 4, 256).transpose(2, 0, 1, 3).reshape(4, 8, G)
    wk = w[:, 2048:3072].reshape(8, 2, 4, HD).transpose(2, 0, 1, 3).reshape(4, 8, 256)
    wv = w[:, 3072:].reshape(8, 2, 4, HD).transpose(2, 0, 1, 3).reshape(4, 8, 256)
    pair = jnp.stack([wq, jnp.concatenate([wk, wv], axis=2)], axis=1)
    extra = jnp.zeros((8, HD), BF)
    extra = extra.at[:, 0].set(attn_gain[0]).at[:, 1].set(ffn_gain[0])
    extra = extra.at[:2, 2].set(qk_gain[0]).at[0, 3].set(jnp.sum(mask).astype(BF))
    pair = jnp.concatenate([pair, jnp.broadcast_to(extra, (4, 2, 8, HD))], axis=3)
    sent = jnp.broadcast_to(pair[None, :, :, None], (2, 4, 2, 8, 8, 640)).reshape(128, 8, 640)
    got = lax.all_to_all(sent, ALL, split_axis=0, concat_axis=0, tiled=True)
    w_own = got.reshape(D, 640)
    w_sib = swap(w_own)
    gain_a = got[:, :, 512].astype(F32).reshape(1, D)
    gain_f = got[:, :, 513].astype(F32).reshape(1, D)
    gain_qk = got[:, :2, 514].astype(F32).reshape(1, 256)
    count = jnp.sum(got[:, 0, 515].astype(F32))
    toks = spread(tok)

    both = jnp.concatenate([out_weight[0], down_weight[0]], axis=0)
    both = lax.all_gather(both, ROWS, axis=0, tiled=False)
    both_sib = swap(both)
    o_own, o_sib = (b[:, :16].reshape(2, 128, D) for b in (both, both_sib))
    d_own, d_sib = (b[:, 16:].reshape(2, 192, D) for b in (both, both_sib))

    gu = gate_up_weight[0].reshape(8, 2, 2, 4, 384).transpose(3, 1, 0, 2, 4).reshape(4, 2, 8, 768)
    gu = jnp.broadcast_to(gu[None, :, :, None], (2, 4, 2, 8, 8, 768)).reshape(128, 8, 768)
    g_own = lax.all_to_all(gu, ALL, split_axis=0, concat_axis=0, tiled=True).reshape(D, 768)
    g_sib = swap(g_own)

    offset = jnp.arange(G, dtype=jnp.int32)
    positions = zh * HALF + c_id * T + offset + (offset // T) * T
    starts = doc_starts[0]
    lo = jnp.max(jnp.where(starts[None, :] <= positions[:, None], starts[None, :], 0), axis=1).reshape(1, G)
    half = HD // 2
    frequency = jnp.exp(-(jnp.arange(half, dtype=F32) * 2.0 / HD) * math.log(THETA))
    angles = positions.astype(F32)[:, None] * frequency[None, :]
    cos, sin = jnp.cos(angles), jnp.sin(angles)
    cos = jnp.concatenate([cos, cos], axis=1)
    sin = jnp.concatenate([-sin, sin], axis=1)

    wide = sds((G, G), BF)
    h_attn, q, kv, qraw, kraw = call(
        qkv_kernel,
        [sds((G, D), BF), wide, wide, sds((G, G), F32), sds((G, 256), F32)],
        [ids, *toks, gain_a, gain_qk, w_own, w_sib, cos, sin],
        smem=1, flops=2 * G * D * D,
    )
    kv_sib = swap(kv)
    far_own = lax.ppermute(kv, "zh", [(0, 1)])
    far_sib = swap(far_own)
    acc, lsum = call(
        near_kernel,
        [sds((G, G), F32), sds((8, G), F32)],
        [ids, q, kv, kv_sib, lo],
        scratch=[pltpu.VMEM((2, 2, 144, G), BF)], smem=1, flops=2 * 2 * G * G * 640,
    )
    att, att_t, lse, *parts = call(
        far_kernel,
        [wide, sds((G, G), F32), sds((8, G), F32)] + partials(),
        [ids, q, far_own, far_sib, lo, acc, lsum, o_own, o_sib],
        scratch=[pltpu.VMEM((2, 2, 144, G), BF), pltpu.VMEM((8, G), F32), pltpu.VMEM((G, G), F32),
                 pltpu.VMEM((G, D), BF)],
        smem=1, flops=2 * 2 * G * G * 1024 + 2 * G * G * D,
    )
    parts = collect(parts)
    mid, h = call(mid_kernel, [tokens_shape(F32), tokens_shape(BF)], [tok, *parts, gain_f])

    hs = spread(h)
    gate, up, act, *parts = call(
        ffn_kernel,
        [sds((G, 768), F32), sds((G, 768), F32), sds((G, 768), BF)] + partials(),
        [ids, *hs, g_own, g_sib, d_own, d_sib],
        scratch=[pltpu.VMEM((G, D), BF), pltpu.VMEM((768, D), BF)], smem=1, flops=6 * G * D * 768,
    )
    parts = collect(parts)
    factor = (TOKENS / count).reshape(1)
    block, grad, grad_low, squares = call(
        loss_kernel,
        [tokens_shape(BF), tokens_shape(F32), tokens_shape(BF), sds((8, D), F32)],
        [factor, mid, *parts, teacher[0], mask.reshape(T, 1)], smem=1,
    )

    gs = spread(grad_low)
    dg, du, *parts = call(
        ffn_back_kernel,
        [sds((G, 768), BF), sds((G, 768), BF)] + partials(),
        [ids, *gs, gate, up, g_own, g_sib, d_own, d_sib],
        scratch=[pltpu.VMEM((G, D), BF), pltpu.VMEM((768, D), BF)], smem=1, flops=6 * G * D * 768,
    )
    parts = collect(parts)
    d_keep, d_send, u_keep, u_send = call(
        ffn_grad_kernel,
        [sds((2, 192, D), F32), sds((2, 192, D), BF), sds((8, 64, 1536), F32), sds((8, 64, 1536), BF)],
        [ids, *hs, *gs, act, dg, du],
        scratch=[pltpu.VMEM((G, D), BF), pltpu.VMEM((G, D), BF)], smem=1, flops=6 * G * D * 768,
    )
    dmid, dmb = call(dmid_kernel, [tokens_shape(F32), tokens_shape(BF)], [grad, *parts, mid, gain_f])

    def reduce_rows(keep, send, rows):
        summed = (keep + swap(send).astype(F32)).astype(BF).reshape(16, rows, D)
        summed = lax.all_to_all(summed, ROWS, split_axis=0, concat_axis=0, tiled=True)
        return jnp.sum(summed.astype(F32), axis=0)

    def reduce_columns(keep, send, cols):
        summed = (keep + swap(send).astype(F32)).astype(BF).reshape(64, 8, cols)
        summed = lax.all_to_all(summed, CHIPS, split_axis=0, concat_axis=0, tiled=True)
        return jnp.sum(summed.astype(F32).reshape(2, 4, 8, 8, cols), axis=(0, 2))

    down_grad = reduce_rows(d_keep, d_send, 24)
    gate_up_grad = reduce_columns(u_keep, u_send, 1536)
    gate_up_grad = gate_up_grad.reshape(4, 8, 2, 2, 384).transpose(1, 2, 3, 0, 4).reshape(8, 2 * FF)

    bs = spread(dmb)
    small = sds((8, G), F32)
    dmb_all, datt, delta, dq, dkv_fo, dkv_fs = call(
        far_back_kernel,
        [sds((G, D), BF), wide, small, sds((G, G), F32), wide, wide],
        [ids, *bs, o_own, o_sib, q, far_own, far_sib, lo, lse, att_t],
        scratch=[pltpu.VMEM((2, 2, HD, G), BF), pltpu.VMEM((G, D), BF), pltpu.VMEM((G, G), F32), pltpu.VMEM((G, G), F32)],
        smem=1, flops=5 * 2 * G * G * 1024,
    )
    far = (dkv_fo.astype(F32) + swap(dkv_fs).astype(F32)).astype(BF)
    from_far = lax.ppermute(far, "zh", [(1, 0)])
    dq, dkv_own, dkv_sib = call(
        near_back_kernel,
        [sds((G, G), F32), sds((G, G), F32), wide],
        [ids, q, kv, kv_sib, lo, lse, datt, delta, dq],
        scratch=[pltpu.VMEM((2, 2, HD, G), BF), pltpu.VMEM((G, G), F32)],
        smem=1, flops=5 * 2 * G * G * 640,
    )
    o_keep, o_send = call(
        out_grad_kernel, [sds((2, 128, D), F32), sds((2, 128, D), BF)], [ids, att, dmb_all],
        smem=1, flops=2 * G * G * D,
    )
    out_grad = reduce_rows(o_keep, o_send, 16)
    dqkv, gain_sums, *parts = call(
        qkv_back_kernel,
        [sds((G, D), BF), sds((1, 256), F32)] + partials(),
        [ids, dq, dkv_own, swap(dkv_sib), from_far, qraw, kraw, gain_qk, cos, sin, w_own, w_sib],
        scratch=[pltpu.VMEM((D, G), BF), pltpu.VMEM((D, G), BF)], smem=1, flops=2 * G * D * D,
    )
    parts = collect(parts)
    q_keep, q_send = call(
        qkv_grad_kernel, [sds((8, 64, D), F32), sds((8, 64, D), BF)], [ids, h_attn, dqkv],
        smem=1, flops=2 * G * D * D,
    )
    tokens_grad, = call(last_kernel, [tokens_shape(F32)], [dmid, *parts, tok, gain_a])
    grads = reduce_columns(q_keep, q_send, D)
    grad_q = grads[:, :, :G].reshape(4, 8, 2, 256).transpose(1, 2, 0, 3).reshape(8, 2048)
    grad_k = grads[:, :, G : G + 256].reshape(4, 8, 2, HD).transpose(1, 2, 0, 3).reshape(8, 1024)
    grad_v = grads[:, :, G + 256 :].reshape(4, 8, 2, HD).transpose(1, 2, 0, 3).reshape(8, 1024)
    qkv_grad = jnp.concatenate([grad_q, grad_k, grad_v], axis=1)

    note = jnp.concatenate(
        [gain_sums.reshape(128, 2), jnp.full((128, 1), jnp.sum(squares)), jnp.zeros((128, 125), F32)], axis=1
    ).reshape(128, 1, 128)
    note = lax.all_to_all(note, ALL, split_axis=0, concat_axis=0, tiled=True)
    note = jnp.sum(note.reshape(128, 128), axis=0)
    mean_loss = note[2] / (D * count)

    def gain_grad(weight, grad_w, gain):
        return jnp.sum(weight.astype(F32) * grad_w, axis=1) / gain.astype(F32)

    return (
        mean_loss,
        block[None],
        tokens_grad[None],
        qkv_grad[None],
        out_grad[None],
        gate_up_grad[None],
        down_grad[None],
        gain_grad(w, qkv_grad, attn_gain[0])[None],
        gain_grad(gate_up_weight[0], gate_up_grad, ffn_gain[0])[None],
        note[:2][None],
    )


def solution(mesh):
    fine = Mesh(mesh.devices.reshape(2, 4, 2, 2, 4), ALL)
    ctx, wsh = ("zh", "x", "c"), ("zl", "y")
    states = P(wsh, ctx, None)
    matrix, vector = P(None, ALL, None), P(None, ALL)
    return jax.shard_map(
        local,
        mesh=fine,
        in_specs=(states, states, P(wsh, None), P(wsh, ctx)) + (matrix,) * 4 + (vector,) * 3,
        out_specs=(P(), states, states) + (matrix,) * 4 + (vector,) * 3,
        check_vma=False,
    )
```

```python
import math

import jax
import jax.numpy as jnp
from jax import lax
from jax.experimental import pallas as pl
from jax.experimental.pallas import tpu as pltpu
from jax.sharding import Mesh
from jax.sharding import PartitionSpec as P

D = 1024
HEADS = 16
KV_HEADS = 8
HD = 128
FF = 3072
T = 128
G = 512
HALF = 1024
EPS = 1e-06
THETA = 1000000.0
SCALE = 1.0 / math.sqrt(HD)
SCALE2 = SCALE / math.log(2.0)
TOKENS = 16384.0
MICROSECOND = 3 * 10**8

ALL = ("zh", "x", "c", "zl", "y")
ROWS = ("zh", "zl", "y")
CHIPS = ("zh", "x", "zl", "y")
BF = jnp.bfloat16
F32 = jnp.float32


def nt(a, b):
    return lax.dot_general(a, b, (((1,), (1,)), ((), ())), preferred_element_type=F32)


def nn(a, b):
    return lax.dot_general(a, b, (((1,), (0,)), ((), ())), preferred_element_type=F32)


def tn(a, b):
    return lax.dot_general(a, b, (((0,), (0,)), ((), ())), preferred_element_type=F32)


def sds(shape, dtype):
    return jax.ShapeDtypeStruct(shape, dtype)


class Moves:
    def __init__(self):
        self.copies, self.started, self.ended = {}, set(), set()

    def start(self, *refs):
        for ref in refs:
            if id(ref) not in self.started:
                self.started.add(id(ref))
                self.copies[id(ref)].start()

    def wait(self, *refs):
        for ref in refs:
            if id(ref) in self.copies and id(ref) not in self.ended:
                self.ended.add(id(ref))
                self.copies[id(ref)].wait()


def kept(shape, dtype):
    return pltpu.HBM(shape, dtype)


def in_hbm(value):
    return pltpu.with_memory_space_constraint(value, pltpu.HBM)


def call(body, outs, args, scratch=(), smem=0, limit=28, after=(), far=(), lazy=False, us=1):
    kept_out = [i for i, o in enumerate(outs) if not isinstance(o, jax.ShapeDtypeStruct)]
    vmem, hbm = pl.BlockSpec(memory_space=pltpu.VMEM), pl.BlockSpec(memory_space=pltpu.HBM)
    specs = [pl.BlockSpec(memory_space=pltpu.SMEM)] * smem
    specs += [hbm if i in far else vmem for i in range(smem, len(args))]
    specs += [pl.BlockSpec(memory_space=pl.ANY)] * len(after)
    count = len(args)
    staged = [(args[i].shape, args[i].dtype) for i in far]
    staged += [(outs[i].inner_aval.shape, outs[i].inner_aval.dtype) for i in kept_out]
    scratch = list(scratch) + [pltpu.VMEM(*a) for a in staged]
    if staged:
        scratch.append(pltpu.SemaphoreType.DMA((len(staged),)))

    def kernel(*refs):
        ins = list(refs[:count])
        results = list(refs[count + len(after) :][: len(outs)])
        rest = list(refs[count + len(after) + len(outs) :])
        if not staged:
            body(*ins, *results, *rest)
            return
        sems = rest.pop()
        stage = rest[len(rest) - len(staged) :]
        rest = rest[: len(rest) - len(staged)]
        moves = Moves()
        for n, i in enumerate(far):
            moves.copies[id(stage[n])] = pltpu.make_async_copy(ins[i], stage[n], sems.at[n])
            ins[i] = stage[n]
        for n, i in enumerate(kept_out, len(far)):
            moves.copies[id(stage[n])] = pltpu.make_async_copy(stage[n], results[i], sems.at[n])
            results[i] = stage[n]
        moves.start(*stage[: len(far)])
        if lazy:
            body(moves, *ins, *results, *rest)
        else:
            moves.wait(*stage[: len(far)])
            body(*ins, *results, *rest)
        moves.start(*stage)
        moves.wait(*stage)

    return pl.pallas_call(
        kernel,
        name=body.__name__,
        out_shape=list(outs),
        in_specs=specs,
        out_specs=[hbm if i in kept_out else vmem for i in range(len(outs))],
        scratch_shapes=scratch,
        compiler_params=pltpu.CompilerParams(vmem_limit_bytes=limit * 1024 * 1024),
        cost_estimate=pl.CostEstimate(flops=MICROSECOND * us, bytes_accessed=1, transcendentals=0),
    )(*[in_hbm(a) if i in far else a for i, a in enumerate(args)], *after)


def behind(value, *after):
    def nothing(*refs):
        del refs

    place = pl.BlockSpec(memory_space=pl.ANY)
    return pl.pallas_call(
        nothing,
        out_shape=sds(value.shape, value.dtype),
        in_specs=[place] * (1 + len(after)),
        out_specs=place,
        input_output_aliases={0: 0},
        cost_estimate=pl.CostEstimate(flops=1, bytes_accessed=1, transcendentals=0),
    )(value, *after)


def shift_from(x_id, k):
    return lax.rem(x_id - k + 4, 4)


def project(rows, weight, product, outs):
    for t in range(4):
        cols = slice(t * 256, (t + 1) * 256)
        value = product(rows, weight(cols))
        for k, out in enumerate(outs):
            out[:, cols] = value[k * T : (k + 1) * T].astype(out.dtype)


def rows_at(index, size):
    return pl.ds(pl.multiple_of(index * size, size), size)


def pack_kernel(ids, w, gu, out_w, down_w, gain_a, gain_f, gain_qk, mask, rows, own, s1, s2, s3, notes):
    for g in range(2):
        rows[g] = out_w[8 * g : 8 * g + 8, :]
    for g in range(3):
        rows[2 + g] = down_w[8 * g : 8 * g + 8, :]
    notes[...] = jnp.zeros_like(notes)
    notes[0:1, :8] = gain_a[...].astype(F32)
    notes[1:2, :8] = gain_f[...].astype(F32)
    notes[2:3, :2] = gain_qk[...].astype(F32)
    notes[3:4, :1] = jnp.sum(mask[...].astype(F32), axis=1, keepdims=True)
    note = notes[...].T[:8].astype(BF)
    for k, out in enumerate((own, s1, s2, s3)):
        x = lax.rem(ids[1] + k, 4)
        places = [(w, 0, 256), (w, HALF, 256)]
        places += [(w, base, HD) for base in (2048, 2560, 3072, 3584)]
        places += [(None, 0, 0)] + [(gu, base, 384) for base in (0, 1536, 3072, 4608)]
        at = 0
        for ref, base, n in places:
            if ref is None:
                out[:, at : at + HD] = note
                at += HD
            else:
                out[:, at : at + n] = ref[:, pl.ds(pl.multiple_of(base + x * n, HD), n)]
                at += n


def join_kernel(p0, p1, p2, p3, first, second):
    for k, ref in enumerate((p0, p1, p2, p3)):
        block, other = ref[:, :1152], ref[:, 1152:]
        for device in range(16):
            first[device, k] = block
            second[device, k] = other


def gather_kernel(ids, t0, t1, t2, t3, toks, scale):
    for k, ref in enumerate((t0, t1, t2, t3)):
        rows = rows_at(shift_from(ids[1], k), T)
        toks[rows, :] = ref[...]
        t = ref[...].astype(F32)
        r = lax.rsqrt(jnp.mean(t * t, axis=-1, keepdims=True) + EPS)
        scale[rows, :] = jnp.broadcast_to(r, (T, HD))


def blocks_of(got, zz, k):
    return jnp.concatenate([got[zz * 8 + other, k].astype(F32) for other in range(8)], axis=0).astype(BF)


def qkv_kernel(moves, ids, toks, scale, own, sib, cos, sin,
               h_ref, q_ref, kv_ref, cross, qraw, kraw, gain, gain_f, qk_gain, factor, weight, wide):
    c_id = ids[2]
    for zz in range(2):
        for k in range(4):
            at = 2 * (4 * zz + shift_from(ids[1], k))
            for whose, ref in ((c_id, own), (1 - c_id, sib)):
                value = blocks_of(ref, zz, k)
                weight[rows_at(at + whose, 64), :] = value[:, :D]
                wide[rows_at(at + whose, 64), :] = value[:, D:]
    moves.start(weight)
    notes = wide[...].T
    gain[...] = notes[0:1].astype(F32)
    gain_f[...] = notes[1:2].astype(F32)
    at = lax.broadcasted_iota(jnp.int32, (D, 256), 0)
    entry = lax.broadcasted_iota(jnp.int32, (D, 256), 1)
    pick = jnp.where(at == 8 * (entry >> 1) + (entry & 1), 1.0, 0.0).astype(BF)
    qk_gain[...] = nn(notes[:16], pick)[2:3]
    count = jnp.sum(notes[3:4].astype(F32), axis=1, keepdims=True)
    factor[...] = jnp.broadcast_to(TOKENS / count, (1, HD))

    def rope(v, gains, rows):
        r = lax.rsqrt(jnp.mean(v * v, axis=-1, keepdims=True) + EPS)
        n = v * r * gains
        return (n * cos[rows, :] + pltpu.roll(n, 64, 1) * sin[rows, :]).astype(BF)

    for j in range(4):
        rows = slice(j * T, (j + 1) * T)
        t = toks[rows, :].astype(F32)
        h = (t * scale[rows, :1] * gain[...]).astype(BF)
        h_ref[rows, :] = h
        q = nn(h, weight[:, :G])
        kv = nn(h, weight[:, G:])
        qraw[rows, :] = q
        kraw[rows, :] = kv[:, :256]
        kv_ref[rows, 256:] = kv[:, 256:].astype(BF)
        for n in range(4):
            q_ref[rows, n * HD : (n + 1) * HD] = rope(q[:, n * HD : (n + 1) * HD], qk_gain[:, :HD], rows)
        for n in range(2):
            kv_ref[rows, n * HD : (n + 1) * HD] = rope(kv[:, n * HD : (n + 1) * HD], qk_gain[:, HD:], rows)
    cross[...] = jnp.where(ids[0] == 0, kv_ref[...], q_ref[...])


def head_pair(ref, hh, j):
    rows = slice(j * T, (j + 1) * T)
    base = hh * 256
    return jnp.concatenate([ref[rows, base : base + HD], ref[rows, base + HD : base + 256]], axis=0)


def row_pair(row):
    return jnp.concatenate([row, row], axis=1)


def key_positions(base, start, count):
    index = lax.broadcasted_iota(jnp.int32, (count, 1), 0) + start
    return base + index + (index >> 7) * T


def query_positions(zh, c, j):
    row = lax.broadcasted_iota(jnp.int32, (1, T), 1) + (zh * HALF + j * 256 + c * T)
    return row_pair(row)


def fill_values(vt, slot, kv_ref):
    for hh in range(2):
        vt[slot, hh, :HD, :] = kv_ref[:, 256 + hh * HD : 256 + (hh + 1) * HD].T
        vt[slot, hh, HD:, :] = jnp.ones((16, G), BF)


def tiles(count):
    return [(t, min(256, count - t)) for t in range(0, count, 256)]


def join_out(c, own, sib, weight):
    for hh in range(2):
        for whose, ref in ((c, own), (1 - c, sib)):
            parts = [ref[hh * 8 + o, g].astype(F32) for o in range(8) for g in range(2)]
            weight[rows_at(2 * hh + whose, HD), :] = jnp.concatenate(parts, axis=0).astype(BF)


def attend(q_ref, kv_ref, vt, slot, hh, j, count, base, qpos, lo_row, causal):
    qj = head_pair(q_ref, hh, j)
    total = None
    for start, n in tiles(count):
        keys = kv_ref[start : start + n, hh * HD : (hh + 1) * HD]
        s = nt(keys, qj)
        kpos = key_positions(base, start, n)
        mask = kpos >= lo_row
        if causal:
            mask = mask & (kpos <= qpos)
        p = jnp.where(mask, jnp.exp2(s * SCALE2), 0.0).astype(BF)
        part = nn(vt[slot, hh, :, start : start + n], p)
        total = part if total is None else total + part
    return total


def near_kernel(ids, q_ref, own, sib, lo, acc, lsum, vt):
    zh, c = ids[0], ids[2]
    fill_values(vt, 0, own)
    fill_values(vt, 1, sib)
    for hh in range(2):
        for j in range(4):
            cols = slice(j * T, (j + 1) * T)
            lo_row = row_pair(lo[:, cols])
            qpos = query_positions(zh, c, j)
            total = None
            for slot, ref in enumerate((own, sib)):
                whose = c if slot == 0 else 1 - c
                part = attend(
                    q_ref, ref, vt, slot, hh, j, (j + 1) * T, zh * HALF + whose * T, qpos, lo_row, True
                )
                total = part if total is None else total + part
            for g in range(2):
                n = 2 * hh + g
                acc[n * HD : (n + 1) * HD, cols] = total[:HD, g * T : (g + 1) * T]
                lsum[n : n + 1, cols] = total[HD : HD + 1, g * T : (g + 1) * T]
    lsum[4:8, :] = jnp.ones((4, G), F32)


def far_kernel(moves, ids, q_ref, own, sib, lo, acc, lsum, rows_own, rows_sib, att, att_t, lse, w_nat, p0, p1, p2, p3, vt, sums, wide, turned):
    zh, x_id, c = ids[0], ids[1], ids[2]
    join_out(c, rows_own, rows_sib, w_nat)
    moves.start(w_nat)
    moves.wait(q_ref, own, sib)
    wide[...] = acc[...]
    sums[...] = lsum[...]

    @pl.when(zh == 1)
    def _():
        fill_values(vt, 0, own)
        fill_values(vt, 1, sib)
        for hh in range(2):
            for j in range(4):
                cols = slice(j * T, (j + 1) * T)
                lo_row = row_pair(lo[:, cols])
                total = None
                for slot, ref in enumerate((own, sib)):
                    whose = c if slot == 0 else 1 - c
                    part = attend(q_ref, ref, vt, slot, hh, j, G, whose * T, None, lo_row, False)
                    total = part if total is None else total + part
                for g in range(2):
                    n = 2 * hh + g
                    wide[n * HD : (n + 1) * HD, cols] += total[:HD, g * T : (g + 1) * T]
                    sums[n : n + 1, cols] += total[HD : HD + 1, g * T : (g + 1) * T]

    lse[...] = jnp.log2(sums[...])
    for n in range(4):
        inverse = 1.0 / sums[n : n + 1, :]
        scaled = wide[n * HD : (n + 1) * HD, :] * inverse
        att_t[n * HD : (n + 1) * HD, :] = scaled
        for j in range(4):
            att[j * T : (j + 1) * T, n * HD : (n + 1) * HD] = scaled[:, j * T : (j + 1) * T].T.astype(BF)
    moves.start(att, att_t)
    for k in range(4):
        turned[k * T : (k + 1) * T, :] = att[rows_at(shift_from(x_id, k), T), :]
    project(turned[...], lambda cols: w_nat[:, cols], nn, (p0, p1, p2, p3))


def stat_pair(stats, row, cols):
    return jnp.concatenate([stats[row : row + 1, cols], stats[row + 1 : row + 2, cols]], axis=1)


def attend_back(q_ref, datt, stats, lo, kv_ref, hh, j, count, base, qpos, dkv=None, kt=None):
    cols = slice(j * T, (j + 1) * T)
    lo_row = row_pair(lo[:, cols])
    lse_row, delta_row = stat_pair(stats, 2 * hh, cols), stat_pair(stats, 4 + 2 * hh, cols)
    qj = head_pair(q_ref, hh, j)
    dj = head_pair(datt, hh, j)
    dq = None
    for start, n in tiles(count):
        rows = slice(start, start + n)
        kc = slice(hh * HD, (hh + 1) * HD)
        vc = slice(256 + hh * HD, 256 + (hh + 1) * HD)
        s = nt(kv_ref[rows, kc], qj)
        dp = nt(kv_ref[rows, vc], dj)
        mask = key_positions(base, start, n) >= lo_row
        if qpos is not None:
            mask = mask & (key_positions(base, start, n) <= qpos)
        p = jnp.where(mask, jnp.exp2(s * SCALE2 - lse_row), 0.0)
        ds = (p * (dp - delta_row) * SCALE).astype(BF)
        if dkv is not None:
            dkv[rows, vc] += nn(p.astype(BF), dj)
            dkv[rows, kc] += nn(ds, qj)
        if kt is not None:
            part = nn(kt[hh, :, start : start + n], ds)
            dq = part if dq is None else dq + part
    return dq


def fill_keys(kt, slot, kv_ref):
    for hh in range(2):
        kt[slot, hh] = kv_ref[:, hh * HD : (hh + 1) * HD].T


def datt_kernel(ids, b0, b1, b2, b3, w_nat, lse, att_t, dmb, datt, stats, sent):
    for k, ref in enumerate((b0, b1, b2, b3)):
        dmb[rows_at(shift_from(ids[1], k), T), :] = ref[...]
    datt[...] = nt(dmb[...], w_nat[...]).astype(BF)
    stats[:4, :] = lse[:4, :]
    for n in range(4):
        cols = slice(n * HD, (n + 1) * HD)
        back = nt(w_nat[cols, :], dmb[...]).astype(BF).astype(F32)
        stats[4 + n : 5 + n, :] = jnp.sum(back * att_t[cols, :], axis=0, keepdims=True)
    sent[:G, :] = datt[...]
    high = stats[...].astype(BF).astype(F32)
    middle = (stats[...] - high).astype(BF).astype(F32)
    low = stats[...] - high - middle
    sent[G:, :] = jnp.concatenate([high, middle, low, jnp.zeros((8, G), F32)], axis=0).astype(BF)


def near_back_kernel(ids, q_ref, own, sib, lo, datt, stats, dq, dkv_own, dkv_sib, kt):
    zh, c = ids[0], ids[2]
    dkv_own[...] = jnp.zeros_like(dkv_own)
    dkv_sib[...] = jnp.zeros_like(dkv_sib)
    fill_keys(kt, 0, own)
    fill_keys(kt, 1, sib)
    for hh in range(2):
        for j in range(4):
            qpos = query_positions(zh, c, j)
            total = None
            for slot, (ref, dref, whose) in enumerate(((own, dkv_own, c), (sib, dkv_sib, 1 - c))):
                part = attend_back(
                    q_ref, datt, stats, lo, ref, hh, j, (j + 1) * T, zh * HALF + whose * T, qpos, dref, kt.at[slot]
                )
                total = part if total is None else total + part
            for g in range(2):
                n = 2 * hh + g
                dq[j * T : (j + 1) * T, n * HD : (n + 1) * HD] = total[:, g * T : (g + 1) * T].T


def far_back_kernel(ids, q, datt, stats, lo, far_own, far_sib, far, lo_far, own, sib,
                    dq_in, dkv_own_in, dkv_sib_in, dq, dkv_own, dkv_sib, kt, total_sib, stats_far):
    zh, c = ids[0], ids[2]
    dq[...] = dq_in[...]
    dkv_own[...] = dkv_own_in[...]
    total_sib[...] = dkv_sib_in[...]

    @pl.when(zh == 1)
    def _():
        fill_keys(kt, 0, far_own)
        fill_keys(kt, 1, far_sib)
        for hh in range(2):
            for j in range(4):
                total = None
                for slot, (ref, whose) in enumerate(((far_own, c), (far_sib, 1 - c))):
                    part = attend_back(q, datt, stats, lo, ref, hh, j, G, whose * T, None, None, kt.at[slot])
                    total = part if total is None else total + part
                for g in range(2):
                    n = 2 * hh + g
                    dq[j * T : (j + 1) * T, n * HD : (n + 1) * HD] += total[:, g * T : (g + 1) * T].T

    @pl.when(zh == 0)
    def _():
        parts = far[G:, :].astype(F32)
        stats_far[...] = parts[:8] + parts[8:16] + parts[16:24]
        for hh in range(2):
            for j in range(4):
                for ref, dref, whose in ((own, dkv_own, c), (sib, total_sib, 1 - c)):
                    attend_back(far_own, far, stats_far, lo_far, ref, hh, j, G, whose * T, None, dref, None)

    dkv_sib[...] = total_sib[...].astype(BF)


def head_back(w, raw, gain, cos, sin):
    w = w * cos - pltpu.roll(w, 64, 1) * sin
    r = lax.rsqrt(jnp.mean(raw * raw, axis=-1, keepdims=True) + EPS)
    a = w * gain
    out = r * a - raw * (r * r * r * jnp.mean(a * raw, axis=-1, keepdims=True))
    return out, jnp.sum(w * raw * r, axis=0, keepdims=True)


def q_back_kernel(dq, qraw, qk_gain, cos, sin, out, gains):
    total = jnp.zeros((1, HD), F32)
    for j in range(4):
        rows = slice(j * T, (j + 1) * T)
        for n in range(4):
            hc = slice(n * HD, (n + 1) * HD)
            value, part = head_back(dq[rows, hc], qraw[rows, hc], qk_gain[:, :HD], cos[rows, :], sin[rows, :])
            total += part
            out[rows, hc] = value.astype(BF)
    gains[...] = total


def kv_back_kernel(moves, ids, dkv, from_sib, kraw, qk_gain, cos, sin, weight, dq, dqkv, gains, p0, p1, p2, p3, turned):
    total = jnp.zeros((1, HD), F32)
    dqkv[:, :G] = dq[...]
    moves.wait(kraw)
    for j in range(4):
        rows = slice(j * T, (j + 1) * T)
        grad = dkv[rows, :] + from_sib[rows, :].astype(F32)
        for n in range(2):
            hc = slice(n * HD, (n + 1) * HD)
            value, part = head_back(grad[:, hc], kraw[rows, hc], qk_gain[:, HD:], cos[rows, :], sin[rows, :])
            total += part
            dqkv[rows, G + n * HD : G + (n + 1) * HD] = value.astype(BF)
        dqkv[rows, G + 256 :] = grad[:, 256:].astype(BF)
    gains[...] = total
    for k in range(4):
        turned[k * T : (k + 1) * T, :] = dqkv[rows_at(shift_from(ids[1], k), T), :]
    moves.wait(weight)
    project(turned[...], lambda cols: weight[cols, :], nt, (p0, p1, p2, p3))


def split_rows(c_id, value, keep, send, index):
    half = value.shape[0] // 2
    first = c_id == 0
    keep[index] = jnp.where(first, value[:half], value[half:])
    send[index] = jnp.where(first, value[half:], value[:half]).astype(BF)


def qkv_grad_kernel(ids, h, dqkv, gain_q, gain_k, squares, keep, send):
    total = jnp.broadcast_to(jnp.sum(squares[...], keepdims=True), (1, HD))
    note = jnp.concatenate([gain_q[...], gain_k[...], total, jnp.zeros((5, HD), F32)], axis=0)
    note = jnp.concatenate([note] * 8, axis=0)
    first = ids[2] == 0
    for b in range(8):
        value = tn(h[:, b * 128 : (b + 1) * 128], dqkv[...])
        keep[b, :, :D] = jnp.where(first, value[:64], value[64:])
        send[b, :, :D] = jnp.where(first, value[64:], value[:64]).astype(BF)
        keep[b, :, D:] = note
        send[b, :, D:] = note.astype(BF)


def add_qkv_kernel(keep, got, out):
    for zz in range(2):
        for x in range(4):
            value = keep[4 * zz + x] + got[4 * zz + x].astype(F32)
            for o in range(8):
                out[zz * 8 + o, x] = value[8 * o : 8 * o + 8].astype(BF)


def sum_qkv_kernel(ids, sums, own, s1, s2, s3, total):
    for x in range(4):
        value = sums[0, x].astype(F32)
        for device in range(1, 16):
            value += sums[device, x].astype(F32)
        total[x] = value
    for k, out in enumerate((own, s1, s2, s3)):
        out[...] = total[lax.rem(ids[1] + k, 4)].astype(BF)


def add_out_kernel(keep, got, out):
    for zz in range(2):
        value = keep[zz] + got[zz].astype(F32)
        for o in range(8):
            for g in range(2):
                out[zz * 8 + o, g] = value[16 * o + 8 * g : 16 * o + 8 * g + 8].astype(BF)


def sum_out_kernel(sums, out):
    for g in range(2):
        value = sums[0, g].astype(F32)
        for device in range(1, 16):
            value += sums[device, g].astype(F32)
        out[8 * g : 8 * g + 8, :] = value


def finish_qkv_kernel(ids, p0, p1, p2, p3, w, grad, gain, note):
    total = jnp.zeros((8, HD), F32)
    gain_sum = jnp.zeros((8, 1), F32)
    for k, ref in enumerate((p0, p1, p2, p3)):
        value = ref[...].astype(F32)
        total += value[:, D:]
        places = [(0, 0, 256), (256, HALF, 256)]
        places += [(G + n * HD, base, HD) for n, base in enumerate((2048, 2560, 3072, 3584))]
        for start, base, n in places:
            at = pl.ds(pl.multiple_of(base + shift_from(ids[1], k) * n, HD), n)
            part = value[:, start : start + n]
            grad[:, at] = part
            gain_sum += jnp.sum(part * w[:, at].astype(F32), axis=1, keepdims=True)
    gain[...] = jnp.broadcast_to(gain_sum, (8, HD))
    note[...] = total


def split_kernel(ids, grads, down, own, s1, s2, s3):
    for g in range(3):
        for half in range(2):
            down[8 * g : 8 * g + 8, half * 512 : (half + 1) * 512] = grads[12 + 2 * g + half].astype(F32)
    for k, out in enumerate((own, s1, s2, s3)):
        x = lax.rem(ids[1] + k, 4)
        for b in range(3):
            out[b] = grads[3 * x + b]


def finish_gate_up_kernel(ids, p0, p1, p2, p3, w, grad, gain):
    gain_sum = jnp.zeros((8, 1), F32)
    for k, ref in enumerate((p0, p1, p2, p3)):
        value = jnp.concatenate([ref[b].astype(F32) for b in range(3)], axis=1)
        for n in range(4):
            at = pl.ds(pl.multiple_of(n * 1536 + shift_from(ids[1], k) * 384, HD), 384)
            part = value[:, n * 384 : (n + 1) * 384]
            grad[:, at] = part
            gain_sum += jnp.sum(part * w[:, at].astype(F32), axis=1, keepdims=True)
    gain[...] = jnp.broadcast_to(gain_sum, (8, HD))


def out_grad_kernel(ids, att, dmb, keep, send):
    for b in range(2):
        split_rows(ids[2], tn(att[:, b * 256 : (b + 1) * 256], dmb[...]), keep, send, b)


def stack4(a, b, c, d):
    return jnp.concatenate([a[...], b[...], c[...], d[...]], axis=0)


def order_kernel(ids, own, sib, rows_own, rows_sib, weight, down):
    for whose, ref, rows in ((ids[2], own, rows_own), (1 - ids[2], sib, rows_sib)):
        for zz in range(2):
            for k in range(4):
                at = rows_at(2 * (4 * zz + shift_from(ids[1], k)) + whose, 64)
                weight[at, :] = blocks_of(ref, zz, k)
            parts = [rows[zz * 8 + o, 2 + g].astype(F32) for o in range(8) for g in range(3)]
            down[rows_at(2 * zz + whose, 192), :] = jnp.concatenate(parts, axis=0).astype(BF)


def ffn_kernel(h0, h1, h2, h3, weight, down, gate, up, act, h, p0, p1, p2, p3):
    h[...] = stack4(h0, h1, h2, h3)
    for t in range(3):
        cols = slice(t * 256, (t + 1) * 256)
        g = nn(h[...], weight[:, cols])
        u = nn(h[...], weight[:, 768 + t * 256 : 768 + (t + 1) * 256])
        gate[:, cols] = g
        up[:, cols] = u
        act[:, cols] = (g * jax.nn.sigmoid(g) * u).astype(BF)
    project(act[...], lambda cols: down[:, cols], nn, (p0, p1, p2, p3))


def ffn_back_kernel(g0, g1, g2, g3, gate, up, weight, down, dgu, p0, p1, p2, p3, gb):
    gb[...] = stack4(g0, g1, g2, g3)
    for t in range(3):
        cols = slice(t * 256, (t + 1) * 256)
        dact = nt(gb[...], down[cols, :])
        g = gate[:, cols]
        u = up[:, cols]
        s = jax.nn.sigmoid(g)
        dgu[:, cols] = (dact * u * s * (1.0 + g * (1.0 - s))).astype(BF)
        dgu[:, 768 + t * 256 : 768 + (t + 1) * 256] = (dact * g * s).astype(BF)
    project(dgu[...], lambda cols: weight[cols, :], nt, (p0, p1, p2, p3))


def ffn_grad_kernel(ids, h, g0, g1, g2, g3, act, dgu, d_keep, d_send, u_keep, u_send, gb):
    c_id = ids[2]
    gb[...] = stack4(g0, g1, g2, g3)
    for b in range(2):
        split_rows(c_id, tn(act[:, b * 384 : (b + 1) * 384], gb[...]), d_keep, d_send, b)
    for b in range(8):
        split_rows(c_id, tn(h[:, b * 128 : (b + 1) * 128], dgu[...]), u_keep, u_send, b)


def pack_grads_kernel(u_keep, u_got, d_keep, d_got, out):
    for zz in range(2):
        for x in range(4):
            value = u_keep[4 * zz + x] + u_got[4 * zz + x].astype(F32)
            for o in range(8):
                for b in range(3):
                    part = value[8 * o : 8 * o + 8, 512 * b : 512 * (b + 1)]
                    out[(zz * 8 + o) * 18 + 3 * x + b] = part.astype(BF)
        value = d_keep[zz] + d_got[zz].astype(F32)
        for o in range(8):
            for g in range(3):
                for half in range(2):
                    part = value[24 * o + 8 * g : 24 * o + 8 * g + 8, 512 * half : 512 * (half + 1)]
                    out[(zz * 8 + o) * 18 + 12 + 2 * g + half] = part.astype(BF)


def total_of(own, r1, r2, r3):
    return own[...] + r1[...].astype(F32) + r2[...].astype(F32) + r3[...].astype(F32)


def mid_kernel(tok, own, r1, r2, r3, gain, mid, h):
    v = tok[...].astype(F32) + total_of(own, r1, r2, r3)
    mid[...] = v
    r = lax.rsqrt(jnp.mean(v * v, axis=-1, keepdims=True) + EPS)
    h[...] = (v * r * gain[...]).astype(BF)


def loss_kernel(factor, mid, own, r1, r2, r3, teacher, mask, block, grad, grad_low, squares):
    v = mid[...] + total_of(own, r1, r2, r3)
    block[...] = v.astype(BF)
    diff = v - teacher[...].astype(F32)
    kept = jnp.broadcast_to(mask[...].astype(F32), (T, T)).T[:, :1] * diff
    out = factor[:, :1] * kept
    grad[...] = out
    grad_low[...] = out.astype(BF)
    squares[...] = jnp.sum((kept * diff).reshape(16, 8, D), axis=0)


def norm_back(v, gain, w):
    r = lax.rsqrt(jnp.mean(v * v, axis=-1, keepdims=True) + EPS)
    a = w * gain
    return r * a - v * (r * r * r * jnp.mean(a * v, axis=-1, keepdims=True))


def dmid_kernel(grad, own, r1, r2, r3, mid, gain, dmid, dmb):
    out = grad[...] + norm_back(mid[...], gain[...], total_of(own, r1, r2, r3))
    dmid[...] = out
    dmb[...] = out.astype(BF)


def last_kernel(dmid, own, r1, r2, r3, tok, gain, out):
    out[...] = dmid[...] + norm_back(tok[...].astype(F32), gain[...], total_of(own, r1, r2, r3))


def ring(k):
    return [(i, (i + k) % 4) for i in range(4)]


def around(v, k):
    return lax.ppermute(v, "x", ring(k))


def spread(v):
    return (v,) + tuple(around(v, k) for k in (1, 2, 3))


def collect(parts):
    return (parts[0],) + tuple(around(parts[k], -k) for k in (1, 2, 3))


def swap(v):
    return lax.ppermute(v, "c", [(0, 1), (1, 0)])


def partials():
    return [sds((T, D), F32)] + [sds((T, D), BF)] * 3


def local(tokens, teacher, doc_starts, valid_mask, qkv_weight, out_weight, gate_up_weight, down_weight,
          attn_gain, ffn_gain, qk_gain):
    zh, x_id, c_id = lax.axis_index("zh"), lax.axis_index("x"), lax.axis_index("c")
    z_id = zh * 2 + lax.axis_index("zl")
    ids = jnp.stack([zh, x_id, c_id, lax.axis_index("y"), z_id]).astype(jnp.int32)
    tok = tokens[0]

    w = qkv_weight[0]
    ts = spread(tok)
    rows, *sent = call(
        pack_kernel, [sds((5, 8, D), BF)] + [sds((8, 2688), BF)] * 4,
        [ids, w, gate_up_weight[0], out_weight[0], down_weight[0], attn_gain, ffn_gain, qk_gain, valid_mask],
        scratch=[pltpu.VMEM((HD, HD), F32)], smem=1, far=(1, 2, 3, 4),
    )
    columns = [sent[0]] + [around(sent[k], k) for k in (1, 2, 3)]
    first, second = call(join_kernel, [sds((16, 4, 8, 1152), BF), kept((16, 4, 8, 1536), BF)], columns)
    w_own = lax.all_to_all(first, ROWS, split_axis=0, concat_axis=0, tiled=True)
    w_sib = swap(w_own)
    toks, scales = call(gather_kernel, [sds((G, D), BF), sds((G, HD), F32)], [ids, *ts], smem=1, us=100)
    rows = lax.all_gather(rows, ROWS, axis=0, tiled=False)

    offset = jnp.arange(G, dtype=jnp.int32)
    positions = zh * HALF + c_id * T + offset + (offset // T) * T
    starts = doc_starts[0]
    reached = positions[None, :, None] + HALF * jnp.arange(2, dtype=jnp.int32)[:, None, None] >= starts[None, None, :]
    lo, lo_far = jnp.split(jnp.max(jnp.where(reached, starts[None, None, :], 0), axis=2), 2, axis=0)
    half = HD // 2
    frequency = jnp.exp(-(jnp.arange(half, dtype=F32) * 2.0 / HD) * math.log(THETA))
    angles = positions.astype(F32)[:, None] * frequency[None, :]
    cos, sin = jnp.cos(angles), jnp.sin(angles)
    cos = jnp.concatenate([cos, cos], axis=1)
    sin = jnp.concatenate([-sin, sin], axis=1)

    square = sds((G, G), BF)
    small = sds((8, G), F32)
    h_attn, q, kv, cross, qraw, kraw, gain_a, gain_f, gain_qk, factor, w_qkv = call(
        qkv_kernel,
        [kept((G, D), BF), kept((G, G), BF), kept((G, G), BF), square, kept((G, G), F32), kept((G, 256), F32),
         sds((1, D), F32), sds((1, D), F32), sds((1, 256), F32), sds((1, HD), F32), kept((D, D), BF)],
        [ids, toks, scales, w_own, w_sib, cos, sin],
        scratch=[pltpu.VMEM((D, HD), BF)], smem=1, lazy=True, after=[lo, lo_far], us=4)
    kv_sib = swap(kv)
    far_own = lax.ppermute(cross, "zh", [(0, 1), (1, 0)])
    acc, lsum = call(
        near_kernel, [sds((G, G), F32), small], [ids, q, kv, kv_sib, lo], after=[far_own],
        scratch=[pltpu.VMEM((2, 2, 144, G), BF)], smem=1, us=20, far=(1, 2, 3),
    )
    rows = behind(rows, acc)
    far_sib, rows_sib = swap(far_own), swap(rows)
    second = lax.all_to_all(behind(second, far_sib), ROWS, split_axis=0, concat_axis=0, tiled=True)
    att, att_t, lse, w_out, *parts = call(
        far_kernel,
        [kept((G, G), BF), kept((G, G), F32), small, kept((G, D), BF)] + partials(),
        [ids, q, far_own, far_sib, lo, acc, lsum, rows, rows_sib], lazy=True, far=(1, 2, 3),
        scratch=[pltpu.VMEM((2, 2, 144, G), BF), pltpu.VMEM((8, G), F32), pltpu.VMEM((G, G), F32),
                 pltpu.VMEM((G, G), BF)],
        smem=1, us=6)
    parts = collect(parts)
    mid, h = call(mid_kernel, [sds((T, D), F32), sds((T, D), BF)], [tok, *parts, gain_f])

    hs = spread(h)
    second = behind(second, h)
    w_gu, w_down = call(
        order_kernel, [sds((D, 1536), BF), sds((768, D), BF)], [ids, second, swap(second), rows, rows_sib],
        smem=1, us=2
    )
    gate, up, act, h_ffn, *parts = call(
        ffn_kernel,
        [sds((G, 768), F32), sds((G, 768), F32), sds((G, 768), BF), sds((G, D), BF)] + partials(),
        [*hs, w_gu, w_down], us=3)
    parts = collect(parts)
    block, grad, grad_low, squares = call(
        loss_kernel,
        [sds((T, D), BF), sds((T, D), F32), sds((T, D), BF), sds((8, D), F32)],
        [factor, mid, *parts, teacher[0], valid_mask],
    )

    gs = spread(grad_low)
    dgu, *parts = call(
        ffn_back_kernel, [sds((G, 1536), BF)] + partials(), [*gs, gate, up, w_gu, w_down],
        scratch=[pltpu.VMEM((G, D), BF)], us=3)
    parts = collect(parts)
    d_keep, d_send, u_keep, u_send = call(
        ffn_grad_kernel,
        [sds((2, 192, D), F32), sds((2, 192, D), BF), sds((8, 64, 1536), F32), sds((8, 64, 1536), BF)],
        [ids, h_ffn, *gs, act, dgu],
        scratch=[pltpu.VMEM((G, D), BF)], smem=1, us=30)
    grads, = call(pack_grads_kernel, [sds((288, 8, 512), BF)], [u_keep, swap(u_send), d_keep, swap(d_send)], us=2)
    dmid, dmb = call(
        dmid_kernel, [sds((T, D), F32), sds((T, D), BF)], [grad, *parts, mid, gain_f], us=30
    )
    bs = spread(dmb)
    dmb_all, datt, stats, sent = call(
        datt_kernel, [sds((G, D), BF), square, small, sds((G + 32, G), BF)], [ids, *bs, w_out, lse, att_t], smem=1, after=[grads], far=(5, 7), us=1)
    grads = lax.psum_scatter(grads, ROWS, scatter_dimension=0, tiled=True)
    far = lax.ppermute(sent, "zh", [(1, 0)])
    dq, dkv_own, dkv_sib = call(
        near_back_kernel, [sds((G, G), F32)] * 3, [ids, q, kv, kv_sib, lo, datt, stats],
        scratch=[pltpu.VMEM((2, 2, HD, G), BF)], smem=1, far=(1, 2, 3), us=1)
    o_keep, o_send = call(
        out_grad_kernel, [sds((2, 128, D), F32), sds((2, 128, D), BF)], [ids, att, dmb_all], smem=1, far=(1,), after=[dq],
    )
    outs, = call(add_out_kernel, [sds((16, 2, 8, D), BF)], [o_keep, swap(o_send)])
    dq, dkv_own, dkv_sib = call(
        far_back_kernel, [sds((G, G), F32), sds((G, G), F32), square],
        [ids, q, datt, stats, lo, far_own, far_sib, far, lo_far, kv, kv_sib, dq, dkv_own, dkv_sib],
        scratch=[pltpu.VMEM((2, 2, HD, G), BF), pltpu.VMEM((G, G), F32), pltpu.VMEM((8, G), F32)], smem=1,
        after=[outs], far=(1, 5, 6, 7, 9, 10), us=1)
    outs = lax.all_to_all(outs, ROWS, split_axis=0, concat_axis=0, tiled=True)
    dkv_sib = swap(dkv_sib)
    out_grad, = call(sum_out_kernel, [sds((16, D), F32)], [outs])
    dq, sum_q = call(q_back_kernel, [square, sds((1, HD), F32)], [dq, qraw, gain_qk, cos, sin], after=[out_grad], far=(1,), us=1)
    dqkv, sum_k, *parts = call(
        kv_back_kernel, [sds((G, D), BF), sds((1, HD), F32)] + partials(),
        [ids, dkv_own, dkv_sib, kraw, gain_qk, cos, sin, w_qkv, dq],
        scratch=[pltpu.VMEM((G, D), BF)], smem=1, far=(3, 7), lazy=True, us=1)
    parts = collect(parts)
    q_keep, q_send = call(
        qkv_grad_kernel, [sds((8, 64, 1152), F32), sds((8, 64, 1152), BF)],
        [ids, h_attn, dqkv, sum_q, sum_k, squares], smem=1, far=(1,), us=1)
    sums, = call(add_qkv_kernel, [sds((16, 4, 8, 1152), BF)], [q_keep, swap(q_send)])
    sums = lax.all_to_all(sums, ROWS, split_axis=0, concat_axis=0, tiled=True)
    tokens_grad, = call(last_kernel, [sds((T, D), F32)], [dmid, *parts, tok, gain_a])
    down_grad, *pieces = call(split_kernel, [sds((24, D), F32)] + [sds((3, 8, 512), BF)] * 4, [ids, grads], smem=1)
    pieces = [pieces[0]] + [around(pieces[k], k) for k in (1, 2, 3)]
    gate_up_grad, gain_f_grad = call(
        finish_gate_up_kernel, [sds((8, 2 * FF), F32), sds((8, HD), F32)], [ids, *pieces, gate_up_weight[0]], smem=1,
    )
    sums = call(
        sum_qkv_kernel, [sds((8, 1152), BF)] * 4, [ids, sums], scratch=[pltpu.VMEM((4, 8, 1152), F32)], smem=1,
        after=[tokens_grad, gate_up_grad],
    )
    sums = [sums[0]] + [around(sums[k], k) for k in (1, 2, 3)]
    qkv_grad, gain_a_grad, note = call(
        finish_qkv_kernel, [sds((8, 4096), F32), sds((8, HD), F32), sds((8, HD), F32)], [ids, *sums, w], smem=1,
    )
    mean_loss = note[2, 0] * factor[0, 0] * (1.0 / (TOKENS * D))
    place = ((zh * 4 + x_id) * 2 + c_id) * 8 + lax.axis_index("zl") * 4 + lax.axis_index("y")
    gain_qk_grad = lax.dynamic_slice(note[:2].reshape(256), (2 * place,), (2,))

    return (
        mean_loss,
        block[None],
        tokens_grad[None],
        qkv_grad[None],
        out_grad[None],
        gate_up_grad[None],
        down_grad[None],
        (gain_a_grad[:, 0] / attn_gain[0].astype(F32))[None],
        (gain_f_grad[:, 0] / ffn_gain[0].astype(F32))[None],
        gain_qk_grad[None],
    )


def solution(mesh):
    fine = Mesh(mesh.devices.reshape(2, 4, 2, 2, 4), ALL)
    ctx, wsh = ("zh", "x", "c"), ("zl", "y")
    states = P(wsh, ctx, None)
    matrix, vector = P(None, ALL, None), P(None, ALL)
    return jax.shard_map(
        local,
        mesh=fine,
        in_specs=(states, states, P(wsh, None), P(wsh, ctx)) + (matrix,) * 4 + (vector,) * 3,
        out_specs=(P(), states, states) + (matrix,) * 4 + (vector,) * 3,
        check_vma=False,
    )
```

```python
import math

import jax
import jax.numpy as jnp
from jax import lax
from jax.experimental import pallas as pl
from jax.experimental.pallas import tpu as pltpu
from jax.sharding import Mesh
from jax.sharding import PartitionSpec as P

D = 1024
HEADS = 16
KV_HEADS = 8
HD = 128
FF = 3072
T = 128
G = 512
HALF = 1024
EPS = 1e-06
THETA = 1000000.0
SCALE = 1.0 / math.sqrt(HD)
SCALE2 = SCALE / math.log(2.0)
TOKENS = 16384.0
MICROSECOND = 3 * 10**8

ALL = ("zh", "x", "c", "zl", "y")
ROWS = ("zh", "zl", "y")
CHIPS = ("zh", "x", "zl", "y")
BF = jnp.bfloat16
F32 = jnp.float32


def nt(a, b):
    return lax.dot_general(a, b, (((1,), (1,)), ((), ())), preferred_element_type=F32)


def nn(a, b):
    return lax.dot_general(a, b, (((1,), (0,)), ((), ())), preferred_element_type=F32)


def tn(a, b):
    return lax.dot_general(a, b, (((0,), (0,)), ((), ())), preferred_element_type=F32)


def sds(shape, dtype):
    return jax.ShapeDtypeStruct(shape, dtype)


class Moves:
    def __init__(self):
        self.copies, self.started, self.ended = {}, set(), set()

    def start(self, *refs):
        for ref in refs:
            if id(ref) not in self.started:
                self.started.add(id(ref))
                self.copies[id(ref)].start()

    def wait(self, *refs):
        for ref in refs:
            if id(ref) in self.copies and id(ref) not in self.ended:
                self.ended.add(id(ref))
                self.copies[id(ref)].wait()


def kept(shape, dtype):
    return pltpu.HBM(shape, dtype)


def in_hbm(value):
    return pltpu.with_memory_space_constraint(value, pltpu.HBM)


def call(body, outs, args, scratch=(), smem=0, limit=28, after=(), far=(), lazy=False, us=1):
    kept_out = [i for i, o in enumerate(outs) if not isinstance(o, jax.ShapeDtypeStruct)]
    vmem, hbm = pl.BlockSpec(memory_space=pltpu.VMEM), pl.BlockSpec(memory_space=pltpu.HBM)
    specs = [pl.BlockSpec(memory_space=pltpu.SMEM)] * smem
    specs += [hbm if i in far else vmem for i in range(smem, len(args))]
    specs += [pl.BlockSpec(memory_space=pl.ANY)] * len(after)
    count = len(args)
    staged = [(args[i].shape, args[i].dtype) for i in far]
    staged += [(outs[i].inner_aval.shape, outs[i].inner_aval.dtype) for i in kept_out]
    scratch = list(scratch) + [pltpu.VMEM(*a) for a in staged]
    if staged:
        scratch.append(pltpu.SemaphoreType.DMA((len(staged),)))

    def kernel(*refs):
        ins = list(refs[:count])
        results = list(refs[count + len(after) :][: len(outs)])
        rest = list(refs[count + len(after) + len(outs) :])
        if not staged:
            body(*ins, *results, *rest)
            return
        sems = rest.pop()
        stage = rest[len(rest) - len(staged) :]
        rest = rest[: len(rest) - len(staged)]
        moves = Moves()
        for n, i in enumerate(far):
            moves.copies[id(stage[n])] = pltpu.make_async_copy(ins[i], stage[n], sems.at[n])
            ins[i] = stage[n]
        for n, i in enumerate(kept_out, len(far)):
            moves.copies[id(stage[n])] = pltpu.make_async_copy(stage[n], results[i], sems.at[n])
            results[i] = stage[n]
        moves.start(*stage[: len(far)])
        if lazy:
            body(moves, *ins, *results, *rest)
        else:
            moves.wait(*stage[: len(far)])
            body(*ins, *results, *rest)
        moves.start(*stage)
        moves.wait(*stage)

    return pl.pallas_call(
        kernel,
        name=body.__name__,
        out_shape=list(outs),
        in_specs=specs,
        out_specs=[hbm if i in kept_out else vmem for i in range(len(outs))],
        scratch_shapes=scratch,
        compiler_params=pltpu.CompilerParams(vmem_limit_bytes=limit * 1024 * 1024),
        cost_estimate=pl.CostEstimate(flops=MICROSECOND * us, bytes_accessed=1, transcendentals=0),
    )(*[in_hbm(a) if i in far else a for i, a in enumerate(args)], *after)


def behind(value, *after):
    def nothing(*refs):
        del refs

    place = pl.BlockSpec(memory_space=pl.ANY)
    return pl.pallas_call(
        nothing,
        out_shape=sds(value.shape, value.dtype),
        in_specs=[place] * (1 + len(after)),
        out_specs=place,
        input_output_aliases={0: 0},
        cost_estimate=pl.CostEstimate(flops=1, bytes_accessed=1, transcendentals=0),
    )(value, *after)


def shift_from(x_id, k):
    return lax.rem(x_id - k + 4, 4)


def project(rows, weight, product, outs):
    for t in range(4):
        cols = slice(t * 256, (t + 1) * 256)
        value = product(rows, weight(cols))
        for k, out in enumerate(outs):
            out[:, cols] = value[k * T : (k + 1) * T].astype(out.dtype)


def rows_at(index, size):
    return pl.ds(pl.multiple_of(index * size, size), size)


def pack_kernel(ids, w, gu, out_w, down_w, gain_a, gain_f, gain_qk, mask, rows, own, s1, s2, s3, notes):
    for g in range(2):
        rows[g] = out_w[8 * g : 8 * g + 8, :]
    for g in range(3):
        rows[2 + g] = down_w[8 * g : 8 * g + 8, :]
    notes[...] = jnp.zeros_like(notes)
    notes[0:1, :8] = gain_a[...].astype(F32)
    notes[1:2, :8] = gain_f[...].astype(F32)
    notes[2:3, :2] = gain_qk[...].astype(F32)
    notes[3:4, :1] = jnp.sum(mask[...].astype(F32), axis=1, keepdims=True)
    note = notes[...].T[:8].astype(BF)
    for k, out in enumerate((own, s1, s2, s3)):
        x = lax.rem(ids[1] + k, 4)
        places = [(w, 0, 256), (w, HALF, 256)]
        places += [(w, base, HD) for base in (2048, 2560, 3072, 3584)]
        places += [(None, 0, 0)] + [(gu, base, 384) for base in (0, 1536, 3072, 4608)]
        at = 0
        for ref, base, n in places:
            if ref is None:
                out[:, at : at + HD] = note
                at += HD
            else:
                out[:, at : at + n] = ref[:, pl.ds(pl.multiple_of(base + x * n, HD), n)]
                at += n


def join_kernel(p0, p1, p2, p3, first, second):
    for k, ref in enumerate((p0, p1, p2, p3)):
        block, other = ref[:, :1152], ref[:, 1152:]
        for device in range(16):
            first[device, k] = block
            second[device, k] = other


def gather_kernel(ids, t0, t1, t2, t3, toks, scale):
    for k, ref in enumerate((t0, t1, t2, t3)):
        rows = rows_at(shift_from(ids[1], k), T)
        toks[rows, :] = ref[...]
        t = ref[...].astype(F32)
        r = lax.rsqrt(jnp.mean(t * t, axis=-1, keepdims=True) + EPS)
        scale[rows, :] = jnp.broadcast_to(r, (T, HD))


def blocks_of(got, zz, k):
    return jnp.concatenate([got[zz * 8 + other, k].astype(F32) for other in range(8)], axis=0).astype(BF)


def qkv_kernel(moves, ids, toks, scale, own, sib, cos, sin,
               h_ref, q_ref, kv_ref, cross, qraw, kraw, gain, gain_f, qk_gain, factor, weight, wide):
    c_id = ids[2]
    for zz in range(2):
        for k in range(4):
            at = 2 * (4 * zz + shift_from(ids[1], k))
            for whose, ref in ((c_id, own), (1 - c_id, sib)):
                value = blocks_of(ref, zz, k)
                weight[rows_at(at + whose, 64), :] = value[:, :D]
                wide[rows_at(at + whose, 64), :] = value[:, D:]
    moves.start(weight)
    notes = wide[...].T
    gain[...] = notes[0:1].astype(F32)
    gain_f[...] = notes[1:2].astype(F32)
    at = lax.broadcasted_iota(jnp.int32, (D, 256), 0)
    entry = lax.broadcasted_iota(jnp.int32, (D, 256), 1)
    pick = jnp.where(at == 8 * (entry >> 1) + (entry & 1), 1.0, 0.0).astype(BF)
    qk_gain[...] = nn(notes[:16], pick)[2:3]
    count = jnp.sum(notes[3:4].astype(F32), axis=1, keepdims=True)
    factor[...] = jnp.broadcast_to(TOKENS / count, (1, HD))

    def rope(v, gains, rows):
        r = lax.rsqrt(jnp.mean(v * v, axis=-1, keepdims=True) + EPS)
        n = v * r * gains
        return (n * cos[rows, :] + pltpu.roll(n, 64, 1) * sin[rows, :]).astype(BF)

    for j in range(4):
        rows = slice(j * T, (j + 1) * T)
        t = toks[rows, :].astype(F32)
        h = (t * scale[rows, :1] * gain[...]).astype(BF)
        h_ref[rows, :] = h
        q = nn(h, weight[:, :G])
        kv = nn(h, weight[:, G:])
        qraw[rows, :] = q
        kraw[rows, :] = kv[:, :256]
        kv_ref[rows, 256:] = kv[:, 256:].astype(BF)
        for n in range(4):
            q_ref[rows, n * HD : (n + 1) * HD] = rope(q[:, n * HD : (n + 1) * HD], qk_gain[:, :HD], rows)
        for n in range(2):
            kv_ref[rows, n * HD : (n + 1) * HD] = rope(kv[:, n * HD : (n + 1) * HD], qk_gain[:, HD:], rows)
    cross[...] = jnp.where(ids[0] == 0, kv_ref[...], q_ref[...])


def head_pair(ref, hh, j):
    rows = slice(j * T, (j + 1) * T)
    base = hh * 256
    return jnp.concatenate([ref[rows, base : base + HD], ref[rows, base + HD : base + 256]], axis=0)


def row_pair(row):
    return jnp.concatenate([row, row], axis=1)


def key_positions(base, start, count):
    index = lax.broadcasted_iota(jnp.int32, (count, 1), 0) + start
    return base + index + (index >> 7) * T


def query_positions(zh, c, j):
    row = lax.broadcasted_iota(jnp.int32, (1, T), 1) + (zh * HALF + j * 256 + c * T)
    return row_pair(row)


def fill_values(vt, slot, kv_ref):
    for hh in range(2):
        vt[slot, hh, :HD, :] = kv_ref[:, 256 + hh * HD : 256 + (hh + 1) * HD].T
        vt[slot, hh, HD:, :] = jnp.ones((16, G), BF)


def tiles(count):
    return [(t, min(256, count - t)) for t in range(0, count, 256)]


def join_out(c, own, sib, weight):
    for hh in range(2):
        for whose, ref in ((c, own), (1 - c, sib)):
            parts = [ref[hh * 8 + o, g].astype(F32) for o in range(8) for g in range(2)]
            weight[rows_at(2 * hh + whose, HD), :] = jnp.concatenate(parts, axis=0).astype(BF)


def attend(q_ref, kv_ref, vt, slot, hh, j, count, base, qpos, lo_row, causal):
    qj = head_pair(q_ref, hh, j)
    total = None
    for start, n in tiles(count):
        keys = kv_ref[start : start + n, hh * HD : (hh + 1) * HD]
        s = nt(keys, qj)
        kpos = key_positions(base, start, n)
        mask = kpos >= lo_row
        if causal:
            mask = mask & (kpos <= qpos)
        p = jnp.where(mask, jnp.exp2(s * SCALE2), 0.0).astype(BF)
        part = nn(vt[slot, hh, :, start : start + n], p)
        total = part if total is None else total + part
    return total


def attention_kernel(moves, ids, q_ref, own, sib, far_own, far_sib, lo, rows_own, rows_sib,
                     att, att_t, lse, w_nat, p0, p1, p2, p3, vt, sums, wide, turned):
    zh, x_id, c = ids[0], ids[1], ids[2]
    join_out(c, rows_own, rows_sib, w_nat)
    moves.start(w_nat)
    moves.wait(q_ref, own, sib, far_own, far_sib)
    fill_values(vt, 0, own)
    fill_values(vt, 1, sib)
    sums[4:8, :] = jnp.ones((4, G), F32)
    for hh in range(2):
        for j in range(4):
            cols = slice(j * T, (j + 1) * T)
            lo_row = row_pair(lo[:, cols])
            qpos = query_positions(zh, c, j)
            total = None
            for slot, (ref, whose) in enumerate(((own, c), (sib, 1 - c))):
                part = attend(
                    q_ref, ref, vt, slot, hh, j, (j + 1) * T, zh * HALF + whose * T, qpos, lo_row, True
                )
                total = part if total is None else total + part
            for g in range(2):
                n = 2 * hh + g
                wide[n * HD : (n + 1) * HD, cols] = total[:HD, g * T : (g + 1) * T]
                sums[n : n + 1, cols] = total[HD : HD + 1, g * T : (g + 1) * T]

    @pl.when(zh == 1)
    def _():
        fill_values(vt, 0, far_own)
        fill_values(vt, 1, far_sib)
        for hh in range(2):
            for j in range(4):
                cols = slice(j * T, (j + 1) * T)
                lo_row = row_pair(lo[:, cols])
                total = None
                for slot, (ref, whose) in enumerate(((far_own, c), (far_sib, 1 - c))):
                    part = attend(q_ref, ref, vt, slot, hh, j, G, whose * T, None, lo_row, False)
                    total = part if total is None else total + part
                for g in range(2):
                    n = 2 * hh + g
                    wide[n * HD : (n + 1) * HD, cols] += total[:HD, g * T : (g + 1) * T]
                    sums[n : n + 1, cols] += total[HD : HD + 1, g * T : (g + 1) * T]

    lse[...] = jnp.log2(sums[...])
    for n in range(4):
        inverse = 1.0 / sums[n : n + 1, :]
        scaled = wide[n * HD : (n + 1) * HD, :] * inverse
        att_t[n * HD : (n + 1) * HD, :] = scaled
        for j in range(4):
            att[j * T : (j + 1) * T, n * HD : (n + 1) * HD] = scaled[:, j * T : (j + 1) * T].T.astype(BF)
    moves.start(att, att_t)
    for k in range(4):
        turned[k * T : (k + 1) * T, :] = att[rows_at(shift_from(x_id, k), T), :]
    project(turned[...], lambda cols: w_nat[:, cols], nn, (p0, p1, p2, p3))


def stat_pair(stats, row, cols):
    return jnp.concatenate([stats[row : row + 1, cols], stats[row + 1 : row + 2, cols]], axis=1)


def attend_back(q_ref, datt, stats, lo, kv_ref, hh, j, count, base, qpos, dkv=None, kt=None):
    cols = slice(j * T, (j + 1) * T)
    lo_row = row_pair(lo[:, cols])
    lse_row, delta_row = stat_pair(stats, 2 * hh, cols), stat_pair(stats, 4 + 2 * hh, cols)
    qj = head_pair(q_ref, hh, j)
    dj = head_pair(datt, hh, j)
    dq = None
    for start, n in tiles(count):
        rows = slice(start, start + n)
        kc = slice(hh * HD, (hh + 1) * HD)
        vc = slice(256 + hh * HD, 256 + (hh + 1) * HD)
        s = nt(kv_ref[rows, kc], qj)
        dp = nt(kv_ref[rows, vc], dj)
        mask = key_positions(base, start, n) >= lo_row
        if qpos is not None:
            mask = mask & (key_positions(base, start, n) <= qpos)
        p = jnp.where(mask, jnp.exp2(s * SCALE2 - lse_row), 0.0)
        ds = (p * (dp - delta_row) * SCALE).astype(BF)
        if dkv is not None:
            dkv[rows, vc] += nn(p.astype(BF), dj)
            dkv[rows, kc] += nn(ds, qj)
        if kt is not None:
            part = nn(kt[hh, :, start : start + n], ds)
            dq = part if dq is None else dq + part
    return dq


def fill_keys(kt, slot, kv_ref):
    for hh in range(2):
        kt[slot, hh] = kv_ref[:, hh * HD : (hh + 1) * HD].T


def datt_kernel(moves, ids, b0, b1, b2, b3, w_nat, lse, att_t, dmb, datt, stats, sent):
    for k, ref in enumerate((b0, b1, b2, b3)):
        dmb[rows_at(shift_from(ids[1], k), T), :] = ref[...]
    moves.wait(w_nat)
    datt[...] = nt(dmb[...], w_nat[...]).astype(BF)
    moves.wait(att_t)
    stats[:4, :] = lse[:4, :]
    for n in range(4):
        cols = slice(n * HD, (n + 1) * HD)
        back = nt(w_nat[cols, :], dmb[...]).astype(BF).astype(F32)
        stats[4 + n : 5 + n, :] = jnp.sum(back * att_t[cols, :], axis=0, keepdims=True)
    sent[:G, :] = datt[...]
    high = stats[...].astype(BF).astype(F32)
    middle = (stats[...] - high).astype(BF).astype(F32)
    low = stats[...] - high - middle
    sent[G:, :] = jnp.concatenate([high, middle, low, jnp.zeros((8, G), F32)], axis=0).astype(BF)


def near_back_kernel(ids, q_ref, own, sib, lo, datt, stats, dq, dkv_own, dkv_sib, kt):
    zh, c = ids[0], ids[2]
    dkv_own[...] = jnp.zeros_like(dkv_own)
    dkv_sib[...] = jnp.zeros_like(dkv_sib)
    fill_keys(kt, 0, own)
    fill_keys(kt, 1, sib)
    for hh in range(2):
        for j in range(4):
            qpos = query_positions(zh, c, j)
            total = None
            for slot, (ref, dref, whose) in enumerate(((own, dkv_own, c), (sib, dkv_sib, 1 - c))):
                part = attend_back(
                    q_ref, datt, stats, lo, ref, hh, j, (j + 1) * T, zh * HALF + whose * T, qpos, dref, kt.at[slot]
                )
                total = part if total is None else total + part
            for g in range(2):
                n = 2 * hh + g
                dq[j * T : (j + 1) * T, n * HD : (n + 1) * HD] = total[:, g * T : (g + 1) * T].T


def far_back_kernel(ids, q, datt, stats, lo, far_own, far_sib, far, lo_far, own, sib,
                    dq_in, dkv_own_in, dkv_sib_in, dq, dkv_own, dkv_sib, kt, total_sib, stats_far):
    zh, c = ids[0], ids[2]
    dq[...] = dq_in[...]
    dkv_own[...] = dkv_own_in[...]
    total_sib[...] = dkv_sib_in[...]

    @pl.when(zh == 1)
    def _():
        fill_keys(kt, 0, far_own)
        fill_keys(kt, 1, far_sib)
        for hh in range(2):
            for j in range(4):
                total = None
                for slot, (ref, whose) in enumerate(((far_own, c), (far_sib, 1 - c))):
                    part = attend_back(q, datt, stats, lo, ref, hh, j, G, whose * T, None, None, kt.at[slot])
                    total = part if total is None else total + part
                for g in range(2):
                    n = 2 * hh + g
                    dq[j * T : (j + 1) * T, n * HD : (n + 1) * HD] += total[:, g * T : (g + 1) * T].T

    @pl.when(zh == 0)
    def _():
        parts = far[G:, :].astype(F32)
        stats_far[...] = parts[:8] + parts[8:16] + parts[16:24]
        for hh in range(2):
            for j in range(4):
                for ref, dref, whose in ((own, dkv_own, c), (sib, total_sib, 1 - c)):
                    attend_back(far_own, far, stats_far, lo_far, ref, hh, j, G, whose * T, None, dref, None)

    dkv_sib[...] = total_sib[...].astype(BF)


def head_back(w, raw, gain, cos, sin):
    w = w * cos - pltpu.roll(w, 64, 1) * sin
    r = lax.rsqrt(jnp.mean(raw * raw, axis=-1, keepdims=True) + EPS)
    a = w * gain
    out = r * a - raw * (r * r * r * jnp.mean(a * raw, axis=-1, keepdims=True))
    return out, jnp.sum(w * raw * r, axis=0, keepdims=True)


def q_back_kernel(dq, qraw, qk_gain, cos, sin, out, gains):
    total = jnp.zeros((1, HD), F32)
    for j in range(4):
        rows = slice(j * T, (j + 1) * T)
        for n in range(4):
            hc = slice(n * HD, (n + 1) * HD)
            value, part = head_back(dq[rows, hc], qraw[rows, hc], qk_gain[:, :HD], cos[rows, :], sin[rows, :])
            total += part
            out[rows, hc] = value.astype(BF)
    gains[...] = total


def kv_back_kernel(moves, ids, dkv, from_sib, kraw, qk_gain, cos, sin, weight, dq, dqkv, gains, p0, p1, p2, p3, turned):
    total = jnp.zeros((1, HD), F32)
    dqkv[:, :G] = dq[...]
    moves.wait(kraw)
    for j in range(4):
        rows = slice(j * T, (j + 1) * T)
        grad = dkv[rows, :] + from_sib[rows, :].astype(F32)
        for n in range(2):
            hc = slice(n * HD, (n + 1) * HD)
            value, part = head_back(grad[:, hc], kraw[rows, hc], qk_gain[:, HD:], cos[rows, :], sin[rows, :])
            total += part
            dqkv[rows, G + n * HD : G + (n + 1) * HD] = value.astype(BF)
        dqkv[rows, G + 256 :] = grad[:, 256:].astype(BF)
    gains[...] = total
    for k in range(4):
        turned[k * T : (k + 1) * T, :] = dqkv[rows_at(shift_from(ids[1], k), T), :]
    moves.wait(weight)
    project(turned[...], lambda cols: weight[cols, :], nt, (p0, p1, p2, p3))


def split_rows(c_id, value, keep, send, index):
    half = value.shape[0] // 2
    first = c_id == 0
    keep[index] = jnp.where(first, value[:half], value[half:])
    send[index] = jnp.where(first, value[half:], value[:half]).astype(BF)


def qkv_grad_kernel(ids, h, dqkv, gain_q, gain_k, squares, keep, send):
    total = jnp.broadcast_to(jnp.sum(squares[...], keepdims=True), (1, HD))
    note = jnp.concatenate([gain_q[...], gain_k[...], total, jnp.zeros((5, HD), F32)], axis=0)
    note = jnp.concatenate([note] * 8, axis=0)
    first = ids[2] == 0
    for b in range(8):
        value = tn(h[:, b * 128 : (b + 1) * 128], dqkv[...])
        keep[b, :, :D] = jnp.where(first, value[:64], value[64:])
        send[b, :, :D] = jnp.where(first, value[64:], value[:64]).astype(BF)
        keep[b, :, D:] = note
        send[b, :, D:] = note.astype(BF)


def add_qkv_kernel(keep, got, out):
    for zz in range(2):
        for x in range(4):
            value = keep[4 * zz + x] + got[4 * zz + x].astype(F32)
            for o in range(8):
                out[zz * 8 + o, x] = value[8 * o : 8 * o + 8].astype(BF)


def sum_qkv_kernel(ids, sums, own, s1, s2, s3, total):
    for x in range(4):
        value = sums[0, x].astype(F32)
        for device in range(1, 16):
            value += sums[device, x].astype(F32)
        total[x] = value
    for k, out in enumerate((own, s1, s2, s3)):
        out[...] = total[lax.rem(ids[1] + k, 4)].astype(BF)


def add_out_kernel(keep, got, out):
    for zz in range(2):
        value = keep[zz] + got[zz].astype(F32)
        for o in range(8):
            for g in range(2):
                out[zz * 8 + o, g] = value[16 * o + 8 * g : 16 * o + 8 * g + 8].astype(BF)


def sum_out_kernel(sums, out):
    for g in range(2):
        value = sums[0, g].astype(F32)
        for device in range(1, 16):
            value += sums[device, g].astype(F32)
        out[8 * g : 8 * g + 8, :] = value


def finish_qkv_kernel(ids, p0, p1, p2, p3, w, grad, gain, note):
    total = jnp.zeros((8, HD), F32)
    gain_sum = jnp.zeros((8, 1), F32)
    for k, ref in enumerate((p0, p1, p2, p3)):
        value = ref[...].astype(F32)
        total += value[:, D:]
        places = [(0, 0, 256), (256, HALF, 256)]
        places += [(G + n * HD, base, HD) for n, base in enumerate((2048, 2560, 3072, 3584))]
        for start, base, n in places:
            at = pl.ds(pl.multiple_of(base + shift_from(ids[1], k) * n, HD), n)
            part = value[:, start : start + n]
            grad[:, at] = part
            gain_sum += jnp.sum(part * w[:, at].astype(F32), axis=1, keepdims=True)
    gain[...] = jnp.broadcast_to(gain_sum, (8, HD))
    note[...] = total


def split_kernel(ids, grads, down, own, s1, s2, s3):
    for g in range(3):
        for half in range(2):
            down[8 * g : 8 * g + 8, half * 512 : (half + 1) * 512] = grads[12 + 2 * g + half].astype(F32)
    for k, out in enumerate((own, s1, s2, s3)):
        x = lax.rem(ids[1] + k, 4)
        for b in range(3):
            out[b] = grads[3 * x + b]


def finish_gate_up_kernel(ids, p0, p1, p2, p3, w, grad, gain):
    gain_sum = jnp.zeros((8, 1), F32)
    for k, ref in enumerate((p0, p1, p2, p3)):
        value = jnp.concatenate([ref[b].astype(F32) for b in range(3)], axis=1)
        for n in range(4):
            at = pl.ds(pl.multiple_of(n * 1536 + shift_from(ids[1], k) * 384, HD), 384)
            part = value[:, n * 384 : (n + 1) * 384]
            grad[:, at] = part
            gain_sum += jnp.sum(part * w[:, at].astype(F32), axis=1, keepdims=True)
    gain[...] = jnp.broadcast_to(gain_sum, (8, HD))


def out_grad_kernel(ids, att, dmb, keep, send):
    for b in range(2):
        split_rows(ids[2], tn(att[:, b * 256 : (b + 1) * 256], dmb[...]), keep, send, b)


def stack4(a, b, c, d):
    return jnp.concatenate([a[...], b[...], c[...], d[...]], axis=0)


def order_kernel(ids, own, sib, rows_own, rows_sib, weight, down):
    for whose, ref, rows in ((ids[2], own, rows_own), (1 - ids[2], sib, rows_sib)):
        for zz in range(2):
            for k in range(4):
                at = rows_at(2 * (4 * zz + shift_from(ids[1], k)) + whose, 64)
                weight[at, :] = blocks_of(ref, zz, k)
            parts = [rows[zz * 8 + o, 2 + g].astype(F32) for o in range(8) for g in range(3)]
            down[rows_at(2 * zz + whose, 192), :] = jnp.concatenate(parts, axis=0).astype(BF)


def ffn_kernel(h0, h1, h2, h3, weight, down, gate, up, act, h, p0, p1, p2, p3):
    h[...] = stack4(h0, h1, h2, h3)
    for t in range(3):
        cols = slice(t * 256, (t + 1) * 256)
        g = nn(h[...], weight[:, cols])
        u = nn(h[...], weight[:, 768 + t * 256 : 768 + (t + 1) * 256])
        gate[:, cols] = g
        up[:, cols] = u
        act[:, cols] = (g * jax.nn.sigmoid(g) * u).astype(BF)
    project(act[...], lambda cols: down[:, cols], nn, (p0, p1, p2, p3))


def ffn_back_kernel(g0, g1, g2, g3, gate, up, weight, down, dgu, p0, p1, p2, p3, gb):
    gb[...] = stack4(g0, g1, g2, g3)
    for t in range(3):
        cols = slice(t * 256, (t + 1) * 256)
        dact = nt(gb[...], down[cols, :])
        g = gate[:, cols]
        u = up[:, cols]
        s = jax.nn.sigmoid(g)
        dgu[:, cols] = (dact * u * s * (1.0 + g * (1.0 - s))).astype(BF)
        dgu[:, 768 + t * 256 : 768 + (t + 1) * 256] = (dact * g * s).astype(BF)
    project(dgu[...], lambda cols: weight[cols, :], nt, (p0, p1, p2, p3))


def ffn_grad_kernel(ids, h, g0, g1, g2, g3, act, dgu, d_keep, d_send, u_keep, u_send, gb):
    c_id = ids[2]
    gb[...] = stack4(g0, g1, g2, g3)
    for b in range(2):
        split_rows(c_id, tn(act[:, b * 384 : (b + 1) * 384], gb[...]), d_keep, d_send, b)
    for b in range(8):
        split_rows(c_id, tn(h[:, b * 128 : (b + 1) * 128], dgu[...]), u_keep, u_send, b)


def pack_grads_kernel(u_keep, u_got, d_keep, d_got, out):
    for zz in range(2):
        for x in range(4):
            value = u_keep[4 * zz + x] + u_got[4 * zz + x].astype(F32)
            for o in range(8):
                for b in range(3):
                    part = value[8 * o : 8 * o + 8, 512 * b : 512 * (b + 1)]
                    out[(zz * 8 + o) * 18 + 3 * x + b] = part.astype(BF)
        value = d_keep[zz] + d_got[zz].astype(F32)
        for o in range(8):
            for g in range(3):
                for half in range(2):
                    part = value[24 * o + 8 * g : 24 * o + 8 * g + 8, 512 * half : 512 * (half + 1)]
                    out[(zz * 8 + o) * 18 + 12 + 2 * g + half] = part.astype(BF)


def total_of(own, r1, r2, r3):
    return own[...] + r1[...].astype(F32) + r2[...].astype(F32) + r3[...].astype(F32)


def mid_kernel(tok, own, r1, r2, r3, gain, mid, h):
    v = tok[...].astype(F32) + total_of(own, r1, r2, r3)
    mid[...] = v
    r = lax.rsqrt(jnp.mean(v * v, axis=-1, keepdims=True) + EPS)
    h[...] = (v * r * gain[...]).astype(BF)


def loss_kernel(factor, mid, own, r1, r2, r3, teacher, mask, block, grad, grad_low, squares):
    v = mid[...] + total_of(own, r1, r2, r3)
    block[...] = v.astype(BF)
    diff = v - teacher[...].astype(F32)
    kept = jnp.broadcast_to(mask[...].astype(F32), (T, T)).T[:, :1] * diff
    out = factor[:, :1] * kept
    grad[...] = out
    grad_low[...] = out.astype(BF)
    squares[...] = jnp.sum((kept * diff).reshape(16, 8, D), axis=0)


def norm_back(v, gain, w):
    r = lax.rsqrt(jnp.mean(v * v, axis=-1, keepdims=True) + EPS)
    a = w * gain
    return r * a - v * (r * r * r * jnp.mean(a * v, axis=-1, keepdims=True))


def dmid_kernel(grad, own, r1, r2, r3, mid, gain, dmid, dmb):
    out = grad[...] + norm_back(mid[...], gain[...], total_of(own, r1, r2, r3))
    dmid[...] = out
    dmb[...] = out.astype(BF)


def last_kernel(dmid, own, r1, r2, r3, tok, gain, out):
    out[...] = dmid[...] + norm_back(tok[...].astype(F32), gain[...], total_of(own, r1, r2, r3))


def ring(k):
    return [(i, (i + k) % 4) for i in range(4)]


def around(v, k):
    return lax.ppermute(v, "x", ring(k))


def spread(v):
    return (v,) + tuple(around(v, k) for k in (1, 2, 3))


def collect(parts):
    return (parts[0],) + tuple(around(parts[k], -k) for k in (1, 2, 3))


def swap(v):
    return lax.ppermute(v, "c", [(0, 1), (1, 0)])


def partials():
    return [sds((T, D), F32)] + [sds((T, D), BF)] * 3


def local(tokens, teacher, doc_starts, valid_mask, qkv_weight, out_weight, gate_up_weight, down_weight,
          attn_gain, ffn_gain, qk_gain):
    zh, x_id, c_id = lax.axis_index("zh"), lax.axis_index("x"), lax.axis_index("c")
    z_id = zh * 2 + lax.axis_index("zl")
    ids = jnp.stack([zh, x_id, c_id, lax.axis_index("y"), z_id]).astype(jnp.int32)
    tok = tokens[0]

    w = qkv_weight[0]
    rows, *sent = call(
        pack_kernel, [sds((5, 8, D), BF)] + [sds((8, 2688), BF)] * 4,
        [ids, w, gate_up_weight[0], out_weight[0], down_weight[0], attn_gain, ffn_gain, qk_gain, valid_mask],
        scratch=[pltpu.VMEM((HD, HD), F32)], smem=1, far=(1, 2, 3, 4),
    )
    columns = [sent[0]] + [around(sent[k], k) for k in (1, 2, 3)]
    first, second = call(join_kernel, [sds((16, 4, 8, 1152), BF), kept((16, 4, 8, 1536), BF)], columns)
    w_own = lax.all_to_all(first, ROWS, split_axis=0, concat_axis=0, tiled=True)
    w_sib = swap(w_own)
    ts = spread(behind(tok, first))
    toks, scales = call(gather_kernel, [sds((G, D), BF), sds((G, HD), F32)], [ids, *ts], smem=1, us=100)
    rows = lax.all_gather(rows, ROWS, axis=0, tiled=False)

    offset = jnp.arange(G, dtype=jnp.int32)
    positions = zh * HALF + c_id * T + offset + (offset // T) * T
    starts = doc_starts[0]
    reached = positions[None, :, None] + HALF * jnp.arange(2, dtype=jnp.int32)[:, None, None] >= starts[None, None, :]
    lo, lo_far = jnp.split(jnp.max(jnp.where(reached, starts[None, None, :], 0), axis=2), 2, axis=0)
    half = HD // 2
    frequency = jnp.exp(-(jnp.arange(half, dtype=F32) * 2.0 / HD) * math.log(THETA))
    angles = positions.astype(F32)[:, None] * frequency[None, :]
    cos, sin = jnp.cos(angles), jnp.sin(angles)
    cos = jnp.concatenate([cos, cos], axis=1)
    sin = jnp.concatenate([-sin, sin], axis=1)

    square = sds((G, G), BF)
    small = sds((8, G), F32)
    h_attn, q, kv, cross, qraw, kraw, gain_a, gain_f, gain_qk, factor, w_qkv = call(
        qkv_kernel,
        [kept((G, D), BF), kept((G, G), BF), kept((G, G), BF), square, kept((G, G), F32), kept((G, 256), F32),
         sds((1, D), F32), sds((1, D), F32), sds((1, 256), F32), sds((1, HD), F32), kept((D, D), BF)],
        [ids, toks, scales, w_own, w_sib, cos, sin],
        scratch=[pltpu.VMEM((D, HD), BF)], smem=1, lazy=True, after=[lo, lo_far], us=4)
    kv_sib = swap(kv)
    far_own = lax.ppermute(cross, "zh", [(0, 1), (1, 0)])
    rows = behind(rows, far_own, kv_sib)
    far_sib, rows_sib = swap(far_own), swap(rows)
    second = lax.all_to_all(behind(second, far_sib), ROWS, split_axis=0, concat_axis=0, tiled=True)
    att, att_t, lse, w_out, *parts = call(
        attention_kernel,
        [kept((G, G), BF), kept((G, G), F32), small, kept((G, D), BF)] + partials(),
        [ids, q, kv, kv_sib, far_own, far_sib, lo, rows, rows_sib],
        scratch=[pltpu.VMEM((2, 2, 144, G), BF), pltpu.VMEM((8, G), F32), pltpu.VMEM((G, G), F32),
                 pltpu.VMEM((G, G), BF)],
        smem=1, lazy=True, far=(1, 2, 3, 4, 5), us=10,
    )
    parts = collect(parts)
    mid, h = call(mid_kernel, [sds((T, D), F32), sds((T, D), BF)], [tok, *parts, gain_f])

    hs = spread(h)
    second = behind(second, h)
    w_gu, w_down = call(
        order_kernel, [sds((D, 1536), BF), sds((768, D), BF)], [ids, second, swap(second), rows, rows_sib],
        smem=1, us=2
    )
    gate, up, act, h_ffn, *parts = call(
        ffn_kernel,
        [sds((G, 768), F32), sds((G, 768), F32), sds((G, 768), BF), sds((G, D), BF)] + partials(),
        [*hs, w_gu, w_down], us=3)
    parts = collect(parts)
    block, grad, grad_low, squares = call(
        loss_kernel,
        [sds((T, D), BF), sds((T, D), F32), sds((T, D), BF), sds((8, D), F32)],
        [factor, mid, *parts, teacher[0], valid_mask],
    )

    gs = spread(grad_low)
    dgu, *parts = call(
        ffn_back_kernel, [sds((G, 1536), BF)] + partials(), [*gs, gate, up, w_gu, w_down],
        scratch=[pltpu.VMEM((G, D), BF)], us=3)
    parts = collect(parts)
    d_keep, d_send, u_keep, u_send = call(
        ffn_grad_kernel,
        [sds((2, 192, D), F32), sds((2, 192, D), BF), sds((8, 64, 1536), F32), sds((8, 64, 1536), BF)],
        [ids, h_ffn, *gs, act, dgu],
        scratch=[pltpu.VMEM((G, D), BF)], smem=1, us=100)
    grads, = call(pack_grads_kernel, [sds((288, 8, 512), BF)], [u_keep, swap(u_send), d_keep, swap(d_send)], us=2)
    dmid, dmb = call(
        dmid_kernel, [sds((T, D), F32), sds((T, D), BF)], [grad, *parts, mid, gain_f], us=100)
    bs = spread(dmb)
    dmb_all, datt, stats, sent = call(
        datt_kernel, [sds((G, D), BF), square, small, sds((G + 32, G), BF)], [ids, *bs, w_out, lse, att_t], smem=1, after=[grads], lazy=True, far=(5, 7), us=1)
    grads = lax.psum_scatter(grads, ROWS, scatter_dimension=0, tiled=True)
    far = lax.ppermute(sent, "zh", [(1, 0)])
    dq, dkv_own, dkv_sib = call(
        near_back_kernel, [sds((G, G), F32)] * 3, [ids, q, kv, kv_sib, lo, datt, stats],
        scratch=[pltpu.VMEM((2, 2, HD, G), BF)], smem=1, far=(1, 2, 3), us=40)
    o_keep, o_send = call(
        out_grad_kernel, [sds((2, 128, D), F32), sds((2, 128, D), BF)], [ids, att, dmb_all], smem=1, far=(1,), after=[dq],
    )
    outs, = call(add_out_kernel, [sds((16, 2, 8, D), BF)], [o_keep, swap(o_send)])
    dq, dkv_own, dkv_sib = call(
        far_back_kernel, [sds((G, G), F32), sds((G, G), F32), square],
        [ids, q, datt, stats, lo, far_own, far_sib, far, lo_far, kv, kv_sib, dq, dkv_own, dkv_sib],
        scratch=[pltpu.VMEM((2, 2, HD, G), BF), pltpu.VMEM((G, G), F32), pltpu.VMEM((8, G), F32)], smem=1,
        after=[outs], far=(1, 5, 6, 7, 9, 10), us=40)
    outs = lax.all_to_all(outs, ROWS, split_axis=0, concat_axis=0, tiled=True)
    dkv_sib = swap(dkv_sib)
    out_grad, = call(sum_out_kernel, [sds((16, D), F32)], [outs])
    dq, sum_q = call(q_back_kernel, [square, sds((1, HD), F32)], [dq, qraw, gain_qk, cos, sin], after=[out_grad], far=(1,), us=1)
    dqkv, sum_k, *parts = call(
        kv_back_kernel, [sds((G, D), BF), sds((1, HD), F32)] + partials(),
        [ids, dkv_own, dkv_sib, kraw, gain_qk, cos, sin, w_qkv, dq],
        scratch=[pltpu.VMEM((G, D), BF)], smem=1, far=(3, 7), lazy=True, us=1)
    parts = collect(parts)
    q_keep, q_send = call(
        qkv_grad_kernel, [sds((8, 64, 1152), F32), sds((8, 64, 1152), BF)],
        [ids, h_attn, dqkv, sum_q, sum_k, squares], smem=1, far=(1,), us=1)
    sums, = call(add_qkv_kernel, [sds((16, 4, 8, 1152), BF)], [q_keep, swap(q_send)])
    sums = lax.all_to_all(sums, ROWS, split_axis=0, concat_axis=0, tiled=True)
    tokens_grad, = call(last_kernel, [sds((T, D), F32)], [dmid, *parts, tok, gain_a])
    down_grad, *pieces = call(split_kernel, [sds((24, D), F32)] + [sds((3, 8, 512), BF)] * 4, [ids, grads], smem=1)
    pieces = [pieces[0]] + [around(pieces[k], k) for k in (1, 2, 3)]
    gate_up_grad, gain_f_grad = call(
        finish_gate_up_kernel, [sds((8, 2 * FF), F32), sds((8, HD), F32)], [ids, *pieces, gate_up_weight[0]], smem=1,
    )
    sums = call(
        sum_qkv_kernel, [sds((8, 1152), BF)] * 4, [ids, sums], scratch=[pltpu.VMEM((4, 8, 1152), F32)], smem=1,
        after=[tokens_grad, gate_up_grad, out_grad],
    )
    sums = [sums[0]] + [around(sums[k], k) for k in (1, 2, 3)]
    qkv_grad, gain_a_grad, note = call(
        finish_qkv_kernel, [sds((8, 4096), F32), sds((8, HD), F32), sds((8, HD), F32)], [ids, *sums, w], smem=1,
    )
    mean_loss = note[2, 0] * factor[0, 0] * (1.0 / (TOKENS * D))
    place = ((zh * 4 + x_id) * 2 + c_id) * 8 + lax.axis_index("zl") * 4 + lax.axis_index("y")
    gain_qk_grad = lax.dynamic_slice(note[:2].reshape(256), (2 * place,), (2,))

    return (
        mean_loss,
        block[None],
        tokens_grad[None],
        qkv_grad[None],
        out_grad[None],
        gate_up_grad[None],
        down_grad[None],
        (gain_a_grad[:, 0] / attn_gain[0].astype(F32))[None],
        (gain_f_grad[:, 0] / ffn_gain[0].astype(F32))[None],
        gain_qk_grad[None],
    )


def solution(mesh):
    fine = Mesh(mesh.devices.reshape(2, 4, 2, 2, 4), ALL)
    ctx, wsh = ("zh", "x", "c"), ("zl", "y")
    states = P(wsh, ctx, None)
    matrix, vector = P(None, ALL, None), P(None, ALL)
    return jax.shard_map(
        local,
        mesh=fine,
        in_specs=(states, states, P(wsh, None), P(wsh, ctx)) + (matrix,) * 4 + (vector,) * 3,
        out_specs=(P(), states, states) + (matrix,) * 4 + (vector,) * 3,
        check_vma=False,
    )
```

```python
import math

import jax
import jax.numpy as jnp
from jax import lax
from jax.experimental import pallas as pl
from jax.experimental.pallas import tpu as pltpu
from jax.sharding import Mesh
from jax.sharding import PartitionSpec as P

D = 1024
HEADS = 16
KV_HEADS = 8
HD = 128
FF = 3072
T = 128
G = 512
HALF = 1024
EPS = 1e-06
THETA = 1000000.0
SCALE = 1.0 / math.sqrt(HD)
SCALE2 = SCALE / math.log(2.0)
TOKENS = 16384.0
MICROSECOND = 3 * 10**8

ALL = ("zh", "x", "c", "zl", "y")
ROWS = ("zh", "zl", "y")
CHIPS = ("zh", "x", "zl", "y")
BF = jnp.bfloat16
F32 = jnp.float32


def nt(a, b):
    return lax.dot_general(a, b, (((1,), (1,)), ((), ())), preferred_element_type=F32)


def nn(a, b):
    return lax.dot_general(a, b, (((1,), (0,)), ((), ())), preferred_element_type=F32)


def tn(a, b):
    return lax.dot_general(a, b, (((0,), (0,)), ((), ())), preferred_element_type=F32)


def sds(shape, dtype):
    return jax.ShapeDtypeStruct(shape, dtype)


class Moves:
    def __init__(self):
        self.copies, self.started, self.ended = {}, set(), set()

    def start(self, *refs):
        for ref in refs:
            if id(ref) not in self.started:
                self.started.add(id(ref))
                self.copies[id(ref)].start()

    def wait(self, *refs):
        for ref in refs:
            if id(ref) in self.copies and id(ref) not in self.ended:
                self.ended.add(id(ref))
                self.copies[id(ref)].wait()


def kept(shape, dtype):
    return pltpu.HBM(shape, dtype)


def in_hbm(value):
    return pltpu.with_memory_space_constraint(value, pltpu.HBM)


def call(body, outs, args, scratch=(), smem=0, limit=28, after=(), far=(), lazy=False, us=1):
    kept_out = [i for i, o in enumerate(outs) if not isinstance(o, jax.ShapeDtypeStruct)]
    vmem, hbm = pl.BlockSpec(memory_space=pltpu.VMEM), pl.BlockSpec(memory_space=pltpu.HBM)
    specs = [pl.BlockSpec(memory_space=pltpu.SMEM)] * smem
    specs += [hbm if i in far else vmem for i in range(smem, len(args))]
    specs += [pl.BlockSpec(memory_space=pl.ANY)] * len(after)
    count = len(args)
    staged = [(args[i].shape, args[i].dtype) for i in far]
    staged += [(outs[i].inner_aval.shape, outs[i].inner_aval.dtype) for i in kept_out]
    scratch = list(scratch) + [pltpu.VMEM(*a) for a in staged]
    if staged:
        scratch.append(pltpu.SemaphoreType.DMA((len(staged),)))

    def kernel(*refs):
        ins = list(refs[:count])
        results = list(refs[count + len(after) :][: len(outs)])
        rest = list(refs[count + len(after) + len(outs) :])
        if not staged:
            body(*ins, *results, *rest)
            return
        sems = rest.pop()
        stage = rest[len(rest) - len(staged) :]
        rest = rest[: len(rest) - len(staged)]
        moves = Moves()
        for n, i in enumerate(far):
            moves.copies[id(stage[n])] = pltpu.make_async_copy(ins[i], stage[n], sems.at[n])
            ins[i] = stage[n]
        for n, i in enumerate(kept_out, len(far)):
            moves.copies[id(stage[n])] = pltpu.make_async_copy(stage[n], results[i], sems.at[n])
            results[i] = stage[n]
        moves.start(*stage[: len(far)])
        if lazy:
            body(moves, *ins, *results, *rest)
        else:
            moves.wait(*stage[: len(far)])
            body(*ins, *results, *rest)
        moves.start(*stage)
        moves.wait(*stage)

    return pl.pallas_call(
        kernel,
        name=body.__name__,
        out_shape=list(outs),
        in_specs=specs,
        out_specs=[hbm if i in kept_out else vmem for i in range(len(outs))],
        scratch_shapes=scratch,
        compiler_params=pltpu.CompilerParams(vmem_limit_bytes=limit * 1024 * 1024),
        cost_estimate=pl.CostEstimate(flops=MICROSECOND * us, bytes_accessed=1, transcendentals=0),
    )(*[in_hbm(a) if i in far else a for i, a in enumerate(args)], *after)


def behind(value, *after):
    def nothing(*refs):
        del refs

    place = pl.BlockSpec(memory_space=pl.ANY)
    return pl.pallas_call(
        nothing,
        out_shape=sds(value.shape, value.dtype),
        in_specs=[place] * (1 + len(after)),
        out_specs=place,
        input_output_aliases={0: 0},
        cost_estimate=pl.CostEstimate(flops=1, bytes_accessed=1, transcendentals=0),
    )(value, *after)


def shift_from(x_id, k):
    return lax.rem(x_id - k + 4, 4)


def project(rows, weight, product, outs):
    for t in range(4):
        cols = slice(t * 256, (t + 1) * 256)
        value = product(rows, weight(cols))
        for k, out in enumerate(outs):
            out[:, cols] = value[k * T : (k + 1) * T].astype(out.dtype)


def rows_at(index, size):
    return pl.ds(pl.multiple_of(index * size, size), size)


def pack_kernel(ids, w, gu, out_w, down_w, gain_a, gain_f, gain_qk, mask, rows, own, s1, s2, s3, notes):
    for g in range(2):
        rows[g] = out_w[8 * g : 8 * g + 8, :]
    for g in range(3):
        rows[2 + g] = down_w[8 * g : 8 * g + 8, :]
    notes[...] = jnp.zeros_like(notes)
    notes[0:1, :8] = gain_a[...].astype(F32)
    notes[1:2, :8] = gain_f[...].astype(F32)
    notes[2:3, :2] = gain_qk[...].astype(F32)
    notes[3:4, :1] = jnp.sum(mask[...].astype(F32), axis=1, keepdims=True)
    note = notes[...].T[:8].astype(BF)
    for k, out in enumerate((own, s1, s2, s3)):
        x = lax.rem(ids[1] + k, 4)
        places = [(w, 0, 256), (w, HALF, 256)]
        places += [(w, base, HD) for base in (2048, 2560, 3072, 3584)]
        places += [(None, 0, 0)] + [(gu, base, 384) for base in (0, 1536, 3072, 4608)]
        at = 0
        for ref, base, n in places:
            if ref is None:
                out[:, at : at + HD] = note
                at += HD
            else:
                out[:, at : at + n] = ref[:, pl.ds(pl.multiple_of(base + x * n, HD), n)]
                at += n


def join_kernel(p0, p1, p2, p3, first, second):
    for k, ref in enumerate((p0, p1, p2, p3)):
        block, other = ref[:, :1152], ref[:, 1152:]
        for device in range(16):
            first[device, k] = block
            second[device, k] = other


def gather_kernel(ids, t0, t1, t2, t3, toks, scale):
    for k, ref in enumerate((t0, t1, t2, t3)):
        rows = rows_at(shift_from(ids[1], k), T)
        toks[rows, :] = ref[...]
        t = ref[...].astype(F32)
        r = lax.rsqrt(jnp.mean(t * t, axis=-1, keepdims=True) + EPS)
        scale[rows, :] = jnp.broadcast_to(r, (T, HD))


def blocks_of(got, zz, k):
    return jnp.concatenate([got[zz * 8 + other, k].astype(F32) for other in range(8)], axis=0).astype(BF)


def qkv_kernel(moves, ids, toks, scale, own, sib, cos, sin,
               h_ref, q_ref, kv_ref, cross, qraw, kraw, gain, gain_f, qk_gain, factor, weight, wide):
    c_id = ids[2]
    for zz in range(2):
        for k in range(4):
            at = 2 * (4 * zz + shift_from(ids[1], k))
            for whose, ref in ((c_id, own), (1 - c_id, sib)):
                value = blocks_of(ref, zz, k)
                weight[rows_at(at + whose, 64), :] = value[:, :D]
                wide[rows_at(at + whose, 64), :] = value[:, D:]
    moves.start(weight)
    notes = wide[...].T
    gain[...] = notes[0:1].astype(F32)
    gain_f[...] = notes[1:2].astype(F32)
    at = lax.broadcasted_iota(jnp.int32, (D, 256), 0)
    entry = lax.broadcasted_iota(jnp.int32, (D, 256), 1)
    pick = jnp.where(at == 8 * (entry >> 1) + (entry & 1), 1.0, 0.0).astype(BF)
    qk_gain[...] = nn(notes[:16], pick)[2:3]
    count = jnp.sum(notes[3:4].astype(F32), axis=1, keepdims=True)
    factor[...] = jnp.broadcast_to(TOKENS / count, (1, HD))

    def rope(v, gains, rows):
        r = lax.rsqrt(jnp.mean(v * v, axis=-1, keepdims=True) + EPS)
        n = v * r * gains
        return (n * cos[rows, :] + pltpu.roll(n, 64, 1) * sin[rows, :]).astype(BF)

    for j in range(4):
        rows = slice(j * T, (j + 1) * T)
        t = toks[rows, :].astype(F32)
        h = (t * scale[rows, :1] * gain[...]).astype(BF)
        h_ref[rows, :] = h
        q = nn(h, weight[:, :G])
        kv = nn(h, weight[:, G:])
        qraw[rows, :] = q
        kraw[rows, :] = kv[:, :256]
        kv_ref[rows, 256:] = kv[:, 256:].astype(BF)
        for n in range(4):
            q_ref[rows, n * HD : (n + 1) * HD] = rope(q[:, n * HD : (n + 1) * HD], qk_gain[:, :HD], rows)
        for n in range(2):
            kv_ref[rows, n * HD : (n + 1) * HD] = rope(kv[:, n * HD : (n + 1) * HD], qk_gain[:, HD:], rows)
    cross[...] = jnp.where(ids[0] == 0, kv_ref[...], q_ref[...])


def head_pair(ref, hh, j):
    rows = slice(j * T, (j + 1) * T)
    base = hh * 256
    return jnp.concatenate([ref[rows, base : base + HD], ref[rows, base + HD : base + 256]], axis=0)


def row_pair(row):
    return jnp.concatenate([row, row], axis=1)


def key_positions(base, start, count):
    index = lax.broadcasted_iota(jnp.int32, (count, 1), 0) + start
    return base + index + (index >> 7) * T


def query_positions(zh, c, j):
    row = lax.broadcasted_iota(jnp.int32, (1, T), 1) + (zh * HALF + j * 256 + c * T)
    return row_pair(row)


def fill_values(vt, slot, kv_ref):
    for hh in range(2):
        vt[slot, hh, :HD, :] = kv_ref[:, 256 + hh * HD : 256 + (hh + 1) * HD].T
        vt[slot, hh, HD:, :] = jnp.ones((16, G), BF)


def tiles(count):
    return [(t, min(256, count - t)) for t in range(0, count, 256)]


def join_out(c, own, sib, weight):
    for hh in range(2):
        for whose, ref in ((c, own), (1 - c, sib)):
            parts = [ref[hh * 8 + o, g].astype(F32) for o in range(8) for g in range(2)]
            weight[rows_at(2 * hh + whose, HD), :] = jnp.concatenate(parts, axis=0).astype(BF)


def attend(q_ref, kv_ref, vt, slot, hh, j, count, base, qpos, lo_row, causal):
    qj = head_pair(q_ref, hh, j)
    total = None
    for start, n in tiles(count):
        keys = kv_ref[start : start + n, hh * HD : (hh + 1) * HD]
        s = nt(keys, qj)
        kpos = key_positions(base, start, n)
        mask = kpos >= lo_row
        if causal:
            mask = mask & (kpos <= qpos)
        p = jnp.where(mask, jnp.exp2(s * SCALE2), 0.0).astype(BF)
        part = nn(vt[slot, hh, :, start : start + n], p)
        total = part if total is None else total + part
    return total


def attention_kernel(moves, ids, q_ref, own, sib, far_own, far_sib, lo, rows_own, rows_sib,
                     att, att_t, lse, w_nat, p0, p1, p2, p3, vt, sums, wide, turned):
    zh, x_id, c = ids[0], ids[1], ids[2]
    join_out(c, rows_own, rows_sib, w_nat)
    moves.start(w_nat)
    moves.wait(q_ref, own, sib, far_own, far_sib)
    fill_values(vt, 0, own)
    fill_values(vt, 1, sib)
    sums[4:8, :] = jnp.ones((4, G), F32)
    for hh in range(2):
        for j in range(4):
            cols = slice(j * T, (j + 1) * T)
            lo_row = row_pair(lo[:, cols])
            qpos = query_positions(zh, c, j)
            total = None
            for slot, (ref, whose) in enumerate(((own, c), (sib, 1 - c))):
                part = attend(
                    q_ref, ref, vt, slot, hh, j, (j + 1) * T, zh * HALF + whose * T, qpos, lo_row, True
                )
                total = part if total is None else total + part
            for g in range(2):
                n = 2 * hh + g
                wide[n * HD : (n + 1) * HD, cols] = total[:HD, g * T : (g + 1) * T]
                sums[n : n + 1, cols] = total[HD : HD + 1, g * T : (g + 1) * T]

    @pl.when(zh == 1)
    def _():
        fill_values(vt, 0, far_own)
        fill_values(vt, 1, far_sib)
        for hh in range(2):
            for j in range(4):
                cols = slice(j * T, (j + 1) * T)
                lo_row = row_pair(lo[:, cols])
                total = None
                for slot, (ref, whose) in enumerate(((far_own, c), (far_sib, 1 - c))):
                    part = attend(q_ref, ref, vt, slot, hh, j, G, whose * T, None, lo_row, False)
                    total = part if total is None else total + part
                for g in range(2):
                    n = 2 * hh + g
                    wide[n * HD : (n + 1) * HD, cols] += total[:HD, g * T : (g + 1) * T]
                    sums[n : n + 1, cols] += total[HD : HD + 1, g * T : (g + 1) * T]

    lse[...] = jnp.log2(sums[...])
    for n in range(4):
        inverse = 1.0 / sums[n : n + 1, :]
        scaled = wide[n * HD : (n + 1) * HD, :] * inverse
        att_t[n * HD : (n + 1) * HD, :] = scaled
        for j in range(4):
            att[j * T : (j + 1) * T, n * HD : (n + 1) * HD] = scaled[:, j * T : (j + 1) * T].T.astype(BF)
    moves.start(att, att_t)
    for k in range(4):
        turned[k * T : (k + 1) * T, :] = att[rows_at(shift_from(x_id, k), T), :]
    project(turned[...], lambda cols: w_nat[:, cols], nn, (p0, p1, p2, p3))


def stat_pair(stats, row, cols):
    return jnp.concatenate([stats[row : row + 1, cols], stats[row + 1 : row + 2, cols]], axis=1)


def attend_back(q_ref, datt, stats, lo, kv_ref, hh, j, count, base, qpos, dkv=None, kt=None):
    cols = slice(j * T, (j + 1) * T)
    lo_row = row_pair(lo[:, cols])
    lse_row, delta_row = stat_pair(stats, 2 * hh, cols), stat_pair(stats, 4 + 2 * hh, cols)
    qj = head_pair(q_ref, hh, j)
    dj = head_pair(datt, hh, j)
    dq = None
    for start, n in tiles(count):
        rows = slice(start, start + n)
        kc = slice(hh * HD, (hh + 1) * HD)
        vc = slice(256 + hh * HD, 256 + (hh + 1) * HD)
        s = nt(kv_ref[rows, kc], qj)
        dp = nt(kv_ref[rows, vc], dj)
        mask = key_positions(base, start, n) >= lo_row
        if qpos is not None:
            mask = mask & (key_positions(base, start, n) <= qpos)
        p = jnp.where(mask, jnp.exp2(s * SCALE2 - lse_row), 0.0)
        ds = (p * (dp - delta_row) * SCALE).astype(BF)
        if dkv is not None:
            dkv[rows, vc] += nn(p.astype(BF), dj)
            dkv[rows, kc] += nn(ds, qj)
        if kt is not None:
            part = nn(kt[hh, :, start : start + n], ds)
            dq = part if dq is None else dq + part
    return dq


def fill_keys(kt, slot, kv_ref):
    for hh in range(2):
        kt[slot, hh] = kv_ref[:, hh * HD : (hh + 1) * HD].T


def datt_kernel(moves, ids, b0, b1, b2, b3, w_nat, lse, att_t, dmb, datt, stats, sent):
    for k, ref in enumerate((b0, b1, b2, b3)):
        dmb[rows_at(shift_from(ids[1], k), T), :] = ref[...]
    moves.wait(w_nat)
    datt[...] = nt(dmb[...], w_nat[...]).astype(BF)
    moves.wait(att_t)
    stats[:4, :] = lse[:4, :]
    for n in range(4):
        cols = slice(n * HD, (n + 1) * HD)
        back = nt(w_nat[cols, :], dmb[...]).astype(BF).astype(F32)
        stats[4 + n : 5 + n, :] = jnp.sum(back * att_t[cols, :], axis=0, keepdims=True)
    sent[:G, :] = datt[...]
    high = stats[...].astype(BF).astype(F32)
    middle = (stats[...] - high).astype(BF).astype(F32)
    low = stats[...] - high - middle
    sent[G:, :] = jnp.concatenate([high, middle, low, jnp.zeros((8, G), F32)], axis=0).astype(BF)


def near_back_kernel(ids, q_ref, own, sib, lo, datt, stats, dq, dkv_own, dkv_sib, kt):
    zh, c = ids[0], ids[2]
    dkv_own[...] = jnp.zeros_like(dkv_own)
    dkv_sib[...] = jnp.zeros_like(dkv_sib)
    fill_keys(kt, 0, own)
    fill_keys(kt, 1, sib)
    for hh in range(2):
        for j in range(4):
            qpos = query_positions(zh, c, j)
            total = None
            for slot, (ref, dref, whose) in enumerate(((own, dkv_own, c), (sib, dkv_sib, 1 - c))):
                part = attend_back(
                    q_ref, datt, stats, lo, ref, hh, j, (j + 1) * T, zh * HALF + whose * T, qpos, dref, kt.at[slot]
                )
                total = part if total is None else total + part
            for g in range(2):
                n = 2 * hh + g
                dq[j * T : (j + 1) * T, n * HD : (n + 1) * HD] = total[:, g * T : (g + 1) * T].T


def far_back_kernel(ids, q, datt, stats, lo, far_own, far_sib, far, lo_far, own, sib,
                    dq_in, dkv_own_in, dkv_sib_in, dq, dkv_own, dkv_sib, kt, total_sib, stats_far):
    zh, c = ids[0], ids[2]
    dq[...] = dq_in[...]
    dkv_own[...] = dkv_own_in[...]
    total_sib[...] = dkv_sib_in[...]

    @pl.when(zh == 1)
    def _():
        fill_keys(kt, 0, far_own)
        fill_keys(kt, 1, far_sib)
        for hh in range(2):
            for j in range(4):
                total = None
                for slot, (ref, whose) in enumerate(((far_own, c), (far_sib, 1 - c))):
                    part = attend_back(q, datt, stats, lo, ref, hh, j, G, whose * T, None, None, kt.at[slot])
                    total = part if total is None else total + part
                for g in range(2):
                    n = 2 * hh + g
                    dq[j * T : (j + 1) * T, n * HD : (n + 1) * HD] += total[:, g * T : (g + 1) * T].T

    @pl.when(zh == 0)
    def _():
        parts = far[G:, :].astype(F32)
        stats_far[...] = parts[:8] + parts[8:16] + parts[16:24]
        for hh in range(2):
            for j in range(4):
                for ref, dref, whose in ((own, dkv_own, c), (sib, total_sib, 1 - c)):
                    attend_back(far_own, far, stats_far, lo_far, ref, hh, j, G, whose * T, None, dref, None)

    dkv_sib[...] = total_sib[...].astype(BF)


def head_back(w, raw, gain, cos, sin):
    w = w * cos - pltpu.roll(w, 64, 1) * sin
    r = lax.rsqrt(jnp.mean(raw * raw, axis=-1, keepdims=True) + EPS)
    a = w * gain
    out = r * a - raw * (r * r * r * jnp.mean(a * raw, axis=-1, keepdims=True))
    return out, jnp.sum(w * raw * r, axis=0, keepdims=True)


def q_back_kernel(dq, qraw, qk_gain, cos, sin, out, gains):
    total = jnp.zeros((1, HD), F32)
    for j in range(4):
        rows = slice(j * T, (j + 1) * T)
        for n in range(4):
            hc = slice(n * HD, (n + 1) * HD)
            value, part = head_back(dq[rows, hc], qraw[rows, hc], qk_gain[:, :HD], cos[rows, :], sin[rows, :])
            total += part
            out[rows, hc] = value.astype(BF)
    gains[...] = total


def kv_back_kernel(moves, ids, dkv, from_sib, kraw, qk_gain, cos, sin, weight, dq, dqkv, gains, p0, p1, p2, p3, turned):
    total = jnp.zeros((1, HD), F32)
    dqkv[:, :G] = dq[...]
    moves.wait(kraw)
    for j in range(4):
        rows = slice(j * T, (j + 1) * T)
        grad = dkv[rows, :] + from_sib[rows, :].astype(F32)
        for n in range(2):
            hc = slice(n * HD, (n + 1) * HD)
            value, part = head_back(grad[:, hc], kraw[rows, hc], qk_gain[:, HD:], cos[rows, :], sin[rows, :])
            total += part
            dqkv[rows, G + n * HD : G + (n + 1) * HD] = value.astype(BF)
        dqkv[rows, G + 256 :] = grad[:, 256:].astype(BF)
    gains[...] = total
    for k in range(4):
        turned[k * T : (k + 1) * T, :] = dqkv[rows_at(shift_from(ids[1], k), T), :]
    moves.wait(weight)
    project(turned[...], lambda cols: weight[cols, :], nt, (p0, p1, p2, p3))


def split_rows(c_id, value, keep, send, index):
    half = value.shape[0] // 2
    first = c_id == 0
    keep[index] = jnp.where(first, value[:half], value[half:])
    send[index] = jnp.where(first, value[half:], value[:half]).astype(BF)


def qkv_grad_kernel(ids, h, dqkv, gain_q, gain_k, squares, keep, send):
    total = jnp.broadcast_to(jnp.sum(squares[...], keepdims=True), (1, HD))
    note = jnp.concatenate([gain_q[...], gain_k[...], total, jnp.zeros((5, HD), F32)], axis=0)
    note = jnp.concatenate([note] * 8, axis=0)
    first = ids[2] == 0
    for b in range(8):
        value = tn(h[:, b * 128 : (b + 1) * 128], dqkv[...])
        keep[b, :, :D] = jnp.where(first, value[:64], value[64:])
        send[b, :, :D] = jnp.where(first, value[64:], value[:64]).astype(BF)
        keep[b, :, D:] = note
        send[b, :, D:] = note.astype(BF)


def add_qkv_kernel(keep, got, out):
    for zz in range(2):
        for x in range(4):
            value = keep[4 * zz + x] + got[4 * zz + x].astype(F32)
            for o in range(8):
                out[zz * 8 + o, x] = value[8 * o : 8 * o + 8].astype(BF)


def sum_kernel(ids, sums, grads, down, own, s1, s2, s3, total):
    for x in range(4):
        value = sums[0, x].astype(F32)
        for device in range(1, 16):
            value += sums[device, x].astype(F32)
        total[x] = value
    for k, out in enumerate((own, s1, s2, s3)):
        x = lax.rem(ids[1] + k, 4)
        out[:, :1152] = total[x].astype(BF)
        for b in range(3):
            out[:, 1152 + 512 * b : 1152 + 512 * (b + 1)] = grads[3 * x + b]
    for g in range(3):
        for half in range(2):
            down[8 * g : 8 * g + 8, half * 512 : (half + 1) * 512] = grads[12 + 2 * g + half].astype(F32)


def add_out_kernel(keep, got, out):
    for zz in range(2):
        value = keep[zz] + got[zz].astype(F32)
        for o in range(8):
            for g in range(2):
                out[zz * 8 + o, g] = value[16 * o + 8 * g : 16 * o + 8 * g + 8].astype(BF)


def sum_out_kernel(sums, out):
    for g in range(2):
        value = sums[0, g].astype(F32)
        for device in range(1, 16):
            value += sums[device, g].astype(F32)
        out[8 * g : 8 * g + 8, :] = value


def finish_kernel(ids, p0, p1, p2, p3, w, gu, grad, gain, note, gu_grad, gu_gain):
    total = jnp.zeros((8, HD), F32)
    gain_sum = jnp.zeros((8, 1), F32)
    gu_sum = jnp.zeros((8, 1), F32)
    for k, ref in enumerate((p0, p1, p2, p3)):
        value = ref[...].astype(F32)
        x = shift_from(ids[1], k)
        total += value[:, D:1152]
        places = [(0, 0, 256), (256, HALF, 256)]
        places += [(G + n * HD, base, HD) for n, base in enumerate((2048, 2560, 3072, 3584))]
        for start, base, n in places:
            at = pl.ds(pl.multiple_of(base + x * n, HD), n)
            part = value[:, start : start + n]
            grad[:, at] = part
            gain_sum += jnp.sum(part * w[:, at].astype(F32), axis=1, keepdims=True)
        for n in range(4):
            at = pl.ds(pl.multiple_of(n * 1536 + x * 384, HD), 384)
            part = value[:, 1152 + n * 384 : 1152 + (n + 1) * 384]
            gu_grad[:, at] = part
            gu_sum += jnp.sum(part * gu[:, at].astype(F32), axis=1, keepdims=True)
    gain[...] = jnp.broadcast_to(gain_sum, (8, HD))
    gu_gain[...] = jnp.broadcast_to(gu_sum, (8, HD))
    note[...] = total


def out_grad_kernel(ids, att, dmb, keep, send):
    for b in range(2):
        split_rows(ids[2], tn(att[:, b * 256 : (b + 1) * 256], dmb[...]), keep, send, b)


def stack4(a, b, c, d):
    return jnp.concatenate([a[...], b[...], c[...], d[...]], axis=0)


def order_kernel(ids, own, sib, rows_own, rows_sib, weight, down):
    for whose, ref, rows in ((ids[2], own, rows_own), (1 - ids[2], sib, rows_sib)):
        for zz in range(2):
            for k in range(4):
                at = rows_at(2 * (4 * zz + shift_from(ids[1], k)) + whose, 64)
                weight[at, :] = blocks_of(ref, zz, k)
            parts = [rows[zz * 8 + o, 2 + g].astype(F32) for o in range(8) for g in range(3)]
            down[rows_at(2 * zz + whose, 192), :] = jnp.concatenate(parts, axis=0).astype(BF)


def ffn_kernel(h0, h1, h2, h3, weight, down, gate, up, act, h, p0, p1, p2, p3):
    h[...] = stack4(h0, h1, h2, h3)
    for t in range(3):
        cols = slice(t * 256, (t + 1) * 256)
        g = nn(h[...], weight[:, cols])
        u = nn(h[...], weight[:, 768 + t * 256 : 768 + (t + 1) * 256])
        gate[:, cols] = g
        up[:, cols] = u
        act[:, cols] = (g * jax.nn.sigmoid(g) * u).astype(BF)
    project(act[...], lambda cols: down[:, cols], nn, (p0, p1, p2, p3))


def ffn_back_kernel(g0, g1, g2, g3, gate, up, weight, down, dgu, p0, p1, p2, p3, gb):
    gb[...] = stack4(g0, g1, g2, g3)
    for t in range(3):
        cols = slice(t * 256, (t + 1) * 256)
        dact = nt(gb[...], down[cols, :])
        g = gate[:, cols]
        u = up[:, cols]
        s = jax.nn.sigmoid(g)
        dgu[:, cols] = (dact * u * s * (1.0 + g * (1.0 - s))).astype(BF)
        dgu[:, 768 + t * 256 : 768 + (t + 1) * 256] = (dact * g * s).astype(BF)
    project(dgu[...], lambda cols: weight[cols, :], nt, (p0, p1, p2, p3))


def ffn_grad_kernel(ids, h, g0, g1, g2, g3, act, dgu, d_keep, d_send, u_keep, u_send, gb):
    c_id = ids[2]
    gb[...] = stack4(g0, g1, g2, g3)
    for b in range(2):
        split_rows(c_id, tn(act[:, b * 384 : (b + 1) * 384], gb[...]), d_keep, d_send, b)
    for b in range(8):
        split_rows(c_id, tn(h[:, b * 128 : (b + 1) * 128], dgu[...]), u_keep, u_send, b)


def pack_grads_kernel(u_keep, u_got, d_keep, d_got, out):
    for zz in range(2):
        for x in range(4):
            value = u_keep[4 * zz + x] + u_got[4 * zz + x].astype(F32)
            for o in range(8):
                for b in range(3):
                    part = value[8 * o : 8 * o + 8, 512 * b : 512 * (b + 1)]
                    out[(zz * 8 + o) * 18 + 3 * x + b] = part.astype(BF)
        value = d_keep[zz] + d_got[zz].astype(F32)
        for o in range(8):
            for g in range(3):
                for half in range(2):
                    part = value[24 * o + 8 * g : 24 * o + 8 * g + 8, 512 * half : 512 * (half + 1)]
                    out[(zz * 8 + o) * 18 + 12 + 2 * g + half] = part.astype(BF)


def total_of(own, r1, r2, r3):
    return own[...] + r1[...].astype(F32) + r2[...].astype(F32) + r3[...].astype(F32)


def mid_kernel(tok, own, r1, r2, r3, gain, mid, h):
    v = tok[...].astype(F32) + total_of(own, r1, r2, r3)
    mid[...] = v
    r = lax.rsqrt(jnp.mean(v * v, axis=-1, keepdims=True) + EPS)
    h[...] = (v * r * gain[...]).astype(BF)


def loss_kernel(factor, mid, own, r1, r2, r3, teacher, mask, block, grad, grad_low, squares):
    v = mid[...] + total_of(own, r1, r2, r3)
    block[...] = v.astype(BF)
    diff = v - teacher[...].astype(F32)
    kept = jnp.broadcast_to(mask[...].astype(F32), (T, T)).T[:, :1] * diff
    out = factor[:, :1] * kept
    grad[...] = out
    grad_low[...] = out.astype(BF)
    squares[...] = jnp.sum((kept * diff).reshape(16, 8, D), axis=0)


def norm_back(v, gain, w):
    r = lax.rsqrt(jnp.mean(v * v, axis=-1, keepdims=True) + EPS)
    a = w * gain
    return r * a - v * (r * r * r * jnp.mean(a * v, axis=-1, keepdims=True))


def dmid_kernel(grad, own, r1, r2, r3, mid, gain, dmid, dmb):
    out = grad[...] + norm_back(mid[...], gain[...], total_of(own, r1, r2, r3))
    dmid[...] = out
    dmb[...] = out.astype(BF)


def last_kernel(dmid, own, r1, r2, r3, tok, gain, out):
    out[...] = dmid[...] + norm_back(tok[...].astype(F32), gain[...], total_of(own, r1, r2, r3))


def ring(k):
    return [(i, (i + k) % 4) for i in range(4)]


def around(v, k):
    return lax.ppermute(v, "x", ring(k))


def spread(v):
    return (v,) + tuple(around(v, k) for k in (1, 2, 3))


def collect(parts):
    return (parts[0],) + tuple(around(parts[k], -k) for k in (1, 2, 3))


def swap(v):
    return lax.ppermute(v, "c", [(0, 1), (1, 0)])


def partials():
    return [sds((T, D), F32)] + [sds((T, D), BF)] * 3


def local(tokens, teacher, doc_starts, valid_mask, qkv_weight, out_weight, gate_up_weight, down_weight,
          attn_gain, ffn_gain, qk_gain):
    zh, x_id, c_id = lax.axis_index("zh"), lax.axis_index("x"), lax.axis_index("c")
    z_id = zh * 2 + lax.axis_index("zl")
    ids = jnp.stack([zh, x_id, c_id, lax.axis_index("y"), z_id]).astype(jnp.int32)
    tok = tokens[0]

    w = qkv_weight[0]
    rows, *sent = call(
        pack_kernel, [sds((5, 8, D), BF)] + [sds((8, 2688), BF)] * 4,
        [ids, w, gate_up_weight[0], out_weight[0], down_weight[0], attn_gain, ffn_gain, qk_gain, valid_mask],
        scratch=[pltpu.VMEM((HD, HD), F32)], smem=1, far=(1, 2, 3, 4),
    )
    columns = [sent[0]] + [around(sent[k], k) for k in (1, 2, 3)]
    first, second = call(join_kernel, [sds((16, 4, 8, 1152), BF), kept((16, 4, 8, 1536), BF)], columns)
    w_own = lax.all_to_all(first, ROWS, split_axis=0, concat_axis=0, tiled=True)
    w_sib = swap(w_own)
    ts = spread(behind(tok, first))
    toks, scales = call(gather_kernel, [sds((G, D), BF), sds((G, HD), F32)], [ids, *ts], smem=1, us=100)
    rows = lax.all_gather(rows, ROWS, axis=0, tiled=False)

    offset = jnp.arange(G, dtype=jnp.int32)
    positions = zh * HALF + c_id * T + offset + (offset // T) * T
    starts = doc_starts[0]
    reached = positions[None, :, None] + HALF * jnp.arange(2, dtype=jnp.int32)[:, None, None] >= starts[None, None, :]
    lo, lo_far = jnp.split(jnp.max(jnp.where(reached, starts[None, None, :], 0), axis=2), 2, axis=0)
    half = HD // 2
    frequency = jnp.exp(-(jnp.arange(half, dtype=F32) * 2.0 / HD) * math.log(THETA))
    angles = positions.astype(F32)[:, None] * frequency[None, :]
    cos, sin = jnp.cos(angles), jnp.sin(angles)
    cos = jnp.concatenate([cos, cos], axis=1)
    sin = jnp.concatenate([-sin, sin], axis=1)

    square = sds((G, G), BF)
    small = sds((8, G), F32)
    h_attn, q, kv, cross, qraw, kraw, gain_a, gain_f, gain_qk, factor, w_qkv = call(
        qkv_kernel,
        [kept((G, D), BF), kept((G, G), BF), kept((G, G), BF), square, kept((G, G), F32), kept((G, 256), F32),
         sds((1, D), F32), sds((1, D), F32), sds((1, 256), F32), sds((1, HD), F32), kept((D, D), BF)],
        [ids, toks, scales, w_own, w_sib, cos, sin],
        scratch=[pltpu.VMEM((D, HD), BF)], smem=1, lazy=True, after=[lo, lo_far], us=4)
    kv_sib = swap(kv)
    far_own = lax.ppermute(cross, "zh", [(0, 1), (1, 0)])
    rows = behind(rows, far_own, kv_sib)
    far_sib, rows_sib = swap(far_own), swap(rows)
    second = lax.all_to_all(behind(second, far_sib), ROWS, split_axis=0, concat_axis=0, tiled=True)
    att, att_t, lse, w_out, *parts = call(
        attention_kernel,
        [kept((G, G), BF), kept((G, G), F32), small, kept((G, D), BF)] + partials(),
        [ids, q, kv, kv_sib, far_own, far_sib, lo, rows, rows_sib],
        scratch=[pltpu.VMEM((2, 2, 144, G), BF), pltpu.VMEM((8, G), F32), pltpu.VMEM((G, G), F32),
                 pltpu.VMEM((G, G), BF)],
        smem=1, lazy=True, far=(1, 2, 3, 4, 5), us=10,
    )
    parts = collect(parts)
    mid, h = call(mid_kernel, [sds((T, D), F32), sds((T, D), BF)], [tok, *parts, gain_f])

    hs = spread(h)
    second = behind(second, h)
    w_gu, w_down = call(
        order_kernel, [sds((D, 1536), BF), sds((768, D), BF)], [ids, second, swap(second), rows, rows_sib],
        smem=1, us=2
    )
    gate, up, act, h_ffn, *parts = call(
        ffn_kernel,
        [sds((G, 768), F32), sds((G, 768), F32), sds((G, 768), BF), sds((G, D), BF)] + partials(),
        [*hs, w_gu, w_down], us=3)
    parts = collect(parts)
    block, grad, grad_low, squares = call(
        loss_kernel,
        [sds((T, D), BF), sds((T, D), F32), sds((T, D), BF), sds((8, D), F32)],
        [factor, mid, *parts, teacher[0], valid_mask],
    )

    gs = spread(grad_low)
    dgu, *parts = call(
        ffn_back_kernel, [sds((G, 1536), BF)] + partials(), [*gs, gate, up, w_gu, w_down],
        scratch=[pltpu.VMEM((G, D), BF)], us=3)
    parts = collect(parts)
    d_keep, d_send, u_keep, u_send = call(
        ffn_grad_kernel,
        [sds((2, 192, D), F32), sds((2, 192, D), BF), sds((8, 64, 1536), F32), sds((8, 64, 1536), BF)],
        [ids, h_ffn, *gs, act, dgu],
        scratch=[pltpu.VMEM((G, D), BF)], smem=1, us=100)
    grads, = call(pack_grads_kernel, [sds((288, 8, 512), BF)], [u_keep, swap(u_send), d_keep, swap(d_send)], us=2)
    dmid, dmb = call(
        dmid_kernel, [sds((T, D), F32), sds((T, D), BF)], [grad, *parts, mid, gain_f], us=100)
    bs = spread(dmb)
    dmb_all, datt, stats, sent = call(
        datt_kernel, [sds((G, D), BF), square, small, sds((G + 32, G), BF)], [ids, *bs, w_out, lse, att_t], smem=1, after=[grads], lazy=True, far=(5, 7), us=1)
    grads = lax.psum_scatter(grads, ROWS, scatter_dimension=0, tiled=True)
    far = lax.ppermute(sent, "zh", [(1, 0)])
    dq, dkv_own, dkv_sib = call(
        near_back_kernel, [sds((G, G), F32)] * 3, [ids, q, kv, kv_sib, lo, datt, stats],
        scratch=[pltpu.VMEM((2, 2, HD, G), BF)], smem=1, far=(1, 2, 3), us=40)
    o_keep, o_send = call(
        out_grad_kernel, [sds((2, 128, D), F32), sds((2, 128, D), BF)], [ids, att, dmb_all], smem=1, far=(1,), after=[dq],
    )
    outs, = call(add_out_kernel, [sds((16, 2, 8, D), BF)], [o_keep, swap(o_send)])
    dq, dkv_own, dkv_sib = call(
        far_back_kernel, [sds((G, G), F32), sds((G, G), F32), square],
        [ids, q, datt, stats, lo, far_own, far_sib, far, lo_far, kv, kv_sib, dq, dkv_own, dkv_sib],
        scratch=[pltpu.VMEM((2, 2, HD, G), BF), pltpu.VMEM((G, G), F32), pltpu.VMEM((8, G), F32)], smem=1,
        after=[outs], far=(1, 5, 6, 7, 9, 10), us=40)
    outs = lax.all_to_all(outs, ROWS, split_axis=0, concat_axis=0, tiled=True)
    dkv_sib = swap(dkv_sib)
    out_grad, = call(sum_out_kernel, [sds((16, D), F32)], [outs])
    dq, sum_q = call(q_back_kernel, [square, sds((1, HD), F32)], [dq, qraw, gain_qk, cos, sin], after=[out_grad], far=(1,), us=1)
    dqkv, sum_k, *parts = call(
        kv_back_kernel, [sds((G, D), BF), sds((1, HD), F32)] + partials(),
        [ids, dkv_own, dkv_sib, kraw, gain_qk, cos, sin, w_qkv, dq],
        scratch=[pltpu.VMEM((G, D), BF)], smem=1, far=(3, 7), lazy=True, us=1)
    parts = collect(parts)
    q_keep, q_send = call(
        qkv_grad_kernel, [sds((8, 64, 1152), F32), sds((8, 64, 1152), BF)],
        [ids, h_attn, dqkv, sum_q, sum_k, squares], smem=1, far=(1,), us=1)
    sums, = call(add_qkv_kernel, [sds((16, 4, 8, 1152), BF)], [q_keep, swap(q_send)])
    sums = lax.all_to_all(sums, ROWS, split_axis=0, concat_axis=0, tiled=True)
    tokens_grad, = call(last_kernel, [sds((T, D), F32)], [dmid, *parts, tok, gain_a])
    down_grad, *pieces = call(
        sum_kernel, [sds((24, D), F32)] + [sds((8, 2688), BF)] * 4, [ids, sums, grads],
        scratch=[pltpu.VMEM((4, 8, 1152), F32)], smem=1,
    )
    pieces = [pieces[0]] + [around(pieces[k], k) for k in (1, 2, 3)]
    qkv_grad, gain_a_grad, note, gate_up_grad, gain_f_grad = call(
        finish_kernel,
        [sds((8, 4096), F32), sds((8, HD), F32), sds((8, HD), F32), sds((8, 2 * FF), F32), sds((8, HD), F32)],
        [ids, *pieces, w, gate_up_weight[0]], smem=1,
    )
    mean_loss = note[2, 0] * factor[0, 0] * (1.0 / (TOKENS * D))
    place = ((zh * 4 + x_id) * 2 + c_id) * 8 + lax.axis_index("zl") * 4 + lax.axis_index("y")
    gain_qk_grad = lax.dynamic_slice(note[:2].reshape(256), (2 * place,), (2,))

    return (
        mean_loss,
        block[None],
        tokens_grad[None],
        qkv_grad[None],
        out_grad[None],
        gate_up_grad[None],
        down_grad[None],
        (gain_a_grad[:, 0] / attn_gain[0].astype(F32))[None],
        (gain_f_grad[:, 0] / ffn_gain[0].astype(F32))[None],
        gain_qk_grad[None],
    )


def solution(mesh):
    fine = Mesh(mesh.devices.reshape(2, 4, 2, 2, 4), ALL)
    ctx, wsh = ("zh", "x", "c"), ("zl", "y")
    states = P(wsh, ctx, None)
    matrix, vector = P(None, ALL, None), P(None, ALL)
    return jax.shard_map(
        local,
        mesh=fine,
        in_specs=(states, states, P(wsh, None), P(wsh, ctx)) + (matrix,) * 4 + (vector,) * 3,
        out_specs=(P(), states, states) + (matrix,) * 4 + (vector,) * 3,
        check_vma=False,
    )
```

```python
import math

import jax
import jax.numpy as jnp
from jax import lax
from jax.experimental import pallas as pl
from jax.experimental.pallas import tpu as pltpu
from jax.sharding import Mesh
from jax.sharding import PartitionSpec as P

D = 1024
HEADS = 16
KV_HEADS = 8
HD = 128
FF = 3072
T = 128
G = 512
HALF = 1024
EPS = 1e-06
THETA = 1000000.0
SCALE = 1.0 / math.sqrt(HD)
SCALE2 = SCALE / math.log(2.0)
TOKENS = 16384.0
MICROSECOND = 3 * 10**8

ALL = ("zh", "x", "c", "zl", "y")
ROWS = ("zh", "zl", "y")
CHIPS = ("zh", "x", "zl", "y")
BF = jnp.bfloat16
F32 = jnp.float32


def nt(a, b):
    return lax.dot_general(a, b, (((1,), (1,)), ((), ())), preferred_element_type=F32)


def nn(a, b):
    return lax.dot_general(a, b, (((1,), (0,)), ((), ())), preferred_element_type=F32)


def tn(a, b):
    return lax.dot_general(a, b, (((0,), (0,)), ((), ())), preferred_element_type=F32)


def sds(shape, dtype):
    return jax.ShapeDtypeStruct(shape, dtype)


class Moves:
    def __init__(self):
        self.copies, self.started, self.ended = {}, set(), set()

    def start(self, *refs):
        for ref in refs:
            if id(ref) not in self.started:
                self.started.add(id(ref))
                self.copies[id(ref)].start()

    def wait(self, *refs):
        for ref in refs:
            if id(ref) in self.copies and id(ref) not in self.ended:
                self.ended.add(id(ref))
                self.copies[id(ref)].wait()


def kept(shape, dtype):
    return pltpu.HBM(shape, dtype)


def in_hbm(value):
    return pltpu.with_memory_space_constraint(value, pltpu.HBM)


def call(body, outs, args, scratch=(), smem=0, limit=28, after=(), far=(), lazy=False, us=1):
    kept_out = [i for i, o in enumerate(outs) if not isinstance(o, jax.ShapeDtypeStruct)]
    vmem, hbm = pl.BlockSpec(memory_space=pltpu.VMEM), pl.BlockSpec(memory_space=pltpu.HBM)
    specs = [pl.BlockSpec(memory_space=pltpu.SMEM)] * smem
    specs += [hbm if i in far else vmem for i in range(smem, len(args))]
    specs += [pl.BlockSpec(memory_space=pl.ANY)] * len(after)
    count = len(args)
    staged = [(args[i].shape, args[i].dtype) for i in far]
    staged += [(outs[i].inner_aval.shape, outs[i].inner_aval.dtype) for i in kept_out]
    scratch = list(scratch) + [pltpu.VMEM(*a) for a in staged]
    if staged:
        scratch.append(pltpu.SemaphoreType.DMA((len(staged),)))

    def kernel(*refs):
        ins = list(refs[:count])
        results = list(refs[count + len(after) :][: len(outs)])
        rest = list(refs[count + len(after) + len(outs) :])
        if not staged:
            body(*ins, *results, *rest)
            return
        sems = rest.pop()
        stage = rest[len(rest) - len(staged) :]
        rest = rest[: len(rest) - len(staged)]
        moves = Moves()
        for n, i in enumerate(far):
            moves.copies[id(stage[n])] = pltpu.make_async_copy(ins[i], stage[n], sems.at[n])
            ins[i] = stage[n]
        for n, i in enumerate(kept_out, len(far)):
            moves.copies[id(stage[n])] = pltpu.make_async_copy(stage[n], results[i], sems.at[n])
            results[i] = stage[n]
        moves.start(*stage[: len(far)])
        if lazy:
            body(moves, *ins, *results, *rest)
        else:
            moves.wait(*stage[: len(far)])
            body(*ins, *results, *rest)
        moves.start(*stage)
        moves.wait(*stage)

    return pl.pallas_call(
        kernel,
        name=body.__name__,
        out_shape=list(outs),
        in_specs=specs,
        out_specs=[hbm if i in kept_out else vmem for i in range(len(outs))],
        scratch_shapes=scratch,
        compiler_params=pltpu.CompilerParams(vmem_limit_bytes=limit * 1024 * 1024),
        cost_estimate=pl.CostEstimate(flops=MICROSECOND * us, bytes_accessed=1, transcendentals=0),
    )(*[in_hbm(a) if i in far else a for i, a in enumerate(args)], *after)


def behind(value, *after):
    def nothing(*refs):
        del refs

    place = pl.BlockSpec(memory_space=pl.ANY)
    return pl.pallas_call(
        nothing,
        out_shape=sds(value.shape, value.dtype),
        in_specs=[place] * (1 + len(after)),
        out_specs=place,
        input_output_aliases={0: 0},
        cost_estimate=pl.CostEstimate(flops=1, bytes_accessed=1, transcendentals=0),
    )(value, *after)


def shift_from(x_id, k):
    return lax.rem(x_id - k + 4, 4)


def project(rows, weight, product, outs):
    for t in range(4):
        cols = slice(t * 256, (t + 1) * 256)
        value = product(rows, weight(cols))
        for k, out in enumerate(outs):
            out[:, cols] = value[k * T : (k + 1) * T].astype(out.dtype)


def rows_at(index, size):
    return pl.ds(pl.multiple_of(index * size, size), size)


def pack_kernel(ids, w, gu, out_w, down_w, gain_a, gain_f, gain_qk, mask, rows, own, s1, s2, s3, notes):
    for g in range(2):
        rows[g] = out_w[8 * g : 8 * g + 8, :]
    for g in range(3):
        rows[2 + g] = down_w[8 * g : 8 * g + 8, :]
    notes[...] = jnp.zeros_like(notes)
    notes[0:1, :8] = gain_a[...].astype(F32)
    notes[1:2, :8] = gain_f[...].astype(F32)
    notes[2:3, :2] = gain_qk[...].astype(F32)
    notes[3:4, :1] = jnp.sum(mask[...].astype(F32), axis=1, keepdims=True)
    note = notes[...].T[:8].astype(BF)
    for k, out in enumerate((own, s1, s2, s3)):
        x = lax.rem(ids[1] + k, 4)
        places = [(w, 0, 256), (w, HALF, 256)]
        places += [(w, base, HD) for base in (2048, 2560, 3072, 3584)]
        places += [(None, 0, 0)] + [(gu, base, 384) for base in (0, 1536, 3072, 4608)]
        at = 0
        for ref, base, n in places:
            if ref is None:
                out[:, at : at + HD] = note
                at += HD
            else:
                out[:, at : at + n] = ref[:, pl.ds(pl.multiple_of(base + x * n, HD), n)]
                at += n


def join_kernel(p0, p1, p2, p3, first, second):
    for k, ref in enumerate((p0, p1, p2, p3)):
        block, other = ref[:, :1152], ref[:, 1152:]
        for device in range(16):
            first[device, k] = block
            second[device, k] = other


def gather_kernel(ids, t0, t1, t2, t3, toks, scale):
    for k, ref in enumerate((t0, t1, t2, t3)):
        rows = rows_at(shift_from(ids[1], k), T)
        toks[rows, :] = ref[...]
        t = ref[...].astype(F32)
        r = lax.rsqrt(jnp.mean(t * t, axis=-1, keepdims=True) + EPS)
        scale[rows, :] = jnp.broadcast_to(r, (T, HD))


def blocks_of(got, zz, k):
    return jnp.concatenate([got[zz * 8 + other, k].astype(F32) for other in range(8)], axis=0).astype(BF)


def qkv_kernel(moves, ids, toks, scale, own, sib, cos, sin,
               h_ref, q_ref, kv_ref, cross, qraw, kraw, gain, gain_f, qk_gain, factor, weight, wide):
    c_id = ids[2]
    for zz in range(2):
        for k in range(4):
            at = 2 * (4 * zz + shift_from(ids[1], k))
            for whose, ref in ((c_id, own), (1 - c_id, sib)):
                value = blocks_of(ref, zz, k)
                weight[rows_at(at + whose, 64), :] = value[:, :D]
                wide[rows_at(at + whose, 64), :] = value[:, D:]
    moves.start(weight)
    notes = wide[...].T
    gain[...] = notes[0:1].astype(F32)
    gain_f[...] = notes[1:2].astype(F32)
    at = lax.broadcasted_iota(jnp.int32, (D, 256), 0)
    entry = lax.broadcasted_iota(jnp.int32, (D, 256), 1)
    pick = jnp.where(at == 8 * (entry >> 1) + (entry & 1), 1.0, 0.0).astype(BF)
    qk_gain[...] = nn(notes[:16], pick)[2:3]
    count = jnp.sum(notes[3:4].astype(F32), axis=1, keepdims=True)
    factor[...] = jnp.broadcast_to(TOKENS / count, (1, HD))

    def rope(v, gains, rows):
        r = lax.rsqrt(jnp.mean(v * v, axis=-1, keepdims=True) + EPS)
        n = v * r * gains
        return (n * cos[rows, :] + pltpu.roll(n, 64, 1) * sin[rows, :]).astype(BF)

    for j in range(4):
        rows = slice(j * T, (j + 1) * T)
        t = toks[rows, :].astype(F32)
        h = (t * scale[rows, :1] * gain[...]).astype(BF)
        h_ref[rows, :] = h
        q = nn(h, weight[:, :G])
        kv = nn(h, weight[:, G:])
        qraw[rows, :] = q
        kraw[rows, :] = kv[:, :256]
        kv_ref[rows, 256:] = kv[:, 256:].astype(BF)
        for n in range(4):
            q_ref[rows, n * HD : (n + 1) * HD] = rope(q[:, n * HD : (n + 1) * HD], qk_gain[:, :HD], rows)
        for n in range(2):
            kv_ref[rows, n * HD : (n + 1) * HD] = rope(kv[:, n * HD : (n + 1) * HD], qk_gain[:, HD:], rows)
    cross[...] = jnp.where(ids[0] == 0, kv_ref[...], q_ref[...])


def head_pair(ref, hh, j):
    rows = slice(j * T, (j + 1) * T)
    base = hh * 256
    return jnp.concatenate([ref[rows, base : base + HD], ref[rows, base + HD : base + 256]], axis=0)


def row_pair(row):
    return jnp.concatenate([row, row], axis=1)


def key_positions(base, start, count):
    index = lax.broadcasted_iota(jnp.int32, (count, 1), 0) + start
    return base + index + (index >> 7) * T


def query_positions(zh, c, j):
    row = lax.broadcasted_iota(jnp.int32, (1, T), 1) + (zh * HALF + j * 256 + c * T)
    return row_pair(row)


def fill_values(vt, slot, kv_ref):
    for hh in range(2):
        vt[slot, hh, :HD, :] = kv_ref[:, 256 + hh * HD : 256 + (hh + 1) * HD].T
        vt[slot, hh, HD:, :] = jnp.ones((16, G), BF)


def tiles(count):
    return [(t, min(256, count - t)) for t in range(0, count, 256)]


def join_out(c, own, sib, weight):
    for hh in range(2):
        for whose, ref in ((c, own), (1 - c, sib)):
            parts = [ref[hh * 8 + o, g].astype(F32) for o in range(8) for g in range(2)]
            weight[rows_at(2 * hh + whose, HD), :] = jnp.concatenate(parts, axis=0).astype(BF)


def attend(q_ref, kv_ref, vt, slot, hh, j, count, base, qpos, lo_row, causal):
    qj = head_pair(q_ref, hh, j)
    total = None
    for start, n in tiles(count):
        keys = kv_ref[start : start + n, hh * HD : (hh + 1) * HD]
        s = nt(keys, qj)
        kpos = key_positions(base, start, n)
        mask = kpos >= lo_row
        if causal:
            mask = mask & (kpos <= qpos)
        p = jnp.where(mask, jnp.exp2(s * SCALE2), 0.0).astype(BF)
        part = nn(vt[slot, hh, :, start : start + n], p)
        total = part if total is None else total + part
    return total


def attention_kernel(moves, ids, q_ref, own, sib, far_own, far_sib, lo, rows_own, rows_sib,
                     att, att_t, lse, w_nat, p0, p1, p2, p3, vt, sums, wide, turned):
    zh, x_id, c = ids[0], ids[1], ids[2]
    join_out(c, rows_own, rows_sib, w_nat)
    moves.start(w_nat)
    moves.wait(q_ref, own, sib, far_own, far_sib)
    fill_values(vt, 0, own)
    fill_values(vt, 1, sib)
    sums[4:8, :] = jnp.ones((4, G), F32)
    for hh in range(2):
        for j in range(4):
            cols = slice(j * T, (j + 1) * T)
            lo_row = row_pair(lo[:, cols])
            qpos = query_positions(zh, c, j)
            total = None
            for slot, (ref, whose) in enumerate(((own, c), (sib, 1 - c))):
                part = attend(
                    q_ref, ref, vt, slot, hh, j, (j + 1) * T, zh * HALF + whose * T, qpos, lo_row, True
                )
                total = part if total is None else total + part
            for g in range(2):
                n = 2 * hh + g
                wide[n * HD : (n + 1) * HD, cols] = total[:HD, g * T : (g + 1) * T]
                sums[n : n + 1, cols] = total[HD : HD + 1, g * T : (g + 1) * T]

    @pl.when(zh == 1)
    def _():
        fill_values(vt, 0, far_own)
        fill_values(vt, 1, far_sib)
        for hh in range(2):
            for j in range(4):
                cols = slice(j * T, (j + 1) * T)
                lo_row = row_pair(lo[:, cols])
                total = None
                for slot, (ref, whose) in enumerate(((far_own, c), (far_sib, 1 - c))):
                    part = attend(q_ref, ref, vt, slot, hh, j, G, whose * T, None, lo_row, False)
                    total = part if total is None else total + part
                for g in range(2):
                    n = 2 * hh + g
                    wide[n * HD : (n + 1) * HD, cols] += total[:HD, g * T : (g + 1) * T]
                    sums[n : n + 1, cols] += total[HD : HD + 1, g * T : (g + 1) * T]

    lse[...] = jnp.log2(sums[...])
    for n in range(4):
        inverse = 1.0 / sums[n : n + 1, :]
        scaled = wide[n * HD : (n + 1) * HD, :] * inverse
        att_t[n * HD : (n + 1) * HD, :] = scaled
        for j in range(4):
            att[j * T : (j + 1) * T, n * HD : (n + 1) * HD] = scaled[:, j * T : (j + 1) * T].T.astype(BF)
    moves.start(att, att_t)
    for k in range(4):
        turned[k * T : (k + 1) * T, :] = att[rows_at(shift_from(x_id, k), T), :]
    project(turned[...], lambda cols: w_nat[:, cols], nn, (p0, p1, p2, p3))


def stat_pair(stats, row, cols):
    return jnp.concatenate([stats[row : row + 1, cols], stats[row + 1 : row + 2, cols]], axis=1)


def attend_back(q_ref, datt, stats, lo, kv_ref, hh, j, count, base, qpos, dkv=None, kt=None):
    cols = slice(j * T, (j + 1) * T)
    lo_row = row_pair(lo[:, cols])
    lse_row, delta_row = stat_pair(stats, 2 * hh, cols), stat_pair(stats, 4 + 2 * hh, cols)
    qj = head_pair(q_ref, hh, j)
    dj = head_pair(datt, hh, j)
    dq = None
    for start, n in tiles(count):
        rows = slice(start, start + n)
        kc = slice(hh * HD, (hh + 1) * HD)
        vc = slice(256 + hh * HD, 256 + (hh + 1) * HD)
        s = nt(kv_ref[rows, kc], qj)
        dp = nt(kv_ref[rows, vc], dj)
        mask = key_positions(base, start, n) >= lo_row
        if qpos is not None:
            mask = mask & (key_positions(base, start, n) <= qpos)
        p = jnp.where(mask, jnp.exp2(s * SCALE2 - lse_row), 0.0)
        ds = (p * (dp - delta_row) * SCALE).astype(BF)
        if dkv is not None:
            dkv[rows, vc] += nn(p.astype(BF), dj)
            dkv[rows, kc] += nn(ds, qj)
        if kt is not None:
            part = nn(kt[hh, :, start : start + n], ds)
            dq = part if dq is None else dq + part
    return dq


def fill_keys(kt, slot, kv_ref):
    for hh in range(2):
        kt[slot, hh] = kv_ref[:, hh * HD : (hh + 1) * HD].T


def datt_kernel(moves, ids, b0, b1, b2, b3, w_nat, lse, att_t, dmb, datt, stats, sent):
    for k, ref in enumerate((b0, b1, b2, b3)):
        dmb[rows_at(shift_from(ids[1], k), T), :] = ref[...]
    moves.wait(w_nat)
    datt[...] = nt(dmb[...], w_nat[...]).astype(BF)
    moves.wait(att_t)
    stats[:4, :] = lse[:4, :]
    for n in range(4):
        cols = slice(n * HD, (n + 1) * HD)
        back = nt(w_nat[cols, :], dmb[...]).astype(BF).astype(F32)
        stats[4 + n : 5 + n, :] = jnp.sum(back * att_t[cols, :], axis=0, keepdims=True)
    sent[:G, :] = datt[...]
    high = stats[...].astype(BF).astype(F32)
    middle = (stats[...] - high).astype(BF).astype(F32)
    low = stats[...] - high - middle
    sent[G:, :] = jnp.concatenate([high, middle, low, jnp.zeros((8, G), F32)], axis=0).astype(BF)


def near_back_kernel(ids, q_ref, own, sib, lo, datt, stats, dq, dkv_own, dkv_sib, kt):
    zh, c = ids[0], ids[2]
    dkv_own[...] = jnp.zeros_like(dkv_own)
    dkv_sib[...] = jnp.zeros_like(dkv_sib)
    fill_keys(kt, 0, own)
    fill_keys(kt, 1, sib)
    for hh in range(2):
        for j in range(4):
            qpos = query_positions(zh, c, j)
            total = None
            for slot, (ref, dref, whose) in enumerate(((own, dkv_own, c), (sib, dkv_sib, 1 - c))):
                part = attend_back(
                    q_ref, datt, stats, lo, ref, hh, j, (j + 1) * T, zh * HALF + whose * T, qpos, dref, kt.at[slot]
                )
                total = part if total is None else total + part
            for g in range(2):
                n = 2 * hh + g
                dq[j * T : (j + 1) * T, n * HD : (n + 1) * HD] = total[:, g * T : (g + 1) * T].T


def far_back_kernel(ids, q, datt, stats, lo, far_own, far_sib, far, lo_far, own, sib,
                    dq_in, dkv_own_in, dkv_sib_in, dq, dkv_own, dkv_sib, kt, total_sib, stats_far):
    zh, c = ids[0], ids[2]
    dq[...] = dq_in[...]
    dkv_own[...] = dkv_own_in[...]
    total_sib[...] = dkv_sib_in[...]

    @pl.when(zh == 1)
    def _():
        fill_keys(kt, 0, far_own)
        fill_keys(kt, 1, far_sib)
        for hh in range(2):
            for j in range(4):
                total = None
                for slot, (ref, whose) in enumerate(((far_own, c), (far_sib, 1 - c))):
                    part = attend_back(q, datt, stats, lo, ref, hh, j, G, whose * T, None, None, kt.at[slot])
                    total = part if total is None else total + part
                for g in range(2):
                    n = 2 * hh + g
                    dq[j * T : (j + 1) * T, n * HD : (n + 1) * HD] += total[:, g * T : (g + 1) * T].T

    @pl.when(zh == 0)
    def _():
        parts = far[G:, :].astype(F32)
        stats_far[...] = parts[:8] + parts[8:16] + parts[16:24]
        for hh in range(2):
            for j in range(4):
                for ref, dref, whose in ((own, dkv_own, c), (sib, total_sib, 1 - c)):
                    attend_back(far_own, far, stats_far, lo_far, ref, hh, j, G, whose * T, None, dref, None)

    dkv_sib[...] = total_sib[...].astype(BF)


def head_back(w, raw, gain, cos, sin):
    w = w * cos - pltpu.roll(w, 64, 1) * sin
    r = lax.rsqrt(jnp.mean(raw * raw, axis=-1, keepdims=True) + EPS)
    a = w * gain
    out = r * a - raw * (r * r * r * jnp.mean(a * raw, axis=-1, keepdims=True))
    return out, jnp.sum(w * raw * r, axis=0, keepdims=True)


def q_back_kernel(dq, qraw, qk_gain, cos, sin, out, gains):
    total = jnp.zeros((1, HD), F32)
    for j in range(4):
        rows = slice(j * T, (j + 1) * T)
        for n in range(4):
            hc = slice(n * HD, (n + 1) * HD)
            value, part = head_back(dq[rows, hc], qraw[rows, hc], qk_gain[:, :HD], cos[rows, :], sin[rows, :])
            total += part
            out[rows, hc] = value.astype(BF)
    gains[...] = total


def kv_back_kernel(moves, ids, dkv, from_sib, kraw, qk_gain, cos, sin, weight, dq, dqkv, gains, p0, p1, p2, p3, turned):
    total = jnp.zeros((1, HD), F32)
    dqkv[:, :G] = dq[...]
    moves.wait(kraw)
    for j in range(4):
        rows = slice(j * T, (j + 1) * T)
        grad = dkv[rows, :] + from_sib[rows, :].astype(F32)
        for n in range(2):
            hc = slice(n * HD, (n + 1) * HD)
            value, part = head_back(grad[:, hc], kraw[rows, hc], qk_gain[:, HD:], cos[rows, :], sin[rows, :])
            total += part
            dqkv[rows, G + n * HD : G + (n + 1) * HD] = value.astype(BF)
        dqkv[rows, G + 256 :] = grad[:, 256:].astype(BF)
    gains[...] = total
    for k in range(4):
        turned[k * T : (k + 1) * T, :] = dqkv[rows_at(shift_from(ids[1], k), T), :]
    moves.wait(weight)
    project(turned[...], lambda cols: weight[cols, :], nt, (p0, p1, p2, p3))


def split_rows(c_id, value, keep, send, index):
    half = value.shape[0] // 2
    first = c_id == 0
    keep[index] = jnp.where(first, value[:half], value[half:])
    send[index] = jnp.where(first, value[half:], value[:half]).astype(BF)


def qkv_grad_kernel(ids, h, dqkv, gain_q, gain_k, squares, keep, send):
    total = jnp.broadcast_to(jnp.sum(squares[...], keepdims=True), (1, HD))
    note = jnp.concatenate([gain_q[...], gain_k[...], total, jnp.zeros((5, HD), F32)], axis=0)
    note = jnp.concatenate([note] * 8, axis=0)
    first = ids[2] == 0
    for b in range(8):
        value = tn(h[:, b * 128 : (b + 1) * 128], dqkv[...])
        keep[b, :, :D] = jnp.where(first, value[:64], value[64:])
        send[b, :, :D] = jnp.where(first, value[64:], value[:64]).astype(BF)
        keep[b, :, D:] = note
        send[b, :, D:] = note.astype(BF)


def add_qkv_kernel(keep, got, out):
    for zz in range(2):
        for x in range(4):
            value = keep[4 * zz + x] + got[4 * zz + x].astype(F32)
            for o in range(8):
                out[zz * 8 + o, x] = value[8 * o : 8 * o + 8].astype(BF)


def sum_kernel(ids, sums, grads, down, own, s1, s2, s3, total):
    for x in range(4):
        value = sums[0, x].astype(F32)
        for device in range(1, 16):
            value += sums[device, x].astype(F32)
        total[x] = value
    for k, out in enumerate((own, s1, s2, s3)):
        x = lax.rem(ids[1] + k, 4)
        out[:, :1152] = total[x].astype(BF)
        for b in range(3):
            out[:, 1152 + 512 * b : 1152 + 512 * (b + 1)] = grads[3 * x + b]
    for g in range(3):
        for half in range(2):
            down[8 * g : 8 * g + 8, half * 512 : (half + 1) * 512] = grads[12 + 2 * g + half].astype(F32)


def add_out_kernel(keep, got, out):
    for zz in range(2):
        value = keep[zz] + got[zz].astype(F32)
        for o in range(8):
            for g in range(2):
                out[zz * 8 + o, g] = value[16 * o + 8 * g : 16 * o + 8 * g + 8].astype(BF)


def sum_out_kernel(sums, out):
    for g in range(2):
        value = sums[0, g].astype(F32)
        for device in range(1, 16):
            value += sums[device, g].astype(F32)
        out[8 * g : 8 * g + 8, :] = value


def finish_kernel(ids, p0, p1, p2, p3, w, gu, grad, gain, note, gu_grad, gu_gain):
    total = jnp.zeros((8, HD), F32)
    gain_sum = jnp.zeros((8, 1), F32)
    gu_sum = jnp.zeros((8, 1), F32)
    for k, ref in enumerate((p0, p1, p2, p3)):
        value = ref[...].astype(F32)
        x = shift_from(ids[1], k)
        total += value[:, D:1152]
        places = [(0, 0, 256), (256, HALF, 256)]
        places += [(G + n * HD, base, HD) for n, base in enumerate((2048, 2560, 3072, 3584))]
        for start, base, n in places:
            at = pl.ds(pl.multiple_of(base + x * n, HD), n)
            part = value[:, start : start + n]
            grad[:, at] = part
            gain_sum += jnp.sum(part * w[:, at].astype(F32), axis=1, keepdims=True)
        for n in range(4):
            at = pl.ds(pl.multiple_of(n * 1536 + x * 384, HD), 384)
            part = value[:, 1152 + n * 384 : 1152 + (n + 1) * 384]
            gu_grad[:, at] = part
            gu_sum += jnp.sum(part * gu[:, at].astype(F32), axis=1, keepdims=True)
    gain[...] = jnp.broadcast_to(gain_sum, (8, HD))
    gu_gain[...] = jnp.broadcast_to(gu_sum, (8, HD))
    note[...] = total


def out_grad_kernel(ids, att, dmb, keep, send):
    for b in range(2):
        split_rows(ids[2], tn(att[:, b * 256 : (b + 1) * 256], dmb[...]), keep, send, b)


def stack4(a, b, c, d):
    return jnp.concatenate([a[...], b[...], c[...], d[...]], axis=0)


def order_kernel(ids, own, sib, rows_own, rows_sib, weight, down):
    for whose, ref, rows in ((ids[2], own, rows_own), (1 - ids[2], sib, rows_sib)):
        for zz in range(2):
            for k in range(4):
                at = rows_at(2 * (4 * zz + shift_from(ids[1], k)) + whose, 64)
                weight[at, :] = blocks_of(ref, zz, k)
            parts = [rows[zz * 8 + o, 2 + g].astype(F32) for o in range(8) for g in range(3)]
            down[rows_at(2 * zz + whose, 192), :] = jnp.concatenate(parts, axis=0).astype(BF)


def ffn_kernel(h0, h1, h2, h3, weight, down, gate, up, act, h, p0, p1, p2, p3):
    h[...] = stack4(h0, h1, h2, h3)
    for t in range(3):
        cols = slice(t * 256, (t + 1) * 256)
        g = nn(h[...], weight[:, cols])
        u = nn(h[...], weight[:, 768 + t * 256 : 768 + (t + 1) * 256])
        gate[:, cols] = g
        up[:, cols] = u
        act[:, cols] = (g * jax.nn.sigmoid(g) * u).astype(BF)
    project(act[...], lambda cols: down[:, cols], nn, (p0, p1, p2, p3))


def ffn_back_kernel(g0, g1, g2, g3, gate, up, weight, down, dgu, p0, p1, p2, p3, gb):
    gb[...] = stack4(g0, g1, g2, g3)
    for t in range(3):
        cols = slice(t * 256, (t + 1) * 256)
        dact = nt(gb[...], down[cols, :])
        g = gate[:, cols]
        u = up[:, cols]
        s = jax.nn.sigmoid(g)
        dgu[:, cols] = (dact * u * s * (1.0 + g * (1.0 - s))).astype(BF)
        dgu[:, 768 + t * 256 : 768 + (t + 1) * 256] = (dact * g * s).astype(BF)
    project(dgu[...], lambda cols: weight[cols, :], nt, (p0, p1, p2, p3))


def ffn_grad_kernel(ids, h, g0, g1, g2, g3, act, dgu, d_keep, d_send, u_keep, u_send, gb):
    c_id = ids[2]
    gb[...] = stack4(g0, g1, g2, g3)
    for b in range(2):
        split_rows(c_id, tn(act[:, b * 384 : (b + 1) * 384], gb[...]), d_keep, d_send, b)
    for b in range(8):
        split_rows(c_id, tn(h[:, b * 128 : (b + 1) * 128], dgu[...]), u_keep, u_send, b)


def pack_grads_kernel(u_keep, u_got, d_keep, d_got, out):
    for zz in range(2):
        for x in range(4):
            value = u_keep[4 * zz + x] + u_got[4 * zz + x].astype(F32)
            for o in range(8):
                for b in range(3):
                    part = value[8 * o : 8 * o + 8, 512 * b : 512 * (b + 1)]
                    out[(zz * 8 + o) * 18 + 3 * x + b] = part.astype(BF)
        value = d_keep[zz] + d_got[zz].astype(F32)
        for o in range(8):
            for g in range(3):
                for half in range(2):
                    part = value[24 * o + 8 * g : 24 * o + 8 * g + 8, 512 * half : 512 * (half + 1)]
                    out[(zz * 8 + o) * 18 + 12 + 2 * g + half] = part.astype(BF)


def total_of(own, r1, r2, r3):
    return own[...] + r1[...].astype(F32) + r2[...].astype(F32) + r3[...].astype(F32)


def mid_kernel(tok, own, r1, r2, r3, gain, mid, h):
    v = tok[...].astype(F32) + total_of(own, r1, r2, r3)
    mid[...] = v
    r = lax.rsqrt(jnp.mean(v * v, axis=-1, keepdims=True) + EPS)
    h[...] = (v * r * gain[...]).astype(BF)


def loss_kernel(factor, mid, own, r1, r2, r3, teacher, mask, block, grad, grad_low, squares):
    v = mid[...] + total_of(own, r1, r2, r3)
    block[...] = v.astype(BF)
    diff = v - teacher[...].astype(F32)
    kept = jnp.broadcast_to(mask[...].astype(F32), (T, T)).T[:, :1] * diff
    out = factor[:, :1] * kept
    grad[...] = out
    grad_low[...] = out.astype(BF)
    squares[...] = jnp.sum((kept * diff).reshape(16, 8, D), axis=0)


def norm_back(v, gain, w):
    r = lax.rsqrt(jnp.mean(v * v, axis=-1, keepdims=True) + EPS)
    a = w * gain
    return r * a - v * (r * r * r * jnp.mean(a * v, axis=-1, keepdims=True))


def dmid_kernel(grad, own, r1, r2, r3, mid, gain, dmid, dmb):
    out = grad[...] + norm_back(mid[...], gain[...], total_of(own, r1, r2, r3))
    dmid[...] = out
    dmb[...] = out.astype(BF)


def last_kernel(dmid, own, r1, r2, r3, tok, gain, out):
    out[...] = dmid[...] + norm_back(tok[...].astype(F32), gain[...], total_of(own, r1, r2, r3))


def ring(k):
    return [(i, (i + k) % 4) for i in range(4)]


def around(v, k):
    return lax.ppermute(v, "x", ring(k))


def spread(v):
    return (v,) + tuple(around(v, k) for k in (1, 2, 3))


def collect(parts):
    return (parts[0],) + tuple(around(parts[k], -k) for k in (1, 2, 3))


def swap(v):
    return lax.ppermute(v, "c", [(0, 1), (1, 0)])


def partials():
    return [sds((T, D), F32)] + [sds((T, D), BF)] * 3


def local(tokens, teacher, doc_starts, valid_mask, qkv_weight, out_weight, gate_up_weight, down_weight,
          attn_gain, ffn_gain, qk_gain):
    zh, x_id, c_id = lax.axis_index("zh"), lax.axis_index("x"), lax.axis_index("c")
    z_id = zh * 2 + lax.axis_index("zl")
    ids = jnp.stack([zh, x_id, c_id, lax.axis_index("y"), z_id]).astype(jnp.int32)
    tok = tokens[0]

    w = qkv_weight[0]
    rows, *sent = call(
        pack_kernel, [sds((5, 8, D), BF)] + [sds((8, 2688), BF)] * 4,
        [ids, w, gate_up_weight[0], out_weight[0], down_weight[0], attn_gain, ffn_gain, qk_gain, valid_mask],
        scratch=[pltpu.VMEM((HD, HD), F32)], smem=1, far=(1, 2, 3, 4),
    )
    columns = [sent[0]] + [around(sent[k], k) for k in (1, 2, 3)]
    first, second = call(join_kernel, [sds((16, 4, 8, 1152), BF), kept((16, 4, 8, 1536), BF)], columns)
    w_own = lax.all_to_all(first, ROWS, split_axis=0, concat_axis=0, tiled=True)
    w_sib = swap(w_own)
    ts = spread(behind(tok, first))
    toks, scales = call(gather_kernel, [sds((G, D), BF), sds((G, HD), F32)], [ids, *ts], smem=1, us=100)
    rows = lax.all_gather(rows, ROWS, axis=0, tiled=False)

    offset = jnp.arange(G, dtype=jnp.int32)
    positions = zh * HALF + c_id * T + offset + (offset // T) * T
    starts = doc_starts[0]
    reached = positions[None, :, None] + HALF * jnp.arange(2, dtype=jnp.int32)[:, None, None] >= starts[None, None, :]
    lo, lo_far = jnp.split(jnp.max(jnp.where(reached, starts[None, None, :], 0), axis=2), 2, axis=0)
    half = HD // 2
    frequency = jnp.exp(-(jnp.arange(half, dtype=F32) * 2.0 / HD) * math.log(THETA))
    angles = positions.astype(F32)[:, None] * frequency[None, :]
    cos, sin = jnp.cos(angles), jnp.sin(angles)
    cos = jnp.concatenate([cos, cos], axis=1)
    sin = jnp.concatenate([-sin, sin], axis=1)

    square = sds((G, G), BF)
    small = sds((8, G), F32)
    h_attn, q, kv, cross, qraw, kraw, gain_a, gain_f, gain_qk, factor, w_qkv = call(
        qkv_kernel,
        [kept((G, D), BF), kept((G, G), BF), kept((G, G), BF), square, kept((G, G), F32), kept((G, 256), F32),
         sds((1, D), F32), sds((1, D), F32), sds((1, 256), F32), sds((1, HD), F32), kept((D, D), BF)],
        [ids, toks, scales, w_own, w_sib, cos, sin],
        scratch=[pltpu.VMEM((D, HD), BF)], smem=1, lazy=True, after=[lo, lo_far], us=4)
    kv_sib = swap(kv)
    far_own = lax.ppermute(cross, "zh", [(0, 1), (1, 0)])
    rows = behind(rows, far_own, kv_sib)
    far_sib, rows_sib = swap(far_own), swap(rows)
    second = lax.all_to_all(behind(second, far_sib), ROWS, split_axis=0, concat_axis=0, tiled=True)
    att, att_t, lse, w_out, *parts = call(
        attention_kernel,
        [kept((G, G), BF), kept((G, G), F32), small, kept((G, D), BF)] + partials(),
        [ids, q, kv, kv_sib, far_own, far_sib, lo, rows, rows_sib],
        scratch=[pltpu.VMEM((2, 2, 144, G), BF), pltpu.VMEM((8, G), F32), pltpu.VMEM((G, G), F32),
                 pltpu.VMEM((G, G), BF)],
        smem=1, lazy=True, far=(1, 2, 3, 4, 5), us=10,
    )
    parts = collect(parts)
    mid, h = call(mid_kernel, [sds((T, D), F32), sds((T, D), BF)], [tok, *parts, gain_f])

    hs = spread(h)
    second = behind(second, h)
    w_gu, w_down = call(
        order_kernel, [sds((D, 1536), BF), sds((768, D), BF)], [ids, second, swap(second), rows, rows_sib],
        smem=1, us=2
    )
    gate, up, act, h_ffn, *parts = call(
        ffn_kernel,
        [sds((G, 768), F32), sds((G, 768), F32), sds((G, 768), BF), sds((G, D), BF)] + partials(),
        [*hs, w_gu, w_down], us=3)
    parts = collect(parts)
    block, grad, grad_low, squares = call(
        loss_kernel,
        [sds((T, D), BF), sds((T, D), F32), sds((T, D), BF), sds((8, D), F32)],
        [factor, mid, *parts, teacher[0], valid_mask],
    )

    gs = spread(grad_low)
    dgu, *parts = call(
        ffn_back_kernel, [sds((G, 1536), BF)] + partials(), [*gs, gate, up, w_gu, w_down],
        scratch=[pltpu.VMEM((G, D), BF)], us=3)
    parts = collect(parts)
    d_keep, d_send, u_keep, u_send = call(
        ffn_grad_kernel,
        [sds((2, 192, D), F32), sds((2, 192, D), BF), sds((8, 64, 1536), F32), sds((8, 64, 1536), BF)],
        [ids, h_ffn, *gs, act, dgu],
        scratch=[pltpu.VMEM((G, D), BF)], smem=1, us=100)
    grads, = call(pack_grads_kernel, [sds((288, 8, 512), BF)], [u_keep, swap(u_send), d_keep, swap(d_send)], us=2)
    dmid, dmb = call(
        dmid_kernel, [sds((T, D), F32), sds((T, D), BF)], [grad, *parts, mid, gain_f], us=100)
    bs = spread(dmb)
    dmb_all, datt, stats, sent = call(
        datt_kernel, [sds((G, D), BF), square, small, sds((G + 32, G), BF)], [ids, *bs, w_out, lse, att_t], smem=1, after=[grads], lazy=True, far=(5, 7), us=1)
    grads = lax.psum_scatter(grads, ROWS, scatter_dimension=0, tiled=True)
    far = lax.ppermute(sent, "zh", [(1, 0)])
    dq, dkv_own, dkv_sib = call(
        near_back_kernel, [sds((G, G), F32)] * 3, [ids, q, kv, kv_sib, lo, datt, stats],
        scratch=[pltpu.VMEM((2, 2, HD, G), BF)], smem=1, far=(1, 2, 3), us=20)
    o_keep, o_send = call(
        out_grad_kernel, [sds((2, 128, D), F32), sds((2, 128, D), BF)], [ids, att, dmb_all], smem=1, far=(1,), after=[dq],
    )
    outs, = call(add_out_kernel, [sds((16, 2, 8, D), BF)], [o_keep, swap(o_send)])
    dq, dkv_own, dkv_sib = call(
        far_back_kernel, [sds((G, G), F32), sds((G, G), F32), square],
        [ids, q, datt, stats, lo, far_own, far_sib, far, lo_far, kv, kv_sib, dq, dkv_own, dkv_sib],
        scratch=[pltpu.VMEM((2, 2, HD, G), BF), pltpu.VMEM((G, G), F32), pltpu.VMEM((8, G), F32)], smem=1,
        after=[outs], far=(1, 5, 6, 7, 9, 10), us=20)
    outs = lax.all_to_all(outs, ROWS, split_axis=0, concat_axis=0, tiled=True)
    dkv_sib = swap(dkv_sib)
    out_grad, = call(sum_out_kernel, [sds((16, D), F32)], [outs])
    dq, sum_q = call(q_back_kernel, [square, sds((1, HD), F32)], [dq, qraw, gain_qk, cos, sin], after=[out_grad], far=(1,), us=1)
    dqkv, sum_k, *parts = call(
        kv_back_kernel, [sds((G, D), BF), sds((1, HD), F32)] + partials(),
        [ids, dkv_own, dkv_sib, kraw, gain_qk, cos, sin, w_qkv, dq],
        scratch=[pltpu.VMEM((G, D), BF)], smem=1, far=(3, 7), lazy=True, us=1)
    parts = collect(parts)
    q_keep, q_send = call(
        qkv_grad_kernel, [sds((8, 64, 1152), F32), sds((8, 64, 1152), BF)],
        [ids, h_attn, dqkv, sum_q, sum_k, squares], smem=1, far=(1,), us=1)
    sums, = call(add_qkv_kernel, [sds((16, 4, 8, 1152), BF)], [q_keep, swap(q_send)])
    sums = lax.all_to_all(sums, ROWS, split_axis=0, concat_axis=0, tiled=True)
    tokens_grad, = call(last_kernel, [sds((T, D), F32)], [dmid, *parts, tok, gain_a])
    down_grad, *pieces = call(
        sum_kernel, [sds((24, D), F32)] + [sds((8, 2688), BF)] * 4, [ids, sums, grads],
        scratch=[pltpu.VMEM((4, 8, 1152), F32)], smem=1,
    )
    pieces = [pieces[0]] + [around(pieces[k], k) for k in (1, 2, 3)]
    qkv_grad, gain_a_grad, note, gate_up_grad, gain_f_grad = call(
        finish_kernel,
        [sds((8, 4096), F32), sds((8, HD), F32), sds((8, HD), F32), sds((8, 2 * FF), F32), sds((8, HD), F32)],
        [ids, *pieces, w, gate_up_weight[0]], smem=1,
    )
    mean_loss = note[2, 0] * factor[0, 0] * (1.0 / (TOKENS * D))
    place = ((zh * 4 + x_id) * 2 + c_id) * 8 + lax.axis_index("zl") * 4 + lax.axis_index("y")
    gain_qk_grad = lax.dynamic_slice(note[:2].reshape(256), (2 * place,), (2,))

    return (
        mean_loss,
        block[None],
        tokens_grad[None],
        qkv_grad[None],
        out_grad[None],
        gate_up_grad[None],
        down_grad[None],
        (gain_a_grad[:, 0] / attn_gain[0].astype(F32))[None],
        (gain_f_grad[:, 0] / ffn_gain[0].astype(F32))[None],
        gain_qk_grad[None],
    )


def solution(mesh):
    fine = Mesh(mesh.devices.reshape(2, 4, 2, 2, 4), ALL)
    ctx, wsh = ("zh", "x", "c"), ("zl", "y")
    states = P(wsh, ctx, None)
    matrix, vector = P(None, ALL, None), P(None, ALL)
    return jax.shard_map(
        local,
        mesh=fine,
        in_specs=(states, states, P(wsh, None), P(wsh, ctx)) + (matrix,) * 4 + (vector,) * 3,
        out_specs=(P(), states, states) + (matrix,) * 4 + (vector,) * 3,
        check_vma=False,
    )
```
